32 devices in a mesh: ctx: 4 (over x, core), fsdp: 8 (over z, y).
Axes of the slice: x: 2, y: 2, z: 4, core: 2. Of those that a mesh axis runs over, the one named last changes fastest.
Arguments:
- tokens: bfloat16 [8, 2048, 768], P('fsdp', 'ctx'), may hold values from -6 to 6
- segments: int32 [8, 2048], P('fsdp', 'ctx'), may hold values from 0 to 3, as said below
- padding: int32 [8, 2048], P('fsdp', 'ctx'), may hold values from 0 to 1, as said below
- w_query: bfloat16 [768, 768], P('fsdp'), may hold values from -0.21875 to 0.21875
- w_key: bfloat16 [768, 768], P('fsdp'), may hold values from -0.21875 to 0.21875
- w_value: bfloat16 [768, 768], P('fsdp'), may hold values from -0.21875 to 0.21875
- w_out: bfloat16 [768, 768], P('fsdp'), may hold values from -1.25 to 1.25
- w_up: bfloat16 [768, 3072], P('fsdp'), may hold values from -0.21875 to 0.21875
- w_gate: bfloat16 [768, 3072], P('fsdp'), may hold values from -0.21875 to 0.21875
- w_down: bfloat16 [3072, 768], P('fsdp'), may hold values from -0.109375 to 0.109375
- bias_query: bfloat16 [768], P('fsdp'), may hold values from -3 to 3
- bias_value: bfloat16 [768], P('fsdp'), may hold values from -3 to 3
- bias_out: bfloat16 [768], P('fsdp'), may hold values from -3 to 3
- bias_down: bfloat16 [768], P('fsdp'), may hold values from -3 to 3
- gain_attn: bfloat16 [768], P('fsdp'), may hold values from 0.25 to 1.75
- shift_attn: bfloat16 [768], P('fsdp'), may hold values from -3 to 3
- gain_ffn: bfloat16 [768], P('fsdp'), may hold values from 0.25 to 1.75
- shift_ffn: bfloat16 [768], P('fsdp'), may hold values from -3 to 3
- cotangent: bfloat16 [8, 2048, 768], P('fsdp', 'ctx'), may hold values from -6 to 6
Outputs:
- layer_out: bfloat16 [8, 2048, 768], P('fsdp', 'ctx')
- grad_tokens: float32 [8, 2048, 768], P('fsdp', 'ctx')
- grad_w_query: float32 [768, 768], P('fsdp')
- grad_w_key: float32 [768, 768], P('fsdp')
- grad_w_value: float32 [768, 768], P('fsdp')
- grad_w_out: float32 [768, 768], P('fsdp')
- grad_w_up: float32 [768, 3072], P('fsdp')
- grad_w_gate: float32 [768, 3072], P('fsdp')
- grad_w_down: float32 [3072, 768], P('fsdp')
- grad_bias_query: float32 [768], P('fsdp')
- grad_bias_value: float32 [768], P('fsdp')
- grad_bias_out: float32 [768], P('fsdp')
- grad_bias_down: float32 [768], P('fsdp')
- grad_gain_attn: float32 [768], P('fsdp')
- grad_shift_attn: float32 [768], P('fsdp')
- grad_gain_ffn: float32 [768], P('fsdp')
- grad_shift_ffn: float32 [768], P('fsdp')
The draws below stay inside these ranges and needn't reach their ends.
Inputs may be any that keep to these rules, and one draw needn't show every extreme that they name: `segments`: along each sequence the document numbers never fall, start at 0 and rise by one where a new document begins. The padding tokens of a sequence form one run at its end.
All inputs are finite; a program needn't handle non-finite values.
Results may differ from the reference program's by a relative error of at most 0.02.
Values may be sent and summed in bfloat16 or wider, within the bound.
No kernel may reach another device: no remote copies, remote signals or barrier semaphores. Data moves between devices by JAX's collectives and lax.ppermute only.
A program may use at most 192 MiB of HBM per device.

```python
import math
import jax
import jax.numpy as jnp
from jax import lax

D = 768
H = 12
HD = 64
FF = 3072
TOK_DEV = 512
HALF = 512
SEQS = 8
LENGTH = 2048
N_CTX = 4


def draw_segments(key, part):
    key = jax.random.fold_in(key, 11)
    offset_key, whole_key = jax.random.split(key)
    offsets = jax.random.randint(offset_key, (SEQS, N_CTX - 1), TOK_DEV // 8, TOK_DEV - TOK_DEV // 8)
    starts = (jnp.arange(1, N_CTX, dtype=jnp.int32) * TOK_DEV)[None, :] + offsets
    position = jnp.arange(LENGTH, dtype=jnp.int32)
    numbers = jnp.sum((position[None, :, None] >= starts[:, None, :]).astype(jnp.int32), axis=2).astype(jnp.int32)
    single = jax.random.randint(whole_key, (), 0, SEQS)
    rows = jnp.arange(SEQS, dtype=jnp.int32)[:, None]
    return jnp.where(rows == single, 0, numbers).astype(jnp.int32)


def draw_padding(key, part):
    key = jax.random.fold_in(key, 23)
    run_length = jax.random.randint(key, (SEQS, 1), 1, HALF + 1)
    position = jnp.arange(LENGTH, dtype=jnp.int32)[None, :]
    return (position >= LENGTH - run_length).astype(jnp.int32)


def levels(stream_key, shape, pieces, low, top_value):
    def one(dim, shards_of):
        heights = jax.random.uniform(jax.random.fold_in(jax.random.fold_in(stream_key, 6), dim), (shards_of,), jnp.float32, low / len(pieces), top_value / len(pieces))
        return jnp.repeat(jnp.exp(heights), shape[dim] // shards_of).reshape((-1,) + (1,) * (len(shape) - dim - 1))

    loudness = one(*pieces[0])
    for cut in pieces[1:]:
        loudness = loudness * one(*cut)
    return loudness


def noise(key, shape, width, bound, cuts=(), kind=jnp.bfloat16):
    gain = levels(key, shape, cuts, -0.22, 0.18) if cuts else 1.0
    drawn = jax.random.normal(key, shape, jnp.float32) * width * gain
    return jnp.minimum(jnp.maximum(drawn, -bound), bound).astype(kind)


def setup_inputs(seed: int = 0) -> dict:
    splits = jax.random.split(jax.random.key(seed), 20)
    return {
        "tokens": noise(splits[0], (SEQS, LENGTH, D), 1.0, 6.0, ((0, 8), (1, 4))),
        "segments": draw_segments(jax.random.fold_in(splits[19], 71), 0),
        "padding": draw_padding(jax.random.fold_in(splits[19], 71), 0),
        "w_query": noise(splits[3], (D, D), D ** -0.5, 0.21875, ((0, 8),)),
        "w_key": noise(splits[4], (D, D), D ** -0.5, 0.21875, ((0, 8),)),
        "w_value": noise(splits[5], (D, D), D ** -0.5, 0.21875, ((0, 8),)),
        "w_out": noise(splits[6], (D, D), (D // 32) ** -0.5, 1.25, ((0, 8),)),
        "w_up": noise(splits[7], (D, FF), D ** -0.5, 0.21875, ((0, 8),)),
        "w_gate": noise(splits[8], (D, FF), D ** -0.5, 0.21875, ((0, 8),)),
        "w_down": noise(splits[9], (FF, D), FF ** -0.5, 0.109375, ((0, 8),)),
        "bias_query": noise(splits[10], (D,), 0.5, 3.0, ((0, 8),)),
        "bias_value": noise(splits[11], (D,), 0.5, 3.0, ((0, 8),)),
        "bias_out": noise(splits[12], (D,), 0.5, 3.0, ((0, 8),)),
        "bias_down": noise(splits[13], (D,), 0.5, 3.0, ((0, 8),)),
        "gain_attn": jnp.clip(1.0 + 0.15 * jax.random.normal(splits[14], (D,), jnp.float32), 0.25, 1.75).astype(jnp.bfloat16),
        "shift_attn": noise(splits[15], (D,), 0.5, 3.0, ((0, 8),)),
        "gain_ffn": jnp.clip(1.0 + 0.15 * jax.random.normal(splits[16], (D,), jnp.float32), 0.25, 1.75).astype(jnp.bfloat16),
        "shift_ffn": noise(splits[17], (D,), 0.5, 3.0, ((0, 8),)),
        "cotangent": noise(splits[18], (SEQS, LENGTH, D), 1.0, 6.0, ((0, 8), (1, 4))),
    }


EPSILON = 1e-06
EXCLUDED = -1e+30

@jax.custom_vjp
def low(v):
    return lax.optimization_barrier(v.astype(jnp.bfloat16)).astype(jnp.float32)

@jax.custom_vjp
def low_back(v):
    return v

def low_keep(v):
    return (low(v), None)

def low_pass(kept, grad):
    return (grad,)

def back_keep(v):
    return (v, None)

def back_low(kept, grad):
    return (low(grad),)
low.defvjp(low_keep, low_pass)
low_back.defvjp(back_keep, back_low)

def head_slopes(number):
    power_two = 2 ** int(math.floor(math.log2(number)))
    first_part = [2.0 ** (-8.0 * (position + 1) / power_two) for position in range(power_two)]
    extra_part = [2.0 ** (-8.0 * (2 * position + 1) / (2 * power_two)) for position in range(number - power_two)]
    return jnp.array(first_part + extra_part, dtype=jnp.float32)

def highest(left_matrix, right_matrix):
    return jnp.dot(left_matrix, right_matrix, precision=lax.Precision.HIGHEST)

def layer_norm(values, gain_vec, offset):
    centred = values - lax.optimization_barrier(jnp.mean(values, axis=-1, keepdims=True))
    variance = lax.optimization_barrier(jnp.mean(centred * centred, axis=-1, keepdims=True))
    return centred * lax.rsqrt(variance + EPSILON) * gain_vec + offset

def attention(queries, keys, values, segments, key_tags, slopes):
    block_rows = math.gcd(LENGTH, 512)
    key_span = block_rows + 2 * HALF
    edge_pad = ((HALF, HALF), (0, 0))
    keys_padded = jnp.pad(keys, edge_pad)
    values_padded = jnp.pad(values, edge_pad)
    tags_padded = jnp.pad(key_tags, (HALF, HALF), constant_values=-2)
    score_scale = 1.0 / math.sqrt(HD)

    def one_block(row_start):
        query_rows = lax.dynamic_slice_in_dim(queries, row_start, block_rows, 0).reshape(block_rows, H, HD)
        key_rows = lax.dynamic_slice_in_dim(keys_padded, row_start, key_span, 0).reshape(key_span, H, HD)
        value_rows = lax.dynamic_slice_in_dim(values_padded, row_start, key_span, 0).reshape(key_span, H, HD)
        tag_rows = lax.dynamic_slice_in_dim(tags_padded, row_start, key_span, 0)
        segment_rows = lax.dynamic_slice_in_dim(segments, row_start, block_rows, 0)
        distance = jnp.abs(jnp.arange(block_rows, dtype=jnp.int32)[:, None] + HALF - jnp.arange(key_span, dtype=jnp.int32)[None, :])
        allowed = (distance <= HALF) & (tag_rows[None, :] == segment_rows[:, None]) | (distance == 0)
        raw_scores = jnp.einsum('qhd,khd->hqk', query_rows, key_rows, precision=lax.Precision.HIGHEST) * score_scale
        raw_scores = raw_scores - slopes[:, None, None] * distance.astype(jnp.float32)[None]
        scores = jnp.where(allowed[None], low_back(raw_scores), EXCLUDED)
        largest = lax.optimization_barrier(jnp.max(scores, axis=-1, keepdims=True))
        weights = jnp.exp(scores - largest)
        probabilities = low(weights / lax.optimization_barrier(jnp.sum(weights, axis=-1, keepdims=True)))
        attended = jnp.einsum('hqk,khd->qhd', probabilities, value_rows, precision=lax.Precision.HIGHEST)
        return attended.reshape(block_rows, H * HD)
    starts = jnp.arange(LENGTH // block_rows, dtype=jnp.int32) * block_rows
    return lax.map(jax.checkpoint(one_block), starts).reshape(LENGTH, H * HD)

def forward(tokens, w_query, w_key, w_value, w_out, w_up, w_gate, w_down, bias_query, bias_value, bias_out, bias_down, gain_attn, shift_attn, gain_ffn, shift_ffn, segments, key_tags, slopes):
    queries = low(low_back(highest(tokens, w_query) + bias_query))
    keys = low(low_back(highest(tokens, w_key)))
    values = low(low_back(highest(tokens, w_value) + bias_value))
    attended = low(low_back(attention(queries, keys, values, segments, key_tags, slopes)))
    normed = layer_norm(tokens + low_back(highest(attended, w_out)) + bias_out, gain_attn, shift_attn)
    normed_low = low(normed)
    up_value = low_back(highest(normed_low, w_up))
    gate_value = low_back(highest(normed_low, w_gate))
    hidden = low(jax.nn.gelu(gate_value, approximate=False) * up_value)
    branch = low_back(highest(hidden, w_down)) + bias_down
    return layer_norm(normed + branch, gain_ffn, shift_ffn)

def reference(tokens, segments, padding, w_query, w_key, w_value, w_out, w_up, w_gate, w_down, bias_query, bias_value, bias_out, bias_down, gain_attn, shift_attn, gain_ffn, shift_ffn, cotangent):
    slopes = head_slopes(H)
    params = tuple((member.astype(jnp.float32) for member in (w_query, w_key, w_value, w_out, w_up, w_gate, w_down, bias_query, bias_value, bias_out, bias_down, gain_attn, shift_attn, gain_ffn, shift_ffn)))

    def one_sequence(totals, sequence_items):
        seq_tokens, seq_segments, seq_padding, seq_cotangent = sequence_items
        key_tags = jnp.where(seq_padding == 1, -1, seq_segments).astype(jnp.int32)

        def layer(inputs, *weights):
            return forward(inputs, *weights, seq_segments, key_tags, slopes)
        result, pullback = jax.vjp(layer, seq_tokens.astype(jnp.float32), *params)
        gradients = pullback(seq_cotangent.astype(jnp.float32))
        totals = tuple((running + gradient for running, gradient in zip(totals, gradients[1:])))
        return (totals, (result.astype(jnp.bfloat16), gradients[0]))
    initial = tuple((jnp.zeros_like(member) for member in params))
    totals, (layer_out, grad_tokens) = lax.scan(one_sequence, initial, (tokens, segments, padding, cotangent))
    return (layer_out, grad_tokens, totals[0], totals[1], totals[2], totals[3], totals[4], totals[5], totals[6], totals[7], totals[8], totals[9], totals[10], totals[11], totals[12], totals[13], totals[14])
```

```python
import math
import jax
import jax.numpy as jnp
from jax import lax
from jax.experimental import pallas as pl
from jax.experimental.pallas import tpu as pltpu
from jax.sharding import PartitionSpec as P

H = 12
HD = 64
FF = 3072
HALF = 512
QB = 256
BIG = 1e30
VMEM_LIMIT = 56 * 1024 * 1024


def dot_nn(a, b):
    return lax.dot_general(a, b, (((1,), (0,)), ((), ())), preferred_element_type=jnp.float32)


def dot_nt(a, b):
    return lax.dot_general(a, b, (((1,), (1,)), ((), ())), preferred_element_type=jnp.float32)


def dot_tn(a, b):
    return lax.dot_general(a, b, (((0,), (0,)), ((), ())), preferred_element_type=jnp.float32)


def fill_distance(dist, seg_ref, tag_ref, span):
    blocks = dist.shape[0]
    for b in range(blocks):
        base = b * QB
        key_pos = lax.broadcasted_iota(jnp.int32, (span, QB), 0)
        row_pos = lax.broadcasted_iota(jnp.int32, (span, QB), 1) + HALF
        gap = jnp.abs(key_pos - row_pos)
        same = tag_ref[base : base + span, :] == seg_ref[:, base : base + QB]
        kept = ((gap <= HALF) & same) | (gap == 0)
        dist[b] = jnp.where(kept, gap.astype(jnp.float32), BIG)


def attn_fwd_kernel(slopes, q_ref, k_ref, v_ref, seg_ref, tag_ref, out_ref, lse_ref, dist):
    rows = q_ref.shape[0]
    span = QB + 2 * HALF
    pair = pl.program_id(0)

    @pl.when(pair == 0)
    def _():
        fill_distance(dist, seg_ref, tag_ref, span)

    lane = lax.broadcasted_iota(jnp.int32, (QB, 2 * HD), 1)
    v_t = v_ref[...].T
    for b in range(rows // QB):
        base = b * QB
        q = q_ref[base : base + QB, :]
        k = k_ref[base : base + span, :]
        parts = []
        for a in range(2):
            mine = (lane >= HD) if a else (lane < HD)
            q_a = jnp.where(mine, q, jnp.zeros_like(q)) * jnp.asarray(1.0 / math.sqrt(HD), q.dtype)
            s = dot_nt(k, q_a) - slopes[2 * pair + a] * dist[b]
            top = jnp.max(s, axis=0, keepdims=True)
            p = jnp.exp(s - top)
            total = jnp.sum(p, axis=0, keepdims=True)
            o_t = dot_nn(v_t[a * HD : (a + 1) * HD, base : base + span], p.astype(jnp.bfloat16))
            parts.append(o_t * (1.0 / total))
            lse_ref[0, a : a + 1, base : base + QB] = top + jnp.log(total)
        out_ref[base : base + QB, :] = jnp.concatenate(parts, axis=0).T.astype(jnp.bfloat16)


def attention_forward(queries, keys, values, seg_row, tag_col, slopes):
    rows, width = queries.shape
    ext = keys.shape[0]
    span = QB + 2 * HALF
    pairs = width // (2 * HD)
    return pl.pallas_call(
        attn_fwd_kernel,
        grid=(pairs,),
        in_specs=[
            pl.BlockSpec(memory_space=pltpu.SMEM),
            pl.BlockSpec((rows, 2 * HD), lambda h: (0, h)),
            pl.BlockSpec((ext, 2 * HD), lambda h: (0, h)),
            pl.BlockSpec((ext, 2 * HD), lambda h: (0, h)),
            pl.BlockSpec((1, rows), lambda h: (0, 0)),
            pl.BlockSpec((ext, 1), lambda h: (0, 0)),
        ],
        out_specs=[
            pl.BlockSpec((rows, 2 * HD), lambda h: (0, h)),
            pl.BlockSpec((1, 8, rows), lambda h: (h, 0, 0)),
        ],
        out_shape=[
            jax.ShapeDtypeStruct((rows, width), jnp.bfloat16),
            jax.ShapeDtypeStruct((pairs, 8, rows), jnp.float32),
        ],
        scratch_shapes=[pltpu.VMEM((rows // QB, span, QB), jnp.float32)],
        compiler_params=pltpu.CompilerParams(vmem_limit_bytes=VMEM_LIMIT),
        cost_estimate=pl.CostEstimate(
            flops=4 * 2 * H * rows * span * HD, bytes_accessed=12 * ext * width, transcendentals=H * rows * span
        ),
    )(slopes, queries, keys, values, seg_row, tag_col)


def attn_bwd_kernel(
    slopes, q_ref, k_ref, v_ref, o_ref, do_ref, lse_ref, seg_ref, tag_ref,
    dq_ref, low_ref, mid_ref, high_ref, dist, dk_acc, dv_acc,
):
    rows = q_ref.shape[0]
    span = QB + 2 * HALF
    pair = pl.program_id(0)

    @pl.when(pair == 0)
    def _():
        fill_distance(dist, seg_ref, tag_ref, span)

    lane = lax.broadcasted_iota(jnp.int32, (QB, 2 * HD), 1)
    lane_one = lax.broadcasted_iota(jnp.int32, (8, 2 * HD), 1)
    k_t = k_ref[...].T
    scale = 1.0 / math.sqrt(HD)
    dk_acc[...] = jnp.zeros_like(dk_acc)
    dv_acc[...] = jnp.zeros_like(dv_acc)
    for b in range(rows // QB):
        base = b * QB
        q = q_ref[base : base + QB, :] * jnp.asarray(scale, jnp.bfloat16)
        do = do_ref[base : base + QB, :]
        k = k_ref[base : base + span, :]
        v = v_ref[base : base + span, :]
        mixed = do.astype(jnp.float32) * o_ref[base : base + QB, :].astype(jnp.float32)
        parts = []
        ps = []
        dss = []
        qs = []
        dos = []
        for a in range(2):
            mine = (lane >= HD) if a else (lane < HD)
            mine_one = (lane_one >= HD) if a else (lane_one < HD)
            q_a = jnp.where(mine, q, jnp.zeros_like(q))
            do_a = jnp.where(mine, do, jnp.zeros_like(do))
            delta = lax.dot_general(
                mine_one.astype(jnp.float32), mixed, (((1,), (1,)), ((), ())),
                preferred_element_type=jnp.float32, precision=lax.Precision.HIGHEST,
            )[0:1]
            s = dot_nt(k, q_a) - slopes[2 * pair + a] * dist[b]
            p = jnp.exp(s - lse_ref[0, a : a + 1, base : base + QB])
            dp = dot_nt(v, do_a)
            ds = (p * (dp - delta)).astype(jnp.bfloat16)
            parts.append(dot_nn(k_t[a * HD : (a + 1) * HD, base : base + span], ds) * scale)
            ps.append(p.astype(jnp.bfloat16))
            dss.append(ds)
            qs.append(q_a)
            dos.append(do_a)
        dq_ref[base : base + QB, :] = jnp.concatenate(parts, axis=0).T.astype(jnp.bfloat16)
        dk_acc[base : base + span, :] += dot_nn(
            jnp.concatenate(dss, axis=1), jnp.concatenate(qs, axis=0)
        )
        dv_acc[base : base + span, :] += dot_nn(
            jnp.concatenate(ps, axis=1), jnp.concatenate(dos, axis=0)
        )
    low_ref[0] = dk_acc[:HALF, :].astype(jnp.bfloat16)
    low_ref[1] = dv_acc[:HALF, :].astype(jnp.bfloat16)
    mid_ref[0] = dk_acc[HALF : HALF + rows, :]
    mid_ref[1] = dv_acc[HALF : HALF + rows, :]
    high_ref[0] = dk_acc[HALF + rows :, :].astype(jnp.bfloat16)
    high_ref[1] = dv_acc[HALF + rows :, :].astype(jnp.bfloat16)


def attention_backward(queries, keys, values, attended, grad_attended, lse, seg_row, tag_col, slopes):
    rows, width = queries.shape
    ext = keys.shape[0]
    span = QB + 2 * HALF
    pairs = width // (2 * HD)
    row_spec = pl.BlockSpec((rows, 2 * HD), lambda h: (0, h))
    ext_spec = pl.BlockSpec((ext, 2 * HD), lambda h: (0, h))
    return pl.pallas_call(
        attn_bwd_kernel,
        grid=(pairs,),
        in_specs=[
            pl.BlockSpec(memory_space=pltpu.SMEM),
            row_spec, ext_spec, ext_spec, row_spec, row_spec,
            pl.BlockSpec((1, 8, rows), lambda h: (h, 0, 0)),
            pl.BlockSpec((1, rows), lambda h: (0, 0)),
            pl.BlockSpec((ext, 1), lambda h: (0, 0)),
        ],
        out_specs=[
            row_spec,
            pl.BlockSpec((2, HALF, 2 * HD), lambda h: (0, 0, h)),
            pl.BlockSpec((2, rows, 2 * HD), lambda h: (0, 0, h)),
            pl.BlockSpec((2, HALF, 2 * HD), lambda h: (0, 0, h)),
        ],
        out_shape=[
            jax.ShapeDtypeStruct((rows, width), jnp.bfloat16),
            jax.ShapeDtypeStruct((2, HALF, width), jnp.bfloat16),
            jax.ShapeDtypeStruct((2, rows, width), jnp.float32),
            jax.ShapeDtypeStruct((2, HALF, width), jnp.bfloat16),
        ],
        scratch_shapes=[
            pltpu.VMEM((rows // QB, span, QB), jnp.float32),
            pltpu.VMEM((ext, 2 * HD), jnp.float32),
            pltpu.VMEM((ext, 2 * HD), jnp.float32),
        ],
        compiler_params=pltpu.CompilerParams(vmem_limit_bytes=VMEM_LIMIT),
        cost_estimate=pl.CostEstimate(
            flops=10 * 2 * H * rows * span * HD, bytes_accessed=20 * ext * width, transcendentals=H * rows * span
        ),
    )(slopes, queries, keys, values, attended, grad_attended, lse, seg_row, tag_col)


EPSILON = 1e-06
VECTORS = 8


def head_slopes(number):
    power_two = 2 ** int(math.floor(math.log2(number)))
    first_part = [2.0 ** (-8.0 * (position + 1) / power_two) for position in range(power_two)]
    extra_part = [
        2.0 ** (-8.0 * (2 * position + 1) / (2 * power_two))
        for position in range(number - power_two)
    ]
    return jnp.array(first_part + extra_part, dtype=jnp.float32)


def from_previous(x):
    count = lax.axis_size("ctx")
    return lax.ppermute(x, "ctx", [(i, i + 1) for i in range(count - 1)])


def from_next(x):
    count = lax.axis_size("ctx")
    return lax.ppermute(x, "ctx", [(i + 1, i) for i in range(count - 1)])


def norm_parts(values, gain_vec, offset):
    centred = values - jnp.mean(values, axis=-1, keepdims=True)
    variance = jnp.mean(centred * centred, axis=-1, keepdims=True)
    inverse = lax.rsqrt(variance + EPSILON)
    normed = centred * inverse
    return (normed * gain_vec + offset, normed, inverse)


def norm_back(upstream, normed, inverse, gain_vec):
    scaled = upstream * gain_vec
    row_inner = (
        scaled
        - jnp.mean(scaled, axis=-1, keepdims=True)
        - normed * jnp.mean(scaled * normed, axis=-1, keepdims=True)
    )
    return (row_inner * inverse, jnp.sum(upstream * normed, axis=0), jnp.sum(upstream, axis=0))


def gelu_product(gate_value, up_value):
    return jax.nn.gelu(gate_value, approximate=False) * up_value


def gather_rows(shard):
    count = lax.axis_size("ctx")
    part = shard.shape[0] // count
    mine = lax.dynamic_slice_in_dim(shard, lax.axis_index("ctx") * part, part, 0)
    return lax.all_gather(mine, ("fsdp", "ctx"), axis=0, tiled=True)


def scatter_rows(full):
    return lax.psum_scatter(
        full.astype(jnp.bfloat16), ("fsdp", "ctx"), scatter_dimension=0, tiled=True
    )


def on_device(
    tokens, segments, padding,
    w_query, w_key, w_value, w_out, w_up, w_gate, w_down,
    bias_query, bias_value, bias_out, bias_down, gain_attn, shift_attn, gain_ffn, shift_ffn,
    cotangent,
):
    inputs = tokens[0]
    rows, width = inputs.shape
    segment_rows = segments[0]
    key_tags = jnp.where(padding[0] == 1, -1, segment_rows)
    tag_low = from_previous(key_tags + 2) - 2
    tag_high = from_next(key_tags + 2) - 2
    tag_col = jnp.concatenate([tag_low, key_tags, tag_high])[:, None]
    seg_row = segment_rows[None, :]
    slopes = head_slopes(H)

    vectors = jnp.stack(
        (bias_query, bias_value, bias_out, bias_down, gain_attn, shift_attn, gain_ffn, shift_ffn), axis=1
    )
    vectors = jnp.pad(vectors, ((0, 0), (0, 128 - VECTORS)))
    full_first = gather_rows(jnp.concatenate((w_query, w_key, w_value, vectors), axis=1))
    full_qkv = full_first[:, : 3 * width]
    vec = full_first[:, 3 * width : 3 * width + VECTORS].T.astype(jnp.float32)
    query_bias, value_bias, out_bias, down_bias, attn_gain, attn_shift, ffn_gain, ffn_shift = [
        vec[i] for i in range(VECTORS)
    ]
    full_mid = gather_rows(jnp.concatenate((w_out, w_up, w_gate), axis=1))
    full_out = full_mid[:, :width]
    full_up_gate = full_mid[:, width:]
    full_down = gather_rows(w_down)

    projected = dot_nn(inputs, full_qkv)
    queries = (projected[:, :width] + query_bias).astype(jnp.bfloat16)
    keys_values = jnp.concatenate(
        (projected[:, width : 2 * width], projected[:, 2 * width :] + value_bias), axis=1
    ).astype(jnp.bfloat16)
    kv_low = from_previous(keys_values[rows - HALF :])
    kv_high = from_next(keys_values[:HALF])
    kv = jnp.concatenate([kv_low, keys_values, kv_high], axis=0)
    keys_ext = kv[:, :width]
    values_ext = kv[:, width:]
    attended, lse = attention_forward(queries, keys_ext, values_ext, seg_row, tag_col, slopes)

    attn_branch = dot_nn(attended, full_out) + out_bias
    first_norm, first_normed, first_inverse = norm_parts(
        inputs.astype(jnp.float32) + attn_branch, attn_gain, attn_shift
    )
    normed_low = first_norm.astype(jnp.bfloat16)
    up_gate = dot_nn(normed_low, full_up_gate)
    up_value = up_gate[:, :FF]
    gate_value = up_gate[:, FF:]
    hidden = gelu_product(gate_value, up_value).astype(jnp.bfloat16)
    ffn_branch = dot_nn(hidden, full_down) + down_bias
    output_value, second_normed, second_inverse = norm_parts(
        first_norm + ffn_branch, ffn_gain, ffn_shift
    )
    layer_out = output_value.astype(jnp.bfloat16)

    upstream = cotangent[0].astype(jnp.float32)
    grad_second, grad_ffn_gain, grad_ffn_shift = norm_back(
        upstream, second_normed, second_inverse, ffn_gain
    )
    grad_down_bias = jnp.sum(grad_second, axis=0)
    grad_branch = grad_second.astype(jnp.bfloat16)
    shard_down = scatter_rows(dot_tn(hidden, grad_branch))

    hidden_grad = dot_nt(grad_branch, full_down)
    unused_value, pullback = jax.vjp(gelu_product, gate_value, up_value)
    grad_gate, grad_up = pullback(hidden_grad)
    grad_up_gate = jnp.concatenate((grad_up, grad_gate), axis=1).astype(jnp.bfloat16)
    shard_up_gate = scatter_rows(dot_tn(normed_low, grad_up_gate))
    grad_normed = grad_second + dot_nt(grad_up_gate, full_up_gate)
    grad_first, grad_attn_gain, grad_attn_shift = norm_back(
        grad_normed, first_normed, first_inverse, attn_gain
    )
    grad_out_bias = jnp.sum(grad_first, axis=0)
    grad_attn_low = grad_first.astype(jnp.bfloat16)
    grad_w_out = dot_tn(attended, grad_attn_low)
    grad_attended = dot_nt(grad_attn_low, full_out).astype(jnp.bfloat16)

    grad_queries, low, mid, high = attention_backward(
        queries, keys_ext, values_ext, attended, grad_attended, lse, seg_row, tag_col, slopes
    )
    centre = mid.at[:, rows - HALF :].add(from_next(low).astype(jnp.float32))
    centre = centre.at[:, :HALF].add(from_previous(high).astype(jnp.float32)).astype(jnp.bfloat16)
    grad_qkv = jnp.concatenate((grad_queries, centre[0], centre[1]), axis=1)
    grad_w_qkv = dot_tn(inputs, grad_qkv)
    grad_query_bias = jnp.sum(grad_queries.astype(jnp.float32), axis=0)
    grad_value_bias = jnp.sum(centre[1].astype(jnp.float32), axis=0)
    grad_vectors = jnp.stack(
        (
            grad_query_bias, grad_value_bias, grad_out_bias, grad_down_bias,
            grad_attn_gain, grad_attn_shift, grad_ffn_gain, grad_ffn_shift,
        ),
        axis=1,
    )
    grad_vectors = jnp.pad(grad_vectors, ((0, 0), (0, 128 - VECTORS)))
    shard_last = scatter_rows(jnp.concatenate((grad_w_qkv, grad_w_out, grad_vectors), axis=1))
    grad_inputs = grad_first + dot_nt(grad_qkv, full_qkv)

    def whole(shard):
        return lax.all_gather(shard, "ctx", axis=0, tiled=True).astype(jnp.float32)

    down = whole(shard_down)
    up_gate_rows = whole(shard_up_gate)
    last = whole(shard_last)
    return (
        layer_out[None],
        grad_inputs[None],
        last[:, :width],
        last[:, width : 2 * width],
        last[:, 2 * width : 3 * width],
        last[:, 3 * width : 4 * width],
        up_gate_rows[:, :FF],
        up_gate_rows[:, FF:],
        down,
    ) + tuple(last[:, 4 * width + i] for i in range(VECTORS))


def solution(mesh):
    rows_spec = P("fsdp", "ctx", None)
    in_specs = (
        (rows_spec, P("fsdp", "ctx"), P("fsdp", "ctx"))
        + (P("fsdp", None),) * 7
        + (P("fsdp"),) * VECTORS
        + (rows_spec,)
    )
    out_specs = (rows_spec, rows_spec) + (P("fsdp", None),) * 7 + (P("fsdp"),) * VECTORS
    return jax.shard_map(
        on_device, mesh=mesh, in_specs=in_specs, out_specs=out_specs, check_vma=False
    )
```

```python
import math
import jax
import jax.numpy as jnp
from jax import lax
from jax.experimental import pallas as pl
from jax.experimental.pallas import tpu as pltpu
from jax.sharding import PartitionSpec as P

H = 12
HD = 64
FF = 3072
HALF = 512
EPSILON = 1e-06
VECTORS = 8
QB = 256
SPAN = QB + 2 * HALF
BIG = 1e30
VMEM_LIMIT = 56 * 1024 * 1024

Z_SWAP = ((0, 1), (1, 0), (2, 3), (3, 2))
Z_MID = ((1, 2), (2, 1))
Z_OUT = ((1, 0), (2, 3))
Z_IN = ((0, 1), (3, 2))


def dot_nn(a, b):
    return lax.dot_general(a, b, (((1,), (0,)), ((), ())), preferred_element_type=jnp.float32)


def dot_nt(a, b):
    return lax.dot_general(a, b, (((1,), (1,)), ((), ())), preferred_element_type=jnp.float32)


def dot_tn(a, b):
    return lax.dot_general(a, b, (((0,), (0,)), ((), ())), preferred_element_type=jnp.float32)


def tie(*values):
    return lax.optimization_barrier(values)


def head_slopes(number):
    power_two = 2 ** int(math.floor(math.log2(number)))
    first_part = [2.0 ** (-8.0 * (position + 1) / power_two) for position in range(power_two)]
    extra_part = [
        2.0 ** (-8.0 * (2 * position + 1) / (2 * power_two))
        for position in range(number - power_two)
    ]
    return jnp.array(first_part + extra_part, dtype=jnp.float32)


def over_core(x):
    count = lax.axis_size("ctx")
    return lax.ppermute(x, "ctx", [(i, i ^ 1) for i in range(count)])


def from_previous_chip(x):
    count = lax.axis_size("ctx")
    return lax.ppermute(x, "ctx", [(i, i + 2) for i in range(count - 2)])


def from_next_chip(x):
    count = lax.axis_size("ctx")
    return lax.ppermute(x, "ctx", [(i + 2, i) for i in range(count - 2)])


def over_x(x):
    return lax.ppermute(x, "ctx", [(i, i ^ 2) for i in range(4)])


def over_y(x):
    return lax.ppermute(x, "fsdp", [(i, i ^ 1) for i in range(8)])


def over_z(x, moves):
    return lax.ppermute(
        x, "fsdp", [(2 * a + y, 2 * b + y) for a, b in moves for y in range(2)]
    )


def ordered(core, own, other, axis):
    return jnp.where(
        core == 0,
        jnp.concatenate([own, other], axis=axis),
        jnp.concatenate([other, own], axis=axis),
    )


def shard_number(k, dy):
    me = lax.axis_index("fsdp")
    return me ^ (2 * k + dy)


def place_kernel(numbers, *refs):
    pieces, out, sems = refs[:8], refs[8], refs[9]
    rows = pieces[0].shape[0]
    copies = [
        pltpu.make_async_copy(
            piece, out.at[pl.ds(pl.multiple_of(numbers[i] * rows, rows), rows), :], sems.at[i]
        )
        for i, piece in enumerate(pieces)
    ]
    for copy in copies:
        copy.start()
    for copy in copies:
        copy.wait()


def place(pieces):
    rows, width = pieces[0].shape
    numbers = jnp.stack([shard_number(k, dy) for dy in range(2) for k in range(4)])
    return pl.pallas_call(
        place_kernel,
        in_specs=[pl.BlockSpec(memory_space=pltpu.SMEM)] + [pl.BlockSpec(memory_space=pl.ANY)] * 8,
        out_specs=pl.BlockSpec(memory_space=pl.ANY),
        out_shape=jax.ShapeDtypeStruct((8 * rows, width), pieces[0].dtype),
        scratch_shapes=[pltpu.SemaphoreType.DMA((8,))],
        cost_estimate=pl.CostEstimate(
            flops=0, bytes_accessed=4 * 8 * rows * width, transcendentals=0
        ),
    )(numbers, *pieces)


class Gather:
    def __init__(self, piece):
        self.own = piece

    def first(self):
        self.y0, self.a, self.b = tie(
            over_y(self.own), over_z(self.own, Z_SWAP), over_z(self.own, Z_MID)
        )

    def second(self):
        self.c, d, self.ya = tie(
            over_z(self.a, Z_MID), over_z(self.b, Z_OUT), over_y(self.a)
        )
        self.z2 = self.c + d

    def third(self):
        e, self.yz2 = tie(over_z(self.c, Z_OUT), over_y(self.z2))
        self.z3 = self.b + e

    def fourth(self):
        self.yz3 = over_y(self.z3)

    def result(self):
        return place(
            [self.own, self.a, self.z2, self.z3, self.y0, self.ya, self.yz2, self.yz3]
        )


class Reduce:
    def __init__(self, full):
        self.full = full
        self.rows = full.shape[0] // 8

    def part(self, k, dy):
        return lax.dynamic_slice_in_dim(
            self.full, shard_number(k, dy) * self.rows, self.rows, 0
        )

    def first(self):
        self.q3 = self.part(3, 0) + over_y(self.part(3, 1))

    def second(self):
        y2, self.e = tie(over_y(self.part(2, 1)), over_z(self.q3, Z_IN))
        self.q2 = self.part(2, 0) + y2

    def third(self):
        y1, self.d, self.c = tie(
            over_y(self.part(1, 1)), over_z(self.q2, Z_IN), over_z(self.q2 + self.e, Z_MID)
        )
        self.q1 = self.part(1, 0) + y1

    def fourth(self):
        y0, b, a = tie(
            over_y(self.part(0, 1)),
            over_z(self.q3 + self.d, Z_MID),
            over_z(self.q1 + self.c, Z_SWAP),
        )
        self.total = self.part(0, 0) + y0 + a + b

    def result(self):
        return self.total


class PlainGather:
    def __init__(self, piece):
        self.own = piece

    def first(self):
        pass

    second = third = fourth = first

    def result(self):
        return lax.all_gather(self.own, "fsdp", axis=0, tiled=True)


class PlainReduce:
    def __init__(self, full):
        self.full = full

    def first(self):
        pass

    second = third = fourth = first

    def result(self):
        return lax.psum_scatter(self.full, "fsdp", scatter_dimension=0, tiled=True)


def both_cores(total, core):
    count = lax.axis_size("ctx")
    if count == 4:
        total = total + over_x(total)
        other = over_core(total)
        first = jnp.where(core == 0, total, other)
        second = jnp.where(core == 0, other, total)
        return first.astype(jnp.float32), second.astype(jnp.float32)
    slots = jnp.stack(
        [jnp.where(core == i, total, jnp.zeros_like(total)) for i in range(2)]
    )
    slots = lax.psum(slots, "ctx").astype(jnp.float32)
    return slots[0], slots[1]


def fill_distance(dist, seg_ref, tag_ref, first_row):
    for b in range(dist.shape[0]):
        base = first_row + b * QB
        key_pos = lax.broadcasted_iota(jnp.int32, (SPAN, QB), 0)
        row_pos = lax.broadcasted_iota(jnp.int32, (SPAN, QB), 1) + HALF
        gap = jnp.abs(key_pos - row_pos)
        same = tag_ref[base : base + SPAN, :] == seg_ref[:, b * QB : (b + 1) * QB]
        kept = ((gap <= HALF) & same) | (gap == 0)
        dist[b] = jnp.where(kept, gap.astype(jnp.float32), BIG)


def attn_fwd_kernel(
    first_row, slopes, q_ref, k_ref, v_ref, seg_ref, tag_ref, out_ref, lse_ref, dist
):
    rows = q_ref.shape[0]
    pair = pl.program_id(0)

    @pl.when(pair == 0)
    def _():
        fill_distance(dist, seg_ref, tag_ref, first_row)

    lane = lax.broadcasted_iota(jnp.int32, (QB, 2 * HD), 1)
    v_t = v_ref[first_row : first_row + rows + 2 * HALF, :].T
    for b in range(rows // QB):
        base = b * QB
        q = q_ref[base : base + QB, :]
        k = k_ref[first_row + base : first_row + base + SPAN, :]
        parts = []
        for a in range(2):
            mine = (lane >= HD) if a else (lane < HD)
            q_a = jnp.where(mine, q, jnp.zeros_like(q)) * jnp.asarray(1.0 / math.sqrt(HD), q.dtype)
            s = dot_nt(k, q_a) - slopes[2 * pair + a] * dist[b]
            top = jnp.max(s, axis=0, keepdims=True)
            p = jnp.exp(s - top)
            total = jnp.sum(p, axis=0, keepdims=True)
            o_t = dot_nn(v_t[a * HD : (a + 1) * HD, base : base + SPAN], p.astype(jnp.bfloat16))
            parts.append(o_t * (1.0 / total))
            lse_ref[0, a : a + 1, base : base + QB] = top + jnp.log(total)
        out_ref[base : base + QB, :] = jnp.concatenate(parts, axis=0).T.astype(jnp.bfloat16)


def attention_forward(part, queries, kv_ext, seg_row, tag_col, slopes):
    rows = HALF
    width = queries.shape[1]
    ext = kv_ext.shape[0]
    pairs = width // (2 * HD)

    def body(*refs):
        attn_fwd_kernel(part * rows, *refs)

    return pl.pallas_call(
        body,
        grid=(pairs,),
        in_specs=[
            pl.BlockSpec(memory_space=pltpu.SMEM),
            pl.BlockSpec((rows, 2 * HD), lambda h: (part, h)),
            pl.BlockSpec((ext, 2 * HD), lambda h: (0, h)),
            pl.BlockSpec((ext, 2 * HD), lambda h: (0, pairs + h)),
            pl.BlockSpec((1, rows), lambda h: (0, part)),
            pl.BlockSpec((ext, 1), lambda h: (0, 0)),
        ],
        out_specs=[
            pl.BlockSpec((rows, 2 * HD), lambda h: (0, h)),
            pl.BlockSpec((1, 8, rows), lambda h: (h, 0, 0)),
        ],
        out_shape=[
            jax.ShapeDtypeStruct((rows, width), jnp.bfloat16),
            jax.ShapeDtypeStruct((pairs, 8, rows), jnp.float32),
        ],
        scratch_shapes=[pltpu.VMEM((rows // QB, SPAN, QB), jnp.float32)],
        compiler_params=pltpu.CompilerParams(vmem_limit_bytes=VMEM_LIMIT),
        cost_estimate=pl.CostEstimate(
            flops=16 * pairs * rows * SPAN * HD,
            bytes_accessed=8 * ext * width,
            transcendentals=2 * pairs * rows * SPAN,
        ),
    )(slopes, queries, kv_ext, kv_ext, seg_row, tag_col)


def attn_bwd_kernel(
    first_row, slopes, q_ref, k_ref, v_ref, o_ref, do_ref, lse_ref, seg_ref, tag_ref,
    dq_ref, dk_ref, dv_ref, dist,
):
    rows = q_ref.shape[0]
    pair = pl.program_id(0)

    @pl.when(pair == 0)
    def _():
        fill_distance(dist, seg_ref, tag_ref, first_row)

    lane = lax.broadcasted_iota(jnp.int32, (QB, 2 * HD), 1)
    lane_one = lax.broadcasted_iota(jnp.int32, (8, 2 * HD), 1)
    k_t = k_ref[first_row : first_row + rows + 2 * HALF, :].T
    scale = 1.0 / math.sqrt(HD)
    dk_ref[...] = jnp.zeros_like(dk_ref)
    dv_ref[...] = jnp.zeros_like(dv_ref)
    for b in range(rows // QB):
        base = b * QB
        q = q_ref[base : base + QB, :] * jnp.asarray(scale, jnp.bfloat16)
        do = do_ref[base : base + QB, :]
        k = k_ref[first_row + base : first_row + base + SPAN, :]
        v = v_ref[first_row + base : first_row + base + SPAN, :]
        mixed = do.astype(jnp.float32) * o_ref[base : base + QB, :].astype(jnp.float32)
        parts = []
        ps = []
        dss = []
        qs = []
        dos = []
        for a in range(2):
            mine = (lane >= HD) if a else (lane < HD)
            mine_one = (lane_one >= HD) if a else (lane_one < HD)
            q_a = jnp.where(mine, q, jnp.zeros_like(q))
            do_a = jnp.where(mine, do, jnp.zeros_like(do))
            delta = lax.dot_general(
                mine_one.astype(jnp.float32), mixed, (((1,), (1,)), ((), ())),
                preferred_element_type=jnp.float32, precision=lax.Precision.HIGHEST,
            )[0:1]
            s = dot_nt(k, q_a) - slopes[2 * pair + a] * dist[b]
            p = jnp.exp(s - lse_ref[0, a : a + 1, base : base + QB])
            dp = dot_nt(v, do_a)
            ds = (p * (dp - delta)).astype(jnp.bfloat16)
            parts.append(dot_nn(k_t[a * HD : (a + 1) * HD, base : base + SPAN], ds) * scale)
            ps.append(p.astype(jnp.bfloat16))
            dss.append(ds)
            qs.append(q_a)
            dos.append(do_a)
        dq_ref[base : base + QB, :] = jnp.concatenate(parts, axis=0).T.astype(jnp.bfloat16)
        dk_ref[base : base + SPAN, :] += dot_nn(
            jnp.concatenate(dss, axis=1), jnp.concatenate(qs, axis=0)
        )
        dv_ref[base : base + SPAN, :] += dot_nn(
            jnp.concatenate(ps, axis=1), jnp.concatenate(dos, axis=0)
        )


def attention_backward(part, queries, kv_ext, attended, grad_attended, lse, seg_row, tag_col, slopes):
    rows = HALF
    width = queries.shape[1]
    ext = kv_ext.shape[0]
    reach = rows + 2 * HALF
    pairs = width // (2 * HD)

    def body(*refs):
        attn_bwd_kernel(part * rows, *refs)

    return pl.pallas_call(
        body,
        grid=(pairs,),
        in_specs=[
            pl.BlockSpec(memory_space=pltpu.SMEM),
            pl.BlockSpec((rows, 2 * HD), lambda h: (part, h)),
            pl.BlockSpec((ext, 2 * HD), lambda h: (0, h)),
            pl.BlockSpec((ext, 2 * HD), lambda h: (0, pairs + h)),
            pl.BlockSpec((rows, 2 * HD), lambda h: (0, h)),
            pl.BlockSpec((rows, 2 * HD), lambda h: (part, h)),
            pl.BlockSpec((1, 8, rows), lambda h: (h, 0, 0)),
            pl.BlockSpec((1, rows), lambda h: (0, part)),
            pl.BlockSpec((ext, 1), lambda h: (0, 0)),
        ],
        out_specs=[
            pl.BlockSpec((rows, 2 * HD), lambda h: (0, h)),
            pl.BlockSpec((reach, 2 * HD), lambda h: (0, h)),
            pl.BlockSpec((reach, 2 * HD), lambda h: (0, h)),
        ],
        out_shape=[
            jax.ShapeDtypeStruct((rows, width), jnp.bfloat16),
            jax.ShapeDtypeStruct((reach, width), jnp.float32),
            jax.ShapeDtypeStruct((reach, width), jnp.float32),
        ],
        scratch_shapes=[pltpu.VMEM((rows // QB, SPAN, QB), jnp.float32)],
        compiler_params=pltpu.CompilerParams(vmem_limit_bytes=VMEM_LIMIT),
        cost_estimate=pl.CostEstimate(
            flops=40 * pairs * rows * SPAN * HD,
            bytes_accessed=16 * ext * width,
            transcendentals=2 * pairs * rows * SPAN,
        ),
    )(slopes, queries, kv_ext, kv_ext, attended, grad_attended, lse, seg_row, tag_col)


def norm_parts(values, gain_vec, offset):
    centred = values - jnp.mean(values, axis=-1, keepdims=True)
    variance = jnp.mean(centred * centred, axis=-1, keepdims=True)
    inverse = lax.rsqrt(variance + EPSILON)
    normed = centred * inverse
    return (normed * gain_vec + offset, normed, inverse)


def norm_back(upstream, normed, inverse, gain_vec):
    scaled = upstream * gain_vec
    row_inner = (
        scaled
        - jnp.mean(scaled, axis=-1, keepdims=True)
        - normed * jnp.mean(scaled * normed, axis=-1, keepdims=True)
    )
    return (row_inner * inverse, jnp.sum(upstream * normed, axis=0), jnp.sum(upstream, axis=0))


def gelu_product(gate_value, up_value):
    return jax.nn.gelu(gate_value, approximate=False) * up_value


def on_device(
    tokens, segments, padding,
    w_query, w_key, w_value, w_out, w_up, w_gate, w_down,
    bias_query, bias_value, bias_out, bias_down, gain_attn, shift_attn, gain_ffn, shift_ffn,
    cotangent,
):
    tuned = lax.axis_size("ctx") == 4 and lax.axis_size("fsdp") == 8
    row_gather, row_reduce = (Gather, Reduce) if tuned else (PlainGather, PlainReduce)
    core = lax.axis_index("ctx") % 2
    inputs = tokens[0]
    rows, width = inputs.shape
    half = width // 2
    half_ff = FF // 2

    def my_columns(matrix, count):
        return lax.dynamic_slice_in_dim(matrix, core * count, count, 1)

    def my_rows(matrix):
        return lax.dynamic_slice_in_dim(matrix, core * rows, rows, 0)

    def other_rows(matrix):
        return lax.dynamic_slice_in_dim(matrix, (1 - core) * rows, rows, 0)

    vectors = jnp.stack(
        (bias_query, bias_value, bias_out, bias_down, gain_attn, shift_attn, gain_ffn, shift_ffn), axis=1
    )
    vectors = jnp.pad(vectors, ((0, 0), (0, 128 - VECTORS)))
    first_piece = jnp.concatenate(
        [my_columns(w, half) for w in (w_query, w_key, w_value)] + [vectors], axis=1
    )
    second_piece = jnp.concatenate(
        [my_columns(w_up, half_ff), my_columns(w_gate, half_ff), my_columns(w_out, half)], axis=1
    )
    shard_down = w_down.shape[0]
    down_piece = lax.dynamic_slice_in_dim(w_down, core * (shard_down // 2), shard_down // 2, 0)
    down_halves = lax.all_gather(down_piece, "fsdp", axis=0)

    first = row_gather(first_piece)
    first.first()
    first.second()
    first.third()
    if tuned:
        first.z3, second_piece = tie(first.z3, second_piece)
    first.fourth()
    second = row_gather(second_piece)
    second.first()

    own_numbers = jnp.stack((segments[0], jnp.where(padding[0] == 1, -1, segments[0])))
    numbers = ordered(core, own_numbers, over_core(own_numbers), 1)
    tags = numbers[1]
    tag_low = from_previous_chip(tags[rows:] + 2) - 2
    tag_high = from_next_chip(tags[:rows] + 2) - 2
    tag_col = jnp.concatenate([tag_low, tags, tag_high])[:, None]
    seg_row = numbers[0][None, :]
    slopes = lax.dynamic_slice_in_dim(head_slopes(H), core * (H // 2), H // 2, 0)
    inputs_all = ordered(core, inputs, over_core(inputs), 0)

    full_first = first.result()
    full_qkv = full_first[:, : 3 * half]
    vec = full_first[:, 3 * half : 3 * half + VECTORS].T.astype(jnp.float32)
    query_bias, value_bias, out_bias, down_bias, attn_gain, attn_shift, ffn_gain, ffn_shift = [
        vec[i] for i in range(VECTORS)
    ]

    def my_part(vector):
        return lax.dynamic_slice_in_dim(vector, core * half, half, 0)

    projected = dot_nn(inputs_all, full_qkv)
    queries = (projected[:, :half] + my_part(query_bias)).astype(jnp.bfloat16)
    keys_values = jnp.concatenate(
        (projected[:, half : 2 * half], projected[:, 2 * half :] + my_part(value_bias)), axis=1
    ).astype(jnp.bfloat16)
    kv_low = from_previous_chip(keys_values[rows:])
    kv_high = from_next_chip(keys_values[:rows])
    kv_ext = jnp.concatenate([kv_low, keys_values, kv_high], axis=0)

    second.second()
    attended_0, lse_0 = attention_forward(0, queries, kv_ext, seg_row, tag_col, slopes)
    attended_1, lse_1 = attention_forward(1, queries, kv_ext, seg_row, tag_col, slopes)
    second.third()
    attended_own = jnp.concatenate([attended_0, attended_1], axis=0)
    attended_all = ordered(core, attended_own, over_core(attended_own), 1)
    attended = my_rows(attended_all)
    second.fourth()

    full_second = second.result()
    full_up_gate = full_second[:, : 2 * half_ff]
    out_half = full_second[:, 2 * half_ff :]
    full_out = ordered(core, out_half, over_core(out_half), 1)
    shards = down_halves.shape[0]
    mine_down = lax.dynamic_slice_in_dim(down_halves, core * (shards // 2), shards // 2, 0)
    send_down = lax.dynamic_slice_in_dim(down_halves, (1 - core) * (shards // 2), shards // 2, 0)
    full_down = ordered(core, mine_down[:, None], over_core(send_down)[:, None], 1).reshape(
        half_ff, width
    )

    attn_branch = dot_nn(attended, full_out) + out_bias
    first_norm, first_normed, first_inverse = norm_parts(
        inputs.astype(jnp.float32) + attn_branch, attn_gain, attn_shift
    )
    own_low = first_norm.astype(jnp.bfloat16)
    normed_low = ordered(core, own_low, over_core(own_low), 0)
    up_gate = dot_nn(normed_low, full_up_gate)
    up_value = up_gate[:, :half_ff]
    gate_value = up_gate[:, half_ff:]
    hidden = gelu_product(gate_value, up_value).astype(jnp.bfloat16)
    ffn_part = dot_nn(hidden, full_down)
    ffn_branch = (
        my_rows(ffn_part)
        + over_core(other_rows(ffn_part).astype(jnp.bfloat16)).astype(jnp.float32)
        + down_bias
    )
    output_value, second_normed, second_inverse = norm_parts(
        first_norm + ffn_branch, ffn_gain, ffn_shift
    )
    layer_out = output_value.astype(jnp.bfloat16)

    upstream = cotangent[0].astype(jnp.float32)
    grad_second, grad_ffn_gain, grad_ffn_shift = norm_back(
        upstream, second_normed, second_inverse, ffn_gain
    )
    grad_down_bias = jnp.sum(grad_second, axis=0)
    own_branch = grad_second.astype(jnp.bfloat16)
    grad_branch = ordered(core, own_branch, over_core(own_branch), 0)
    grad_down = dot_tn(hidden, grad_branch).astype(jnp.bfloat16)
    grad_down = grad_down.reshape(shards // 2, 2, shard_down // 2, width)
    keep = lax.dynamic_index_in_dim(grad_down, core, 1, keepdims=False)
    send = lax.dynamic_index_in_dim(grad_down, 1 - core, 1, keepdims=False)
    grad_down = ordered(core, keep, over_core(send), 0).reshape(shards * shard_down // 2, width)
    down_total = lax.psum_scatter(grad_down, "fsdp", scatter_dimension=0, tiled=True)

    hidden_grad = dot_nt(grad_branch, full_down)
    unused_value, pullback = jax.vjp(gelu_product, gate_value, up_value)
    grad_gate, grad_up = pullback(hidden_grad)
    grad_up_gate = jnp.concatenate((grad_up, grad_gate), axis=1).astype(jnp.bfloat16)
    reduce_ffn = row_reduce(dot_tn(normed_low, grad_up_gate).astype(jnp.bfloat16))
    reduce_ffn.first()
    normed_part = dot_nt(grad_up_gate, full_up_gate)
    grad_normed = (
        grad_second
        + my_rows(normed_part)
        + over_core(other_rows(normed_part).astype(jnp.bfloat16)).astype(jnp.float32)
    )
    grad_first, grad_attn_gain, grad_attn_shift = norm_back(
        grad_normed, first_normed, first_inverse, attn_gain
    )
    grad_out_bias = jnp.sum(grad_first, axis=0)
    own_attn_low = grad_first.astype(jnp.bfloat16)
    grad_attn_low = ordered(
        core,
        my_columns(own_attn_low, half),
        over_core(lax.dynamic_slice_in_dim(own_attn_low, (1 - core) * half, half, 1)),
        0,
    )
    grad_w_out = dot_tn(attended_all, grad_attn_low)
    own_grad = dot_nt(own_attn_low, full_out).astype(jnp.bfloat16)
    grad_attended = ordered(
        core,
        my_columns(own_grad, half),
        over_core(lax.dynamic_slice_in_dim(own_grad, (1 - core) * half, half, 1)),
        0,
    )
    reduce_ffn.second()

    dq_0, dk_0, dv_0 = attention_backward(
        0, queries, kv_ext, attended_0, grad_attended, lse_0, seg_row, tag_col, slopes
    )
    dq_1, dk_1, dv_1 = attention_backward(
        1, queries, kv_ext, attended_1, grad_attended, lse_1, seg_row, tag_col, slopes
    )
    reduce_ffn.third()
    reach_0 = jnp.concatenate([dk_0, dv_0], axis=1)
    reach_1 = jnp.concatenate([dk_1, dv_1], axis=1)
    low = reach_0[:HALF].astype(jnp.bfloat16)
    high = reach_1[2 * HALF :].astype(jnp.bfloat16)
    from_next = from_next_chip(low).astype(jnp.float32)
    from_previous = from_previous_chip(high).astype(jnp.float32)
    centre = jnp.concatenate(
        [
            reach_0[HALF : 2 * HALF] + reach_1[:HALF] + from_previous,
            reach_0[2 * HALF :] + reach_1[HALF : 2 * HALF] + from_next,
        ],
        axis=0,
    ).astype(jnp.bfloat16)
    grad_qkv = jnp.concatenate((jnp.concatenate([dq_0, dq_1], axis=0), centre), axis=1)
    reduce_ffn.fourth()
    grad_w_qkv = dot_tn(inputs_all, grad_qkv)

    def spread(vector):
        return lax.dynamic_update_slice_in_dim(jnp.zeros((width,), jnp.float32), vector, core * half, 0)

    grad_query_bias = spread(jnp.sum(grad_qkv[:, :half].astype(jnp.float32), axis=0))
    grad_value_bias = spread(jnp.sum(grad_qkv[:, 2 * half :].astype(jnp.float32), axis=0))
    grad_vectors = jnp.stack(
        (
            grad_query_bias, grad_value_bias, grad_out_bias, grad_down_bias,
            grad_attn_gain, grad_attn_shift, grad_ffn_gain, grad_ffn_shift,
        ),
        axis=0,
    )
    grad_vectors = (grad_vectors + over_core(grad_vectors)).T
    grad_vectors = jnp.pad(grad_vectors, ((0, 0), (0, 128 - VECTORS)))
    last = row_reduce(
        jnp.concatenate((grad_w_qkv, grad_w_out, grad_vectors), axis=1).astype(jnp.bfloat16)
    )
    last.first()
    last.second()
    last.third()
    last.fourth()
    input_part = dot_nt(grad_qkv, full_qkv)
    grad_inputs = (
        grad_first
        + my_rows(input_part)
        + over_core(other_rows(input_part).astype(jnp.bfloat16)).astype(jnp.float32)
    )

    down_0, down_1 = both_cores(down_total, core)
    ffn_0, ffn_1 = both_cores(reduce_ffn.result(), core)
    last_0, last_1 = both_cores(last.result(), core)

    def columns(start, count, source_0, source_1):
        return jnp.concatenate(
            (source_0[:, start : start + count], source_1[:, start : start + count]), axis=1
        )

    return (
        layer_out[None],
        grad_inputs[None],
        columns(0, half, last_0, last_1),
        columns(half, half, last_0, last_1),
        columns(2 * half, half, last_0, last_1),
        columns(3 * half, half, last_0, last_1),
        columns(0, half_ff, ffn_0, ffn_1),
        columns(half_ff, half_ff, ffn_0, ffn_1),
        jnp.concatenate((down_0, down_1), axis=0),
    ) + tuple(last_0[:, 4 * half + i] for i in range(VECTORS))


def solution(mesh):
    rows_spec = P("fsdp", "ctx", None)
    in_specs = (
        (rows_spec, P("fsdp", "ctx"), P("fsdp", "ctx"))
        + (P("fsdp", None),) * 7
        + (P("fsdp"),) * VECTORS
        + (rows_spec,)
    )
    out_specs = (rows_spec, rows_spec) + (P("fsdp", None),) * 7 + (P("fsdp"),) * VECTORS
    return jax.shard_map(
        on_device, mesh=mesh, in_specs=in_specs, out_specs=out_specs, check_vma=False
    )
```

```python
import math
import jax
import jax.numpy as jnp
from jax import lax
from jax.experimental import pallas as pl
from jax.experimental.pallas import tpu as pltpu
from jax.sharding import PartitionSpec as P

H = 12
HD = 64
FF = 3072
HALF = 512
EPSILON = 1e-06
VECTORS = 8
QB = 256
ROW_BLOCK = 1024
SPAN = QB + 2 * HALF
BIG = 1e30
VMEM_LIMIT = 56 * 1024 * 1024
SHORT = pl.CostEstimate(flops=1024, bytes_accessed=1024, transcendentals=0)

Z_SWAP = ((0, 1), (1, 0), (2, 3), (3, 2))
Z_MID = ((1, 2), (2, 1))
Z_OUT = ((1, 0), (2, 3))
Z_IN = ((0, 1), (3, 2))


def dot_nn(a, b):
    return lax.dot_general(a, b, (((1,), (0,)), ((), ())), preferred_element_type=jnp.float32)


def dot_nt(a, b):
    return lax.dot_general(a, b, (((1,), (1,)), ((), ())), preferred_element_type=jnp.float32)


def dot_tn(a, b):
    return lax.dot_general(a, b, (((0,), (0,)), ((), ())), preferred_element_type=jnp.float32)


def tie(*values):
    return lax.optimization_barrier(values)


def head_slopes(number):
    power_two = 2 ** int(math.floor(math.log2(number)))
    first_part = [2.0 ** (-8.0 * (position + 1) / power_two) for position in range(power_two)]
    extra_part = [
        2.0 ** (-8.0 * (2 * position + 1) / (2 * power_two))
        for position in range(number - power_two)
    ]
    return jnp.array(first_part + extra_part, dtype=jnp.float32)


def over_core(x):
    count = lax.axis_size("ctx")
    return lax.ppermute(x, "ctx", [(i, i ^ 1) for i in range(count)])


def from_previous_chip(x):
    count = lax.axis_size("ctx")
    return lax.ppermute(x, "ctx", [(i, i + 2) for i in range(count - 2)])


def from_next_chip(x):
    count = lax.axis_size("ctx")
    return lax.ppermute(x, "ctx", [(i + 2, i) for i in range(count - 2)])


def over_x(x):
    return lax.ppermute(x, "ctx", [(i, i ^ 2) for i in range(4)])


def over_y(x):
    return lax.ppermute(x, "fsdp", [(i, i ^ 1) for i in range(8)])


def over_z(x, moves):
    return lax.ppermute(
        x, "fsdp", [(2 * a + y, 2 * b + y) for a, b in moves for y in range(2)]
    )


def ordered(core, own, other, axis):
    return jnp.where(
        core == 0,
        jnp.concatenate([own, other], axis=axis),
        jnp.concatenate([other, own], axis=axis),
    )


def shard_number(k, dy):
    me = lax.axis_index("fsdp")
    return me ^ (2 * k + dy)


class Chain:
    live = ()

    def join(self, *values):
        held = tie(*[getattr(self, name) for name in self.live], *values)
        for name, value in zip(self.live, held):
            setattr(self, name, value)
        return held[len(self.live) :]


class Gather(Chain):
    def __init__(self, piece):
        self.own = piece

    def first_z(self):
        self.a = over_z(self.own, Z_SWAP)
        self.b = over_z(self.own, Z_MID)

    def first_y(self):
        self.y0 = over_y(self.own)
        self.live = ("y0", "a", "b")

    def first(self):
        self.first_z()
        self.first_y()

    def second(self, *values):
        self.a, self.b, *values = tie(self.a, self.b, *values)
        self.c = over_z(self.a, Z_MID)
        self.d = over_z(self.b, Z_OUT)
        self.ya = over_y(self.a)
        self.live = ("c", "d", "ya")
        return values

    def third(self, *values):
        self.z2, *values = tie(self.c + self.d, *values)
        self.e = over_z(self.c, Z_OUT)
        self.yz2 = over_y(self.z2)
        self.live = ("e", "yz2")
        return values

    def fourth(self, *values):
        self.z3, *values = tie(self.b + self.e, *values)
        self.yz3 = over_y(self.z3)
        self.live = ("yz3",)
        return values

    def pieces(self):
        return [self.own, self.a, self.z2, self.z3, self.y0, self.ya, self.yz2, self.yz3]

    def numbers(self):
        return jnp.stack([shard_number(k, dy) for dy in range(2) for k in range(4)])


class Reduce(Chain):
    def __init__(self, full):
        self.full = full
        self.rows = full.shape[1] // 8

    def part(self, k, dy):
        return lax.dynamic_slice_in_dim(
            self.full, shard_number(k, dy) * self.rows, self.rows, 1
        )

    def first(self, *values):
        send, *values = tie(self.part(3, 1), *values)
        self.y = over_y(send)
        self.live = ("y",)
        return values

    def second(self, *values):
        self.q3, send, *values = tie(self.part(3, 0) + self.y, self.part(2, 1), *values)
        self.y = over_y(send)
        self.e = over_z(self.q3, Z_IN)
        self.live = ("y", "e")
        return values

    def third(self, *values):
        q2 = self.part(2, 0) + self.y
        self.q2, on, send, *values = tie(q2, q2 + self.e, self.part(1, 1), *values)
        self.y = over_y(send)
        self.d = over_z(self.q2, Z_IN)
        self.c = over_z(on, Z_MID)
        self.live = ("y", "d", "c")
        return values

    def fourth(self, *values):
        on_b, on_a, send, *values = tie(
            self.q3 + self.d, self.part(1, 0) + self.y + self.c, self.part(0, 1), *values
        )
        self.y = over_y(send)
        self.b = over_z(on_b, Z_MID)
        self.a = over_z(on_a, Z_SWAP)
        self.live = ("y", "b", "a")
        return values

    def result(self):
        return self.part(0, 0) + self.y + self.a + self.b


class PlainGather(Chain):
    def __init__(self, piece):
        self.own = piece

    def first(self, *values):
        return values

    first_z = first_y = second = third = fourth = first

    def pieces(self):
        whole = lax.all_gather(self.own, "fsdp", axis=0, tiled=True)
        rows = whole.shape[0] // 8
        return [whole[i * rows : (i + 1) * rows] for i in range(8)]

    def numbers(self):
        return jnp.arange(8, dtype=jnp.int32)


class PlainReduce(Chain):
    def __init__(self, full):
        self.full = full

    def first(self, *values):
        return values

    second = third = fourth = first

    def result(self):
        return lax.psum_scatter(self.full, "fsdp", scatter_dimension=1, tiled=True)


def chips_sum(total):
    count = lax.axis_size("ctx")
    if count == 4:
        return total + over_x(total)
    core = lax.axis_index("ctx") % 2
    slots = jnp.stack(
        [jnp.where(core == i, total, jnp.zeros_like(total)) for i in range(2)]
    )
    return lax.dynamic_index_in_dim(lax.psum(slots, "ctx"), core, 0, keepdims=False)


def local_blocks(chip):
    return (
        (pl.multiple_of(chip * QB, QB), pl.multiple_of(chip * QB, QB), HALF + QB, chip * HALF),
        (pl.multiple_of((1 - chip) * QB, QB), 0, 2 * HALF, QB + chip * QB),
    )


def reach_blocks(chip):
    return ((0, 0, SPAN, HALF), (QB, QB, SPAN, HALF))


def rows_at(start, count):
    return pl.ds(start, count)


def fill_distance(dist, block, seg_ref, tag_ref):
    q_at, k_at, span, shift = block
    key_pos = lax.broadcasted_iota(jnp.int32, (span, QB), 0)
    row_pos = lax.broadcasted_iota(jnp.int32, (span, QB), 1) + shift
    gap = jnp.abs(key_pos - row_pos)
    same = tag_ref[rows_at(k_at, span), :] == seg_ref[:, rows_at(q_at, QB)]
    kept = ((gap <= HALF) & same) | (gap == 0)
    dist[...] = jnp.where(kept, gap.astype(jnp.float32), BIG)


def attn_fwd_kernel(
    plan, chip, slopes, q_ref, k_ref, v_ref, seg_ref, tag_ref, out_ref, lse_ref, *dists
):
    pair = pl.program_id(0)
    blocks = plan(chip[0])

    @pl.when(pair == 0)
    def _():
        for dist, block in zip(dists, blocks):
            fill_distance(dist, block, seg_ref, tag_ref)

    lane = lax.broadcasted_iota(jnp.int32, (QB, 2 * HD), 1)
    for dist, (q_at, k_at, span, shift) in zip(dists, blocks):
        q = q_ref[rows_at(q_at, QB), :]
        k = k_ref[rows_at(k_at, span), :]
        v_t = v_ref[rows_at(k_at, span), :].T
        parts = []
        for a in range(2):
            mine = (lane >= HD) if a else (lane < HD)
            q_a = jnp.where(mine, q, jnp.zeros_like(q)) * jnp.asarray(1.0 / math.sqrt(HD), q.dtype)
            s = dot_nt(k, q_a) - slopes[2 * pair + a] * dist[...]
            top = jnp.max(s, axis=0, keepdims=True)
            p = jnp.exp(s - top)
            total = jnp.sum(p, axis=0, keepdims=True)
            o_t = dot_nn(v_t[a * HD : (a + 1) * HD, :], p.astype(jnp.bfloat16))
            parts.append(o_t * (1.0 / total))
            lse_ref[0, a : a + 1, rows_at(q_at, QB)] = top + jnp.log(total)
        out_ref[rows_at(q_at, QB), :] = jnp.concatenate(parts, axis=0).T.astype(jnp.bfloat16)


def distances(plan):
    return [pltpu.VMEM((block[2], QB), jnp.float32) for block in plan(0)]


def attention_forward(plan, chip, queries, keys_values, seg_row, tag_col, slopes):
    rows, width = queries.shape
    ext = keys_values.shape[0]
    pairs = width // (2 * HD)

    def body(*refs):
        attn_fwd_kernel(plan, *refs)

    return pl.pallas_call(
        body,
        grid=(pairs,),
        in_specs=[
            pl.BlockSpec(memory_space=pltpu.SMEM),
            pl.BlockSpec(memory_space=pltpu.SMEM),
            pl.BlockSpec((rows, 2 * HD), lambda h: (0, h)),
            pl.BlockSpec((ext, 2 * HD), lambda h: (0, h)),
            pl.BlockSpec((ext, 2 * HD), lambda h: (0, pairs + h)),
            pl.BlockSpec((1, rows), lambda h: (0, 0)),
            pl.BlockSpec((ext, 1), lambda h: (0, 0)),
        ],
        out_specs=[
            pl.BlockSpec((rows, 2 * HD), lambda h: (0, h)),
            pl.BlockSpec((1, 8, rows), lambda h: (h, 0, 0)),
        ],
        out_shape=[
            jax.ShapeDtypeStruct((rows, width), jnp.bfloat16),
            jax.ShapeDtypeStruct((pairs, 8, rows), jnp.float32),
        ],
        scratch_shapes=distances(plan),
        compiler_params=pltpu.CompilerParams(vmem_limit_bytes=VMEM_LIMIT),
        cost_estimate=SHORT,
    )(chip, slopes, queries, keys_values, keys_values, seg_row, tag_col)


def attn_bwd_kernel(
    plan, low, chip, slopes, q_ref, k_ref, v_ref, o_ref, do_ref, do_else_ref, lse_ref, seg_ref, tag_ref, start_ref,
    dq_ref, dkv_ref, beyond_ref, *dists,
):
    step = pl.program_id(0)
    pair = step + low
    blocks = plan(chip[0])

    @pl.when(step == 0)
    def _():
        for dist, block in zip(dists, blocks):
            fill_distance(dist, block, seg_ref, tag_ref)

    lane = lax.broadcasted_iota(jnp.int32, (QB, 2 * HD), 1)
    lane_one = lax.broadcasted_iota(jnp.int32, (8, 2 * HD), 1)
    scale = 1.0 / math.sqrt(HD)
    if start_ref is None:
        dkv_ref[...] = jnp.zeros_like(dkv_ref)
    else:
        count = dkv_ref.shape[1]
        dkv_ref[...] = start_ref[:, rows_at(pl.multiple_of(chip[0] * HALF, HALF), count), :]
    for dist, (q_at, k_at, span, shift) in zip(dists, blocks):
        q = q_ref[rows_at(q_at, QB), :] * jnp.asarray(scale, jnp.bfloat16)
        do = jnp.where(chip[1] == 1, do_ref[rows_at(q_at, QB), :], do_else_ref[rows_at(q_at, QB), :])
        k = k_ref[rows_at(k_at, span), :]
        v = v_ref[rows_at(k_at, span), :]
        k_t = k.T
        mixed = do.astype(jnp.float32) * o_ref[rows_at(q_at, QB), :].astype(jnp.float32)
        parts = []
        ps = []
        dss = []
        qs = []
        dos = []
        for a in range(2):
            mine = (lane >= HD) if a else (lane < HD)
            mine_one = (lane_one >= HD) if a else (lane_one < HD)
            q_a = jnp.where(mine, q, jnp.zeros_like(q))
            do_a = jnp.where(mine, do, jnp.zeros_like(do))
            delta = lax.dot_general(
                mine_one.astype(jnp.float32), mixed, (((1,), (1,)), ((), ())),
                preferred_element_type=jnp.float32, precision=lax.Precision.HIGHEST,
            )[0:1]
            s = dot_nt(k, q_a) - slopes[2 * pair + a] * dist[...]
            p = jnp.exp(s - lse_ref[0, a : a + 1, rows_at(q_at, QB)])
            dp = dot_nt(v, do_a)
            ds = (p * (dp - delta)).astype(jnp.bfloat16)
            parts.append(dot_nn(k_t[a * HD : (a + 1) * HD, :], ds) * scale)
            ps.append(p.astype(jnp.bfloat16))
            dss.append(ds)
            qs.append(q_a)
            dos.append(do_a)
        dq_ref[rows_at(q_at, QB), :] = jnp.concatenate(parts, axis=0).T.astype(jnp.bfloat16)
        dkv_ref[0, rows_at(k_at, span), :] += dot_nn(
            jnp.concatenate(dss, axis=1), jnp.concatenate(qs, axis=0)
        )
        dkv_ref[1, rows_at(k_at, span), :] += dot_nn(
            jnp.concatenate(ps, axis=1), jnp.concatenate(dos, axis=0)
        )
    if beyond_ref is not None:
        other = pl.multiple_of((1 - chip[0]) * 2 * HALF, HALF)
        beyond_ref[...] = dkv_ref[:, rows_at(other, HALF), :].astype(jnp.bfloat16)


def attention_backward(
    plan, chip, queries, keys_values, attended, grad_if, grad_else, lse, seg_row, tag_col, slopes, start,
    low=0, count=None, into=(),
):
    rows, width = queries.shape
    ext = keys_values.shape[0]
    pairs = width // (2 * HD)
    count = pairs if count is None else count
    inner = pl.BlockSpec((rows, 2 * HD), lambda h: (0, low + h))
    starts = () if start is None else (start,)

    def body(*refs):
        if start is None:
            refs = refs[:11] + (None,) + refs[11 + len(into) :]
        else:
            refs = refs[:14] + (None,) + refs[14:]
        attn_bwd_kernel(plan, low, *refs)

    return pl.pallas_call(
        body,
        grid=(count,),
        in_specs=[
            pl.BlockSpec(memory_space=pltpu.SMEM),
            pl.BlockSpec(memory_space=pltpu.SMEM),
            inner,
            pl.BlockSpec((ext, 2 * HD), lambda h: (0, low + h)),
            pl.BlockSpec((ext, 2 * HD), lambda h: (0, pairs + low + h)),
            inner,
            inner,
            inner,
            pl.BlockSpec((1, 8, rows), lambda h: (low + h, 0, 0)),
            pl.BlockSpec((1, rows), lambda h: (0, 0)),
            pl.BlockSpec((ext, 1), lambda h: (0, 0)),
        ]
        + [pl.BlockSpec((2, s.shape[1], 2 * HD), lambda h: (0, 0, low + h)) for s in starts]
        + [pl.BlockSpec(memory_space=pl.ANY)] * len(into),
        out_specs=[inner, pl.BlockSpec((2, ext, 2 * HD), lambda h: (0, 0, low + h))]
        + [pl.BlockSpec((2, HALF, 2 * HD), lambda h: (0, 0, low + h))] * (1 - len(starts)),
        out_shape=[
            jax.ShapeDtypeStruct((rows, width), jnp.bfloat16),
            jax.ShapeDtypeStruct((2, ext, width), jnp.float32),
        ]
        + [jax.ShapeDtypeStruct((2, HALF, width), jnp.bfloat16)] * (1 - len(starts)),
        input_output_aliases={11 + i: i for i in range(len(into))},
        scratch_shapes=distances(plan),
        compiler_params=pltpu.CompilerParams(vmem_limit_bytes=VMEM_LIMIT),
        cost_estimate=SHORT,
    )(
        chip, slopes, queries, keys_values, keys_values, attended, grad_if, grad_else, lse,
        seg_row, tag_col, *starts, *into,
    )


def norm_parts(values, gain_vec, offset):
    centred = values - jnp.mean(values, axis=-1, keepdims=True)
    variance = jnp.mean(centred * centred, axis=-1, keepdims=True)
    inverse = lax.rsqrt(variance + EPSILON)
    normed = centred * inverse
    return (normed * gain_vec + offset, normed, inverse)


def project_kernel(
    place_numbers, spot, x_ref, *refs
):
    pieces = refs[:8]
    vec_ref, w_ref, out_ref, local_ref, reach_ref, kv_ref, send_ref, weight = refs[8:]
    core, chip = spot[0], spot[1]
    fill_weight(place_numbers, pieces, weight)
    half = out_ref.shape[1]
    rows = local_ref.shape[0]
    w_ref[...] = weight[:, : 3 * half]
    out_ref[...] = weight[:, 3 * half : 4 * half]
    vec = weight[:, 4 * half :].astype(jnp.float32).T[:VECTORS, :]
    vec_ref[...] = vec
    projected = dot_nn(x_ref[...], weight[:, : 3 * half])

    def bias(i):
        return jnp.where(core == 0, vec[i : i + 1, :half], vec[i : i + 1, half:])

    queries = (projected[:, :half] + bias(0)).astype(jnp.bfloat16)
    first = chip == 0
    local_ref[...] = jnp.where(first, queries[:rows], queries[rows:])
    reach_ref[...] = jnp.where(first, queries[rows:], queries[:rows])
    keys = projected[:, half : 2 * half].astype(jnp.bfloat16)
    values = (projected[:, 2 * half :] + bias(1)).astype(jnp.bfloat16)
    kv_ref[:, :half] = keys
    kv_ref[:, half:] = values
    send_ref[:, :half] = jnp.where(first, keys[rows:], keys[:rows])
    send_ref[:, half:] = jnp.where(first, values[rows:], values[:rows])


def project(numbers, spot, x, pieces):
    all_rows, width = x.shape
    half = width // 2
    rows = all_rows // 2
    whole = pl.BlockSpec(memory_space=pltpu.VMEM)
    smem = pl.BlockSpec(memory_space=pltpu.SMEM)
    low = jnp.bfloat16
    return pl.pallas_call(
        project_kernel,
        in_specs=[smem, smem] + [whole] * 9,
        out_specs=[whole] * 7,
        out_shape=[
            jax.ShapeDtypeStruct((VECTORS, width), jnp.float32),
            jax.ShapeDtypeStruct((width, 3 * half), low),
            jax.ShapeDtypeStruct((width, half), low),
            jax.ShapeDtypeStruct((rows, half), low),
            jax.ShapeDtypeStruct((rows, half), low),
            jax.ShapeDtypeStruct((all_rows, width), low),
            jax.ShapeDtypeStruct((rows, width), low),
        ],
        scratch_shapes=[pltpu.VMEM((width, pieces[0].shape[1]), low)],
        compiler_params=pltpu.CompilerParams(vmem_limit_bytes=VMEM_LIMIT),
        cost_estimate=SHORT,
    )(numbers, spot, x, *pieces)


def first_norm_kernel(
    core, vec_ref, attended_ref, mine_ref, other_ref, x_ref,
    norm_ref, normed_ref, inverse_ref, low_ref, w_ref,
):
    half = mine_ref.shape[1]
    rows = norm_ref.shape[0]
    first = core[0] == 0

    @pl.when(pl.program_id(0) == 0)
    def _():
        w_ref[:, :half] = jnp.where(first, mine_ref[...], other_ref[...])
        w_ref[:, half:] = jnp.where(first, other_ref[...], mine_ref[...])

    at = pl.multiple_of(core[0] * rows * pl.num_programs(0) + pl.program_id(0) * rows, rows)
    branch = dot_nn(attended_ref[pl.ds(at, rows), :], w_ref[...]) + vec_ref[2:3, :]
    norm, normed, inverse = norm_parts(
        x_ref[...].astype(jnp.float32) + branch, vec_ref[4:5, :], vec_ref[5:6, :]
    )
    norm_ref[...] = norm
    normed_ref[...] = normed
    inverse_ref[...] = inverse
    low_ref[...] = norm.astype(jnp.bfloat16)


def first_norm_of(core, vec, attended, mine, other, x):
    rows, width = x.shape
    steps = 2
    block = pl.BlockSpec((rows // steps, width), lambda i: (i, 0))

    def all_of(a):
        return pl.BlockSpec(a.shape, lambda i: (0, 0))

    return pl.pallas_call(
        first_norm_kernel,
        grid=(steps,),
        in_specs=[pl.BlockSpec(memory_space=pltpu.SMEM)]
        + [all_of(a) for a in (vec, attended, mine, other)]
        + [block],
        out_specs=[
            block, block, pl.BlockSpec((rows // steps, 1), lambda i: (i, 0)), block,
            pl.BlockSpec((width, width), lambda i: (0, 0)),
        ],
        out_shape=[
            jax.ShapeDtypeStruct((rows, width), jnp.float32),
            jax.ShapeDtypeStruct((rows, width), jnp.float32),
            jax.ShapeDtypeStruct((rows, 1), jnp.float32),
            jax.ShapeDtypeStruct((rows, width), jnp.bfloat16),
            jax.ShapeDtypeStruct((width, width), jnp.bfloat16),
        ],
        compiler_params=pltpu.CompilerParams(vmem_limit_bytes=VMEM_LIMIT),
        cost_estimate=SHORT,
    )(core, vec, attended, mine, other, x)


def norm_back(upstream, normed, inverse, gain_vec):
    scaled = upstream * gain_vec
    row_inner = (
        scaled
        - jnp.mean(scaled, axis=-1, keepdims=True)
        - normed * jnp.mean(scaled * normed, axis=-1, keepdims=True)
    )
    return row_inner * inverse


def last_grads_kernel(
    spot, x_ref, local_ref, reach_ref, dkv_ref, beyond_ref, out_w_ref, attn_ref, ffn_ref,
    last_ref, grad_ref,
):
    core, chip = spot[0], spot[1]
    first = chip == 0
    rows, half = local_ref.shape
    grad_ref[:rows, :half] = jnp.where(first, local_ref[...], reach_ref[...])
    grad_ref[rows:, :half] = jnp.where(first, reach_ref[...], local_ref[...])
    for t in range(2):
        got = beyond_ref[t].astype(jnp.float32)
        part = slice((t + 1) * half, (t + 2) * half)
        top = dkv_ref[t, :rows, :] + jnp.where(first, 0.0, got)
        low = dkv_ref[t, rows:, :] + jnp.where(first, got, 0.0)
        grad_ref[:rows, part] = top.astype(jnp.bfloat16)
        grad_ref[rows:, part] = low.astype(jnp.bfloat16)
    grads = grad_ref[...]
    last_ref[0, :, : 3 * half] = dot_tn(x_ref[...], grads).astype(jnp.bfloat16)
    last_ref[0, :, 3 * half : 4 * half] = out_w_ref[...]
    sums = [
        jnp.sum(grads[:, i * half : (i + 1) * half].astype(jnp.float32), axis=0, keepdims=True)
        for i in (0, 2)
    ]
    nothing = jnp.zeros_like(sums[0])
    vectors = [
        jnp.where(
            core == 0, jnp.concatenate([s, nothing], axis=1), jnp.concatenate([nothing, s], axis=1)
        )
        for s in sums
    ]
    vectors += [attn_ref[2:3, :], ffn_ref[2:3, :], attn_ref[0:2, :], ffn_ref[0:2, :]]
    vectors.append(jnp.zeros((128 - VECTORS, 2 * half), jnp.float32))
    last_ref[0, :, 4 * half :] = jnp.concatenate(vectors, axis=0).T.astype(jnp.bfloat16)


def last_grads(spot, x, dq_local, dq_reach, dkv, beyond, grad_w_out, attn_sums, ffn_sums):
    all_rows, width = x.shape
    half = width // 2
    whole = pl.BlockSpec(memory_space=pltpu.VMEM)
    return pl.pallas_call(
        last_grads_kernel,
        in_specs=[pl.BlockSpec(memory_space=pltpu.SMEM)] + [whole] * 8,
        out_specs=[whole] * 2,
        out_shape=[
            jax.ShapeDtypeStruct((1, width, 4 * half + 128), jnp.bfloat16),
            jax.ShapeDtypeStruct((all_rows, 3 * half), jnp.bfloat16),
        ],
        compiler_params=pltpu.CompilerParams(vmem_limit_bytes=VMEM_LIMIT),
        cost_estimate=SHORT,
    )(spot, x, dq_local, dq_reach, dkv, beyond, grad_w_out, attn_sums, ffn_sums)


def finish_kernel(core, mine_ref, other_ref, *outs):
    first = core[0] == 0
    half = outs[0].shape[1] // 2
    for i, out in enumerate(outs[:4]):
        part = slice(i * half, (i + 1) * half)
        mine, other = mine_ref[:, part].astype(jnp.float32), other_ref[:, part].astype(jnp.float32)
        out[:, :half] = jnp.where(first, mine, other)
        out[:, half:] = jnp.where(first, other, mine)
    mine, other = mine_ref[:, 4 * half :], other_ref[:, 4 * half :]
    outs[4][...] = (mine.astype(jnp.float32) + other.astype(jnp.float32)).T[:VECTORS, :]


def finish(core, mine, other):
    rows, columns = mine.shape
    width = (columns - 128) // 2
    whole = pl.BlockSpec(memory_space=pltpu.VMEM)
    results = pl.pallas_call(
        finish_kernel,
        in_specs=[pl.BlockSpec(memory_space=pltpu.SMEM)] + [whole] * 2,
        out_specs=[whole] * 5,
        out_shape=[jax.ShapeDtypeStruct((rows, width), jnp.float32)] * 4
        + [jax.ShapeDtypeStruct((VECTORS, rows), jnp.float32)],
        cost_estimate=SHORT,
    )(core, mine, other)
    return results[:4], results[4]


def add_sums(step, sums_ref, *columns):
    rows = [jnp.sum(value, axis=0, keepdims=True) for value in columns]
    rows.append(jnp.zeros((8 - len(rows), sums_ref.shape[1]), jnp.float32))
    add_up(step, sums_ref, jnp.concatenate(rows, axis=0))


def second_norm_kernel(
    vec_ref, norm_ref, part_ref, sent_ref, cot_ref, out_ref, grad_ref, low_ref, sums_ref
):
    step = pl.program_id(0)
    bias, gain, shift = vec_ref[3:4, :], vec_ref[6:7, :], vec_ref[7:8, :]
    value = norm_ref[...] + part_ref[...] + sent_ref[...].astype(jnp.float32) + bias
    result, normed, inverse = norm_parts(value, gain, shift)
    out_ref[...] = result.astype(jnp.bfloat16)
    upstream = cot_ref[...].astype(jnp.float32)
    grad = norm_back(upstream, normed, inverse, gain)
    grad_ref[...] = grad
    low_ref[...] = grad.astype(jnp.bfloat16)
    add_sums(step, sums_ref, upstream * normed, upstream, grad)


def second_norm(vec, first_norm, part, sent, cotangent):
    rows, width = part.shape
    block = pl.BlockSpec((rows // 4, width), lambda i: (i, 0))
    eight = pl.BlockSpec((8, width), lambda i: (0, 0))
    return pl.pallas_call(
        second_norm_kernel,
        grid=(4,),
        in_specs=[eight] + [block] * 4,
        out_specs=[block] * 3 + [eight],
        out_shape=[
            jax.ShapeDtypeStruct((rows, width), jnp.bfloat16),
            jax.ShapeDtypeStruct((rows, width), jnp.float32),
            jax.ShapeDtypeStruct((rows, width), jnp.bfloat16),
            jax.ShapeDtypeStruct((8, width), jnp.float32),
        ],
        compiler_params=pltpu.CompilerParams(vmem_limit_bytes=VMEM_LIMIT),
        cost_estimate=SHORT,
    )(vec, first_norm, part, sent, cotangent)


def first_norm_back_kernel(
    core, vec_ref, w_ref, up_ref, part_ref, sent_ref, normed_ref, inverse_ref,
    grad_ref, low_mine, low_theirs, back_mine, back_theirs, sums_ref,
):
    step = pl.program_id(0)
    half = low_mine.shape[1]
    upstream = up_ref[...] + part_ref[...] + sent_ref[...].astype(jnp.float32)
    normed = normed_ref[...]
    grad = norm_back(upstream, normed, inverse_ref[...], vec_ref[4:5, :])
    grad_ref[...] = grad
    low = grad.astype(jnp.bfloat16)
    back = dot_nt(low, w_ref[...]).astype(jnp.bfloat16)
    first = core[0] == 0
    for value, mine, theirs in ((low, low_mine, low_theirs), (back, back_mine, back_theirs)):
        left, right = value[:, :half], value[:, half:]
        mine[...] = jnp.where(first, left, right)
        theirs[...] = jnp.where(first, right, left)
    add_sums(step, sums_ref, upstream * normed, upstream, grad)


def first_norm_back(core, vec, w_out, grad_second, part, sent, normed, inverse):
    rows, width = part.shape
    steps = 2
    block = pl.BlockSpec((rows // steps, width), lambda i: (i, 0))
    halves = pl.BlockSpec((rows // steps, width // 2), lambda i: (i, 0))
    eight = pl.BlockSpec((8, width), lambda i: (0, 0))
    return pl.pallas_call(
        first_norm_back_kernel,
        grid=(steps,),
        in_specs=[
            pl.BlockSpec(memory_space=pltpu.SMEM),
            eight,
            pl.BlockSpec((width, width), lambda i: (0, 0)),
        ]
        + [block] * 4
        + [pl.BlockSpec((rows // steps, 1), lambda i: (i, 0))],
        out_specs=[block] + [halves] * 4 + [eight],
        out_shape=[jax.ShapeDtypeStruct((rows, width), jnp.float32)]
        + [jax.ShapeDtypeStruct((rows, width // 2), jnp.bfloat16)] * 4
        + [jax.ShapeDtypeStruct((8, width), jnp.float32)],
        compiler_params=pltpu.CompilerParams(vmem_limit_bytes=VMEM_LIMIT),
        cost_estimate=SHORT,
    )(core, vec, w_out, grad_second, part, sent, normed, inverse)


def lay_out_kernel(core, mine_ref, other_ref, up_ref, gate_ref, down_ref):
    first = core[0] == 0
    count, shard_rows, width = mine_ref.shape
    groups = count // 3
    shards = width // shard_rows

    def both(i):
        mine, other = mine_ref[i].astype(jnp.float32), other_ref[i].astype(jnp.float32)
        return jnp.where(first, mine, other), jnp.where(first, other, mine)

    for g in range(groups):
        for c, value in enumerate(both(2 * groups + g)):
            at = (c * groups + g) * shard_rows
            down_ref[at : at + shard_rows, :] = value
        for t, out in ((0, up_ref), (1, gate_ref)):
            for c, value in enumerate(both(2 * g + t)):
                for s in range(shards):
                    at = ((s * 2 + c) * groups + g) * shard_rows
                    out[:, at : at + shard_rows] = value[:, s * shard_rows : (s + 1) * shard_rows]


def lay_out(core, mine, other):
    count, shard_rows, width = mine.shape
    columns = count // 3 * 2 * width
    whole = pl.BlockSpec(memory_space=pltpu.VMEM)
    return pl.pallas_call(
        lay_out_kernel,
        in_specs=[pl.BlockSpec(memory_space=pltpu.SMEM)] + [whole] * 2,
        out_specs=[whole] * 3,
        out_shape=[
            jax.ShapeDtypeStruct((shard_rows, columns), jnp.float32),
            jax.ShapeDtypeStruct((shard_rows, columns), jnp.float32),
            jax.ShapeDtypeStruct((count // 3 * 2 * shard_rows, width), jnp.float32),
        ],
        compiler_params=pltpu.CompilerParams(vmem_limit_bytes=VMEM_LIMIT),
        cost_estimate=SHORT,
    )(core, mine, other)


def phi_parts(v):
    cdf = 0.5 * (1.0 + lax.erf(v * math.sqrt(0.5)))
    density = jnp.exp(-0.5 * v * v) * (1.0 / math.sqrt(2.0 * math.pi))
    return cdf, cdf + v * density


def fill_weight(numbers, pieces, weight):
    rows = pieces[0].shape[0]
    for i, piece in enumerate(pieces):
        weight[pl.ds(pl.multiple_of(numbers[i] * rows, rows), rows), :] = piece[...]


def add_up(step, total, out):
    @pl.when(step == 0)
    def _():
        total[...] = out

    @pl.when(step > 0)
    def _():
        total[...] += out


def ffn_fwd_kernel(numbers, own_ref, other_ref, *refs):
    ups, gates, downs = refs[:8], refs[8:16], refs[16:24]
    hid_ref, act_ref, slope_ref, part_ref, send_ref = refs[24:29]
    x_all, up_w, gate_w, down_w, total = refs[29:]
    step = pl.program_id(0)
    rows = own_ref.shape[0]

    @pl.when(step == 0)
    def _():
        x_all[:rows, :] = own_ref[...]
        x_all[rows:, :] = other_ref[...]

    fill_weight(numbers, ups, up_w)
    fill_weight(numbers, gates, gate_w)
    fill_weight(numbers, downs, down_w)
    outs = []
    columns = up_w.shape[1]
    piece = columns // 2
    for i in range(2):
        part = slice(i * piece, (i + 1) * piece)
        x = x_all[...]
        up = dot_nn(x, up_w[:, part])
        gate = dot_nn(x, gate_w[:, part])
        cdf, derivative = phi_parts(gate)
        act = gate * cdf
        hidden = (act * up).astype(jnp.bfloat16)
        hid_ref[:, part] = hidden
        act_ref[:, part] = act.astype(jnp.bfloat16)
        slope_ref[:, part] = (derivative * up).astype(jnp.bfloat16)
        outs.append(dot_nn(hidden, down_w[part, :]))
    add_up(step, total, outs[0] + outs[1])

    @pl.when(step == pl.num_programs(0) - 1)
    def _():
        part_ref[...] = total[:rows, :]
        send_ref[...] = total[rows:, :].astype(jnp.bfloat16)


def piece_specs(rows, width, columns):
    steps = columns // width
    return [
        pl.BlockSpec((rows, width), lambda f, t=t: (0, t * steps + f))
        for t in range(3)
        for i in range(8)
    ]


def ffn_forward(own, other, pieces, numbers, columns):
    rows, width = own.shape
    steps = columns // width
    wide = pl.BlockSpec((2 * rows, width), lambda f: (0, f))
    whole = pl.BlockSpec((rows, width), lambda f: (0, 0))
    return pl.pallas_call(
        ffn_fwd_kernel,
        grid=(steps,),
        in_specs=[pl.BlockSpec(memory_space=pltpu.SMEM), whole, whole]
        + piece_specs(pieces[0].shape[0], width, columns),
        out_specs=[wide, wide, wide, whole, whole],
        out_shape=[jax.ShapeDtypeStruct((2 * rows, columns), jnp.bfloat16)] * 3
        + [
            jax.ShapeDtypeStruct((rows, width), jnp.float32),
            jax.ShapeDtypeStruct((rows, width), jnp.bfloat16),
        ],
        scratch_shapes=[
            pltpu.VMEM((2 * rows, width), jnp.bfloat16),
            pltpu.VMEM((width, width), jnp.bfloat16),
            pltpu.VMEM((width, width), jnp.bfloat16),
            pltpu.VMEM((width, width), jnp.bfloat16),
            pltpu.VMEM((2 * rows, width), jnp.float32),
        ],
        compiler_params=pltpu.CompilerParams(vmem_limit_bytes=VMEM_LIMIT),
        cost_estimate=SHORT,
    )(numbers, own, other, *(pieces * 3))


def down_grad_kernel(group, branch_ref, branch_other_ref, hid_ref, grad_ref):
    rows = branch_ref.shape[0]
    total = dot_tn(hid_ref[:rows, :], branch_ref[...])
    grad_ref[...] = (total + dot_tn(hid_ref[rows:, :], branch_other_ref[...])).astype(jnp.bfloat16)


def down_grad(group, branch, branch_other, hidden):
    rows, width = branch.shape
    whole = pl.BlockSpec((rows, width), lambda i, group: (0, 0))
    return pl.pallas_call(
        down_grad_kernel,
        grid_spec=pltpu.PrefetchScalarGridSpec(
            num_scalar_prefetch=1,
            grid=(1,),
            in_specs=[
                whole, whole, pl.BlockSpec((2 * rows, width), lambda i, group: (0, group[0])),
            ],
            out_specs=pl.BlockSpec((width, width), lambda i, group: (0, 0)),
        ),
        out_shape=jax.ShapeDtypeStruct((width, width), jnp.bfloat16),
        compiler_params=pltpu.CompilerParams(vmem_limit_bytes=VMEM_LIMIT),
        cost_estimate=SHORT,
    )(group, branch, branch_other, hidden)


def add_last_kernel(all_ref, keep_ref, got_ref, out_ref):
    out_ref[0] = keep_ref[...] + got_ref[...]


def add_last(grads, keep, got):
    last = grads.shape[0] - 1
    whole = pl.BlockSpec(memory_space=pltpu.VMEM)
    return pl.pallas_call(
        add_last_kernel,
        grid=(1,),
        in_specs=[pl.BlockSpec(memory_space=pl.ANY), whole, whole],
        out_specs=pl.BlockSpec((1,) + grads.shape[1:], lambda i: (last, 0, 0)),
        out_shape=jax.ShapeDtypeStruct(grads.shape, grads.dtype),
        input_output_aliases={0: 0},
        compiler_params=pltpu.CompilerParams(vmem_limit_bytes=VMEM_LIMIT),
        cost_estimate=SHORT,
    )(grads, keep, got)


def ffn_bwd_kernel(numbers, own_ref, other_ref, branch_ref, branch_other_ref, act_ref, slope_ref, *refs):
    ups, gates, downs = refs[:8], refs[8:16], refs[16:24]
    grad_ref, part_ref, send_ref = refs[24:27]
    x_all, branch_all, up_w, gate_w, down_w, total = refs[27:]
    step = pl.program_id(0)
    rows = own_ref.shape[0]

    @pl.when(step == 0)
    def _():
        x_all[:rows, :] = own_ref[...]
        x_all[rows:, :] = other_ref[...]
        branch_all[:rows, :] = branch_ref[...]
        branch_all[rows:, :] = branch_other_ref[...]

    fill_weight(numbers, ups, up_w)
    fill_weight(numbers, gates, gate_w)
    fill_weight(numbers, downs, down_w)
    d_hidden = dot_nt(branch_all[...], down_w[...])
    d_up = (d_hidden * act_ref[...].astype(jnp.float32)).astype(jnp.bfloat16)
    d_gate = (d_hidden * slope_ref[...].astype(jnp.float32)).astype(jnp.bfloat16)
    add_up(step, total, dot_nt(d_up, up_w[...]) + dot_nt(d_gate, gate_w[...]))
    x = x_all[...]
    grad_ref[0] = dot_tn(x, d_up).astype(jnp.bfloat16)
    grad_ref[1] = dot_tn(x, d_gate).astype(jnp.bfloat16)

    @pl.when(step == pl.num_programs(0) - 1)
    def _():
        part_ref[...] = total[:rows, :]
        send_ref[...] = total[rows:, :].astype(jnp.bfloat16)


def ffn_backward(own, other, branch, branch_other, act, slope, pieces, numbers, columns):
    rows, width = own.shape
    steps = columns // width
    wide = pl.BlockSpec((2 * rows, width), lambda f: (0, f))
    whole = pl.BlockSpec((rows, width), lambda f: (0, 0))
    return pl.pallas_call(
        ffn_bwd_kernel,
        grid=(steps,),
        in_specs=[pl.BlockSpec(memory_space=pltpu.SMEM)]
        + [whole] * 4
        + [wide] * 2
        + piece_specs(pieces[0].shape[0], width, columns),
        out_specs=[
            pl.BlockSpec((2, width, width), lambda f: (f, 0, 0)),
            whole,
            whole,
        ],
        out_shape=[
            jax.ShapeDtypeStruct((2 * steps + 1, width, width), jnp.bfloat16),
            jax.ShapeDtypeStruct((rows, width), jnp.float32),
            jax.ShapeDtypeStruct((rows, width), jnp.bfloat16),
        ],
        scratch_shapes=[
            pltpu.VMEM((2 * rows, width), jnp.bfloat16),
            pltpu.VMEM((2 * rows, width), jnp.bfloat16),
            pltpu.VMEM((width, width), jnp.bfloat16),
            pltpu.VMEM((width, width), jnp.bfloat16),
            pltpu.VMEM((width, width), jnp.bfloat16),
            pltpu.VMEM((2 * rows, width), jnp.float32),
        ],
        compiler_params=pltpu.CompilerParams(vmem_limit_bytes=VMEM_LIMIT),
        cost_estimate=SHORT,
    )(numbers, own, other, branch, branch_other, act, slope, *(pieces * 3))


def pack_kernel(core, up_ref, gate_ref, down_ref, out_ref):
    first = core[0] == 0
    shard_rows = up_ref.shape[0]
    width = down_ref.shape[1]
    shards = width // shard_rows
    groups = down_ref.shape[0] // shard_rows // 2
    at = 0
    for ref in (up_ref, gate_ref):
        for g in range(groups):
            for s in range(shards):
                left = (s * 2 * groups + g) * shard_rows
                right = left + groups * shard_rows
                out_ref[:, at : at + shard_rows] = jnp.where(
                    first, ref[:, left : left + shard_rows], ref[:, right : right + shard_rows]
                )
                at += shard_rows
    for g in range(groups):
        top = g * shard_rows
        low = top + groups * shard_rows
        out_ref[:, at : at + width] = jnp.where(
            first, down_ref[top : top + shard_rows, :], down_ref[low : low + shard_rows, :]
        )
        at += width


def pack(core, up, gate, down):
    shard_rows = up.shape[0]
    width = down.shape[1]
    whole = pl.BlockSpec(memory_space=pltpu.VMEM)
    return pl.pallas_call(
        pack_kernel,
        in_specs=[pl.BlockSpec(memory_space=pltpu.SMEM)] + [whole] * 3,
        out_specs=whole,
        out_shape=jax.ShapeDtypeStruct(
            (shard_rows, up.shape[1] + down.shape[0] // shard_rows // 2 * width), jnp.bfloat16
        ),
        compiler_params=pltpu.CompilerParams(vmem_limit_bytes=VMEM_LIMIT),
        cost_estimate=SHORT,
    )(core, up, gate, down)


def pack_first_kernel(core, *refs):
    first = core[0] == 0
    half = refs[0].shape[1] // 2
    out_ref = refs[-1]
    for i, ref in enumerate(refs[:4]):
        out_ref[:, i * half : (i + 1) * half] = jnp.where(first, ref[:, :half], ref[:, half:])
    out_ref[:, 4 * half :] = refs[4][...]


def pack_first(core, matrices, vectors):
    rows, width = matrices[0].shape
    whole = pl.BlockSpec(memory_space=pltpu.VMEM)
    return pl.pallas_call(
        pack_first_kernel,
        in_specs=[pl.BlockSpec(memory_space=pltpu.SMEM)] + [whole] * 5,
        out_specs=whole,
        out_shape=jax.ShapeDtypeStruct((rows, 2 * width + vectors.shape[1]), jnp.bfloat16),
        cost_estimate=SHORT,
    )(core, *matrices, vectors)


def on_device(
    tokens, segments, padding,
    w_query, w_key, w_value, w_out, w_up, w_gate, w_down,
    bias_query, bias_value, bias_out, bias_down, gain_attn, shift_attn, gain_ffn, shift_ffn,
    cotangent,
):
    tuned = lax.axis_size("ctx") == 4 and lax.axis_size("fsdp") == 8
    row_gather, row_reduce = (Gather, Reduce) if tuned else (PlainGather, PlainReduce)
    core = lax.axis_index("ctx") % 2
    chip = lax.axis_index("ctx") // 2
    chip_ref = chip[None].astype(jnp.int32)
    core_ref = core[None].astype(jnp.int32)
    inputs = tokens[0]
    rows, width = inputs.shape
    half = width // 2
    half_ff = FF // 2

    def cut(value, which, count, axis):
        return lax.dynamic_slice_in_dim(value, which * count, count, axis)

    def share(mine, theirs, axis):
        return ordered(core, mine, over_core(theirs), axis)

    vectors = jnp.stack(
        (bias_query, bias_value, bias_out, bias_down, gain_attn, shift_attn, gain_ffn, shift_ffn), axis=1
    )
    vectors = jnp.pad(vectors, ((0, 0), (0, 128 - VECTORS)))
    first = row_gather(pack_first(core_ref, (w_query, w_key, w_value, w_out), vectors))
    second = row_gather(pack(core_ref, w_up, w_gate, w_down))
    first.first()

    own_numbers = jnp.stack((segments[0], jnp.where(padding[0] == 1, -1, segments[0])))
    numbers = share(own_numbers, own_numbers, 1)
    slopes = cut(head_slopes(H), core, H // 2, 0)
    (numbers,) = first.join(numbers)
    tags = numbers[1]
    seg_row = numbers[0][None, :]
    if tuned:
        tags_send = jnp.where(chip == 0, tags[rows:], tags[:rows]) + 2
        first.second()
        beyond = over_x(tags_send)
        beyond, second.own = first.join(beyond, second.own)
        beyond = beyond - 2
        tags_reach = ordered(chip, tags, beyond, 0)[:, None]
        tags_local = tags[:, None]
        seg_local = cut(seg_row, chip, rows, 1)
        seg_reach = cut(seg_row, 1 - chip, rows, 1)
    else:
        tag_low = from_previous_chip(tags[rows:] + 2) - 2
        tag_high = from_next_chip(tags[:rows] + 2) - 2
        tags_wide = jnp.concatenate([tag_low, tags, tag_high])[:, None]
    first.third()
    inputs_all = share(inputs, inputs, 0)
    (inputs_all,) = first.join(inputs_all)
    (second.own,) = first.fourth(second.own)
    second.first_z()
    (second.own,) = first.join(second.own)
    second.first_y()

    spot = jnp.stack((core, chip if tuned else jnp.zeros_like(chip))).astype(jnp.int32)
    vec, full_qkv, out_half, queries_local, queries_reach, keys_values, beyond = project(
        first.numbers(), spot, inputs_all, first.pieces()
    )
    out_other = over_core(out_half)
    if tuned:
        queries_local, queries_reach, keys_values, beyond = second.join(
            queries_local, queries_reach, keys_values, beyond
        )
        beyond = over_x(beyond)
        second.second()
        attended_local, lse_local = attention_forward(
            local_blocks, chip_ref, queries_local, keys_values, seg_local, tags_local, slopes
        )
        attended_local, lse_local, beyond = second.join(attended_local, lse_local, beyond)
        keys_values, beyond = second.third(keys_values, beyond)
        kv_reach = ordered(chip, keys_values, beyond, 0)
        attended_reach, lse_reach = attention_forward(
            reach_blocks, chip_ref, queries_reach, kv_reach, seg_reach, tags_reach, slopes
        )
        attended_own = ordered(chip, attended_local, attended_reach, 0)
        (attended_own,) = second.join(attended_own)
        (attended_own,) = second.fourth(attended_own)
    else:
        queries = jnp.concatenate([queries_local, queries_reach], axis=0)
        kv_low = from_previous_chip(keys_values[rows:])
        kv_high = from_next_chip(keys_values[:rows])
        kv_wide = jnp.concatenate([kv_low, keys_values, kv_high], axis=0)
        spans = [(i * rows, i * rows + rows + 2 * HALF) for i in range(2)]
        forward_parts = [
            attention_forward(
                reach_blocks, chip_ref, queries[i * rows : (i + 1) * rows], kv_wide[low:high],
                seg_row[:, i * rows : (i + 1) * rows], tags_wide[low:high], slopes,
            )
            for i, (low, high) in enumerate(spans)
        ]
        attended_own = jnp.concatenate([part[0] for part in forward_parts], axis=0)
    attended_all = share(attended_own, attended_own, 1)
    first_norm, first_normed, first_inverse, own_low, full_out = first_norm_of(
        core_ref, vec, attended_all, out_half, out_other, inputs
    )
    other_low = over_core(own_low)
    if tuned:
        own_low, other_low = second.join(own_low, other_low)
    pieces = second.pieces()
    places = second.numbers()
    hidden, act, slope, ffn_part, ffn_send = ffn_forward(own_low, other_low, pieces, places, half_ff)
    layer_out, grad_second, own_branch, ffn_sums = second_norm(
        vec, first_norm, ffn_part, over_core(ffn_send), cotangent[0]
    )
    branch_other = over_core(own_branch)
    group = chip_ref if tuned else jnp.zeros_like(chip_ref)
    down_send = down_grad(1 - group, own_branch, branch_other, hidden)
    if tuned:
        down_send, own_branch, branch_other = tie(down_send, own_branch, branch_other)
        down_got = over_x(down_send)
    down_keep = down_grad(group, own_branch, branch_other, hidden)
    down_keep, own_branch, branch_other = tie(down_keep, own_branch, branch_other)
    grad_weights, normed_part, normed_send = ffn_backward(
        own_low, other_low, own_branch, branch_other, act, slope, pieces, places, half_ff
    )
    if tuned:
        grad_weights, normed_send, down_got = tie(grad_weights, normed_send, down_got)
        grad_weights = add_last(grad_weights, down_keep, down_got)
    else:
        grad_weights = jnp.concatenate([grad_weights[:-1], down_keep[None], down_send[None]])
    reduce_ffn = row_reduce(grad_weights)
    (normed_send,) = reduce_ffn.first(normed_send)
    grad_first, low_mine, low_theirs, back_mine, back_theirs, attn_sums = first_norm_back(
        core_ref, vec, full_out, grad_second, normed_part, over_core(normed_send),
        first_normed, first_inverse,
    )
    back_other = over_core(back_theirs)
    low_other = over_core(low_theirs)

    if tuned:
        back_ref = jnp.stack((chip, core == chip)).astype(jnp.int32)
        def reach_part(low, count, into):
            return attention_backward(
                reach_blocks, back_ref, queries_reach, kv_reach, attended_reach, back_other, back_mine,
                lse_reach, seg_reach, tags_reach, slopes, None, low, count, into,
            )

        low_all = ordered(core, low_mine, low_other, 0)
        pairs = half // (2 * HD)
        reached = reduce_ffn.join(*reach_part(0, pairs - 1, ()))
        reached = reduce_ffn.second(*reached)
        dq_reach, dkv_reach, beyond = reach_part(pairs - 1, 1, tuple(reached))
        dq_reach, dkv_reach, beyond, low_all = tie(dq_reach, dkv_reach, beyond, low_all)
        beyond = over_x(beyond)
        grad_w_out = dot_tn(attended_all, low_all)
        dq_reach, dkv_reach, grad_w_out = reduce_ffn.join(dq_reach, dkv_reach, grad_w_out)
        dq_reach, dkv_reach, grad_w_out = reduce_ffn.third(dq_reach, dkv_reach, grad_w_out)
        dq_local, dkv_local = attention_backward(
            local_blocks, back_ref, queries_local, keys_values, attended_local,
            back_mine, back_other, lse_local, seg_local, tags_local, slopes, dkv_reach,
        )
        dq_local, dkv_local, beyond = reduce_ffn.join(dq_local, dkv_local, beyond)
        reduce_ffn.fourth()
    else:
        grad_attended = ordered(core, back_mine, back_other, 0)
        back_ref = jnp.ones((2,), jnp.int32)
        backward_parts = [
            attention_backward(
                reach_blocks, back_ref, queries[i * rows : (i + 1) * rows], kv_wide[low:high],
                forward_parts[i][0], grad_attended[i * rows : (i + 1) * rows],
                grad_attended[i * rows : (i + 1) * rows], forward_parts[i][1],
                seg_row[:, i * rows : (i + 1) * rows], tags_wide[low:high], slopes, None,
            )
            for i, (low, high) in enumerate(spans)
        ]
        dq_local, dq_reach = [part[0] for part in backward_parts]
        reach_0, reach_1 = [part[1] for part in backward_parts]
        from_next = from_next_chip(reach_0[:, :HALF].astype(jnp.bfloat16)).astype(jnp.float32)
        from_previous = from_previous_chip(reach_1[:, rows + HALF :].astype(jnp.bfloat16)).astype(jnp.float32)
        centre = jnp.pad(reach_0[:, HALF:], ((0, 0), (0, 2 * rows - reach_0.shape[1] + HALF), (0, 0)))
        centre = centre + jnp.pad(
            reach_1[:, : rows + HALF], ((0, 0), (2 * rows - rows - HALF, 0), (0, 0))
        )
        centre = centre.at[:, 2 * rows - HALF :].add(from_next)
        dkv_local = centre.at[:, :HALF].add(from_previous)
        beyond = jnp.zeros_like(from_next, dtype=jnp.bfloat16)
        grad_w_out = dot_tn(attended_all, ordered(core, low_mine, low_other, 0))
    grad_last, grad_qkv = last_grads(
        spot, inputs_all, dq_local, dq_reach, dkv_local, beyond, grad_w_out.astype(jnp.bfloat16),
        attn_sums, ffn_sums,
    )
    last = row_reduce(grad_last)
    last.first()
    reduce_ffn.join()
    last.join()
    last.second()
    input_part = dot_nt(grad_qkv, full_qkv)
    grad_inputs = (
        grad_first
        + cut(input_part, core, rows, 0)
        + over_core(cut(input_part, 1 - core, rows, 0).astype(jnp.bfloat16)).astype(jnp.float32)
    )
    ffn_mine = reduce_ffn.result()
    if tuned:
        got = over_x(ffn_mine)
        ffn_mine = jnp.concatenate(
            [ffn_mine[:-1] + got[:-1], ordered(chip, ffn_mine[-1:], got[-1:], 0)], axis=0
        )
    else:
        ffn_mine = chips_sum(ffn_mine)
    (grad_inputs,) = last.join(grad_inputs)
    last.third()
    last.join()
    last.fourth()
    grad_up, grad_gate, grad_down = lay_out(core_ref, ffn_mine, over_core(ffn_mine))
    if tuned:
        grad_up, grad_gate, grad_down = last.join(grad_up, grad_gate, grad_down)
    last_mine = chips_sum(last.result())[0]
    last_rows, vector_rows = finish(core_ref, last_mine, over_core(last_mine))

    return (
        layer_out[None],
        grad_inputs[None],
        *last_rows,
        grad_up,
        grad_gate,
        grad_down,
    ) + tuple(vector_rows[i] for i in range(VECTORS))


def solution(mesh):
    rows_spec = P("fsdp", "ctx", None)
    in_specs = (
        (rows_spec, P("fsdp", "ctx"), P("fsdp", "ctx"))
        + (P("fsdp", None),) * 7
        + (P("fsdp"),) * VECTORS
        + (rows_spec,)
    )
    out_specs = (rows_spec, rows_spec) + (P("fsdp", None),) * 7 + (P("fsdp"),) * VECTORS
    return jax.shard_map(
        on_device, mesh=mesh, in_specs=in_specs, out_specs=out_specs, check_vma=False
    )
```

```python
import math
import jax
import jax.numpy as jnp
from jax import lax
from jax.experimental import pallas as pl
from jax.experimental.pallas import tpu as pltpu
from jax.sharding import PartitionSpec as P

H = 12
HD = 64
FF = 3072
HALF = 512
EPSILON = 1e-06
VECTORS = 8
QB = 256
ROW_BLOCK = 1024
SPAN = QB + 2 * HALF
BIG = 1e30
VMEM_LIMIT = 56 * 1024 * 1024
SHORT = pl.CostEstimate(flops=1024, bytes_accessed=1024, transcendentals=0)

Z_SWAP = ((0, 1), (1, 0), (2, 3), (3, 2))
Z_MID = ((1, 2), (2, 1))
Z_OUT = ((1, 0), (2, 3))
Z_IN = ((0, 1), (3, 2))


def dot_nn(a, b):
    return lax.dot_general(a, b, (((1,), (0,)), ((), ())), preferred_element_type=jnp.float32)


def dot_nt(a, b):
    return lax.dot_general(a, b, (((1,), (1,)), ((), ())), preferred_element_type=jnp.float32)


def dot_tn(a, b):
    return lax.dot_general(a, b, (((0,), (0,)), ((), ())), preferred_element_type=jnp.float32)


def tie(*values):
    return lax.optimization_barrier(values)


def head_slopes(number):
    power_two = 2 ** int(math.floor(math.log2(number)))
    first_part = [2.0 ** (-8.0 * (position + 1) / power_two) for position in range(power_two)]
    extra_part = [
        2.0 ** (-8.0 * (2 * position + 1) / (2 * power_two))
        for position in range(number - power_two)
    ]
    return jnp.array(first_part + extra_part, dtype=jnp.float32)


def over_core(x):
    count = lax.axis_size("ctx")
    return lax.ppermute(x, "ctx", [(i, i ^ 1) for i in range(count)])


def from_previous_chip(x):
    count = lax.axis_size("ctx")
    return lax.ppermute(x, "ctx", [(i, i + 2) for i in range(count - 2)])


def from_next_chip(x):
    count = lax.axis_size("ctx")
    return lax.ppermute(x, "ctx", [(i + 2, i) for i in range(count - 2)])


def over_x(x):
    return lax.ppermute(x, "ctx", [(i, i ^ 2) for i in range(4)])


def over_y(x):
    return lax.ppermute(x, "fsdp", [(i, i ^ 1) for i in range(8)])


def over_z(x, moves):
    return lax.ppermute(
        x, "fsdp", [(2 * a + y, 2 * b + y) for a, b in moves for y in range(2)]
    )


def ordered(core, own, other, axis):
    return jnp.where(
        core == 0,
        jnp.concatenate([own, other], axis=axis),
        jnp.concatenate([other, own], axis=axis),
    )


def shard_number(k, dy):
    me = lax.axis_index("fsdp")
    return me ^ (2 * k + dy)


class Chain:
    live = ()

    def join(self, *values):
        held = tie(*[getattr(self, name) for name in self.live], *values)
        for name, value in zip(self.live, held):
            setattr(self, name, value)
        return held[len(self.live) :]


class Gather(Chain):
    def __init__(self, piece):
        self.own = piece

    def first_z(self):
        self.a = over_z(self.own, Z_SWAP)
        self.b = over_z(self.own, Z_MID)

    def first_y(self):
        self.y0 = over_y(self.own)
        self.live = ("y0", "a", "b")

    def first(self):
        self.first_z()
        self.first_y()

    def second(self, *values):
        self.a, self.b, *values = tie(self.a, self.b, *values)
        self.c = over_z(self.a, Z_MID)
        self.d = over_z(self.b, Z_OUT)
        self.ya = over_y(self.a)
        self.live = ("c", "d", "ya")
        return values

    def third(self, *values):
        self.z2, *values = tie(self.c + self.d, *values)
        self.e = over_z(self.c, Z_OUT)
        self.yz2 = over_y(self.z2)
        self.live = ("e", "yz2")
        return values

    def fourth(self, *values):
        self.z3, *values = tie(self.b + self.e, *values)
        self.yz3 = over_y(self.z3)
        self.live = ("yz3",)
        return values

    def pieces(self):
        return [self.own, self.a, self.z2, self.z3, self.y0, self.ya, self.yz2, self.yz3]

    def numbers(self):
        return jnp.stack([shard_number(k, dy) for dy in range(2) for k in range(4)])


class Reduce(Chain):
    def __init__(self, full):
        self.full = full
        self.rows = full.shape[1] // 8

    def part(self, k, dy):
        return lax.dynamic_slice_in_dim(
            self.full, shard_number(k, dy) * self.rows, self.rows, 1
        )

    def first(self, *values):
        send, *values = tie(self.part(3, 1), *values)
        self.y = over_y(send)
        self.live = ("y",)
        return values

    def second(self, *values):
        self.q3, send, *values = tie(self.part(3, 0) + self.y, self.part(2, 1), *values)
        self.y = over_y(send)
        self.e = over_z(self.q3, Z_IN)
        self.live = ("y", "e")
        return values

    def third(self, *values):
        q2 = self.part(2, 0) + self.y
        self.q2, on, send, *values = tie(q2, q2 + self.e, self.part(1, 1), *values)
        self.y = over_y(send)
        self.d = over_z(self.q2, Z_IN)
        self.c = over_z(on, Z_MID)
        self.live = ("y", "d", "c")
        return values

    def fourth(self, *values):
        on_b, on_a, send, *values = tie(
            self.q3 + self.d, self.part(1, 0) + self.y + self.c, self.part(0, 1), *values
        )
        self.y = over_y(send)
        self.b = over_z(on_b, Z_MID)
        self.a = over_z(on_a, Z_SWAP)
        self.live = ("y", "b", "a")
        return values

    def result(self):
        return self.part(0, 0) + self.y + self.a + self.b


class PlainGather(Chain):
    def __init__(self, piece):
        self.own = piece

    def first(self, *values):
        return values

    first_z = first_y = second = third = fourth = first

    def pieces(self):
        whole = lax.all_gather(self.own, "fsdp", axis=0, tiled=True)
        rows = whole.shape[0] // 8
        return [whole[i * rows : (i + 1) * rows] for i in range(8)]

    def numbers(self):
        return jnp.arange(8, dtype=jnp.int32)


class PlainReduce(Chain):
    def __init__(self, full):
        self.full = full

    def first(self, *values):
        return values

    second = third = fourth = first

    def result(self):
        return lax.psum_scatter(self.full, "fsdp", scatter_dimension=1, tiled=True)


def chips_sum(total):
    count = lax.axis_size("ctx")
    if count == 4:
        return total + over_x(total)
    core = lax.axis_index("ctx") % 2
    slots = jnp.stack(
        [jnp.where(core == i, total, jnp.zeros_like(total)) for i in range(2)]
    )
    return lax.dynamic_index_in_dim(lax.psum(slots, "ctx"), core, 0, keepdims=False)


def local_blocks(chip):
    return (
        (pl.multiple_of(chip * QB, QB), pl.multiple_of(chip * QB, QB), HALF + QB, chip * HALF),
        (pl.multiple_of((1 - chip) * QB, QB), 0, 2 * HALF, QB + chip * QB),
    )


def reach_blocks(chip):
    return ((0, 0, SPAN, HALF), (QB, QB, SPAN, HALF))


def rows_at(start, count):
    return pl.ds(start, count)


def both_chips(chip, local_ref, beyond_ref, all_ref):
    own = local_ref.shape[0]
    count = beyond_ref.shape[0]
    all_ref[rows_at(pl.multiple_of(chip * count, count), own), :] = local_ref[...]
    all_ref[rows_at(pl.multiple_of((1 - chip) * own, count), count), :] = beyond_ref[...]


def fill_distance(dist, block, seg_ref, tag_ref):
    q_at, k_at, span, shift = block
    key_pos = lax.broadcasted_iota(jnp.int32, (span, QB), 0)
    row_pos = lax.broadcasted_iota(jnp.int32, (span, QB), 1) + shift
    gap = jnp.abs(key_pos - row_pos)
    same = tag_ref[rows_at(k_at, span), :] == seg_ref[:, rows_at(q_at, QB)]
    kept = ((gap <= HALF) & same) | (gap == 0)
    dist[...] = jnp.where(kept, gap.astype(jnp.float32), BIG)


def attn_fwd_kernel(
    plan, chip, slopes, q_ref, k_ref, v_ref, seg_ref, tag_ref, k_else, v_else, out_ref, lse_ref, *dists
):
    pair = pl.program_id(0)
    blocks = plan(chip[0])
    if k_else is not None:
        *dists, k_all, v_all = dists
        both_chips(chip[0], k_ref, k_else, k_all)
        both_chips(chip[0], v_ref, v_else, v_all)
        k_ref, v_ref = k_all, v_all

    @pl.when(pair == 0)
    def _():
        for dist, block in zip(dists, blocks):
            fill_distance(dist, block, seg_ref, tag_ref)

    lane = lax.broadcasted_iota(jnp.int32, (QB, 2 * HD), 1)
    for dist, (q_at, k_at, span, shift) in zip(dists, blocks):
        q = q_ref[rows_at(q_at, QB), :]
        k = k_ref[rows_at(k_at, span), :]
        v_t = v_ref[rows_at(k_at, span), :].T
        parts = []
        for a in range(2):
            mine = (lane >= HD) if a else (lane < HD)
            q_a = jnp.where(mine, q, jnp.zeros_like(q)) * jnp.asarray(1.0 / math.sqrt(HD), q.dtype)
            s = dot_nt(k, q_a) - slopes[2 * pair + a] * dist[...]
            top = jnp.max(s, axis=0, keepdims=True)
            p = jnp.exp(s - top)
            total = jnp.sum(p, axis=0, keepdims=True)
            o_t = dot_nn(v_t[a * HD : (a + 1) * HD, :], p.astype(jnp.bfloat16))
            parts.append(o_t * (1.0 / total))
            lse_ref[0, a : a + 1, rows_at(q_at, QB)] = top + jnp.log(total)
        out_ref[rows_at(q_at, QB), :] = jnp.concatenate(parts, axis=0).T.astype(jnp.bfloat16)


def distances(plan):
    return [pltpu.VMEM((block[2], QB), jnp.float32) for block in plan(0)]


def attention_forward(plan, chip, queries, keys_values, seg_row, tag_col, slopes, beyond=None):
    rows, width = queries.shape
    ext = tag_col.shape[0]
    own = keys_values.shape[0]
    more = () if beyond is None else (beyond, beyond)
    pairs = width // (2 * HD)

    def body(*refs):
        if beyond is None:
            refs = refs[:7] + (None, None) + refs[7:]
        attn_fwd_kernel(plan, *refs)

    return pl.pallas_call(
        body,
        grid=(pairs,),
        in_specs=[
            pl.BlockSpec(memory_space=pltpu.SMEM),
            pl.BlockSpec(memory_space=pltpu.SMEM),
            pl.BlockSpec((rows, 2 * HD), lambda h: (0, h)),
            pl.BlockSpec((own, 2 * HD), lambda h: (0, h)),
            pl.BlockSpec((own, 2 * HD), lambda h: (0, pairs + h)),
            pl.BlockSpec((1, rows), lambda h: (0, 0)),
            pl.BlockSpec((ext, 1), lambda h: (0, 0)),
        ]
        + [
            pl.BlockSpec((ext - own, 2 * HD), lambda h, t=t: (0, t * pairs + h))
            for t in range(len(more))
        ],
        out_specs=[
            pl.BlockSpec((rows, 2 * HD), lambda h: (0, h)),
            pl.BlockSpec((1, 8, rows), lambda h: (h, 0, 0)),
        ],
        out_shape=[
            jax.ShapeDtypeStruct((rows, width), jnp.bfloat16),
            jax.ShapeDtypeStruct((pairs, 8, rows), jnp.float32),
        ],
        scratch_shapes=distances(plan) + [pltpu.VMEM((ext, 2 * HD), jnp.bfloat16)] * len(more),
        compiler_params=pltpu.CompilerParams(vmem_limit_bytes=VMEM_LIMIT),
        cost_estimate=SHORT,
    )(chip, slopes, queries, keys_values, keys_values, seg_row, tag_col, *more)


def attn_bwd_kernel(
    plan, low, chip, slopes, q_ref, k_ref, v_ref, o_ref, do_ref, do_else_ref, lse_ref, seg_ref, tag_ref, start_ref,
    k_else, v_else, dq_ref, dkv_ref, beyond_ref, *dists,
):
    step = pl.program_id(0)
    pair = step + low
    blocks = plan(chip[0])
    if k_else is not None:
        *dists, k_all, v_all = dists
        both_chips(chip[0], k_ref, k_else, k_all)
        both_chips(chip[0], v_ref, v_else, v_all)
        k_ref, v_ref = k_all, v_all

    @pl.when(step == 0)
    def _():
        for dist, block in zip(dists, blocks):
            fill_distance(dist, block, seg_ref, tag_ref)

    lane = lax.broadcasted_iota(jnp.int32, (QB, 2 * HD), 1)
    lane_one = lax.broadcasted_iota(jnp.int32, (8, 2 * HD), 1)
    scale = 1.0 / math.sqrt(HD)
    if start_ref is None:
        dkv_ref[...] = jnp.zeros_like(dkv_ref)
    else:
        count = dkv_ref.shape[1]
        dkv_ref[...] = start_ref[:, rows_at(pl.multiple_of(chip[0] * HALF, HALF), count), :]
    for dist, (q_at, k_at, span, shift) in zip(dists, blocks):
        q = q_ref[rows_at(q_at, QB), :] * jnp.asarray(scale, jnp.bfloat16)
        do = jnp.where(chip[1] == 1, do_ref[rows_at(q_at, QB), :], do_else_ref[rows_at(q_at, QB), :])
        k = k_ref[rows_at(k_at, span), :]
        v = v_ref[rows_at(k_at, span), :]
        k_t = k.T
        mixed = do.astype(jnp.float32) * o_ref[rows_at(q_at, QB), :].astype(jnp.float32)
        parts = []
        ps = []
        dss = []
        qs = []
        dos = []
        for a in range(2):
            mine = (lane >= HD) if a else (lane < HD)
            mine_one = (lane_one >= HD) if a else (lane_one < HD)
            q_a = jnp.where(mine, q, jnp.zeros_like(q))
            do_a = jnp.where(mine, do, jnp.zeros_like(do))
            delta = lax.dot_general(
                mine_one.astype(jnp.float32), mixed, (((1,), (1,)), ((), ())),
                preferred_element_type=jnp.float32, precision=lax.Precision.HIGHEST,
            )[0:1]
            s = dot_nt(k, q_a) - slopes[2 * pair + a] * dist[...]
            p = jnp.exp(s - lse_ref[0, a : a + 1, rows_at(q_at, QB)])
            dp = dot_nt(v, do_a)
            ds = (p * (dp - delta)).astype(jnp.bfloat16)
            parts.append(dot_nn(k_t[a * HD : (a + 1) * HD, :], ds) * scale)
            ps.append(p.astype(jnp.bfloat16))
            dss.append(ds)
            qs.append(q_a)
            dos.append(do_a)
        dq_ref[rows_at(q_at, QB), :] = jnp.concatenate(parts, axis=0).T.astype(jnp.bfloat16)
        dkv_ref[0, rows_at(k_at, span), :] += dot_nn(
            jnp.concatenate(dss, axis=1), jnp.concatenate(qs, axis=0)
        )
        dkv_ref[1, rows_at(k_at, span), :] += dot_nn(
            jnp.concatenate(ps, axis=1), jnp.concatenate(dos, axis=0)
        )
    if beyond_ref is not None:
        other = pl.multiple_of((1 - chip[0]) * 2 * HALF, HALF)
        beyond_ref[...] = dkv_ref[:, rows_at(other, HALF), :].astype(jnp.bfloat16)


def attention_backward(
    plan, chip, queries, keys_values, attended, grad_if, grad_else, lse, seg_row, tag_col, slopes, start,
    low=0, count=None, into=(), beyond=None,
):
    rows, width = queries.shape
    ext = tag_col.shape[0]
    own = keys_values.shape[0]
    more = () if beyond is None else (beyond, beyond)
    pairs = width // (2 * HD)
    count = pairs if count is None else count
    inner = pl.BlockSpec((rows, 2 * HD), lambda h: (0, low + h))
    starts = () if start is None else (start,)

    def body(*refs):
        refs = list(refs)
        fixed, refs = refs[:11], refs[11:]
        begin = refs.pop(0) if starts else None
        others = [refs.pop(0) for _ in more] or [None, None]
        refs = refs[len(into) :]
        outs, refs = refs[: 3 - len(starts)], refs[3 - len(starts) :]
        outs += [None] * len(starts)
        attn_bwd_kernel(plan, low, *fixed, begin, *others, *outs, *refs)

    return pl.pallas_call(
        body,
        grid=(count,),
        in_specs=[
            pl.BlockSpec(memory_space=pltpu.SMEM),
            pl.BlockSpec(memory_space=pltpu.SMEM),
            inner,
            pl.BlockSpec((own, 2 * HD), lambda h: (0, low + h)),
            pl.BlockSpec((own, 2 * HD), lambda h: (0, pairs + low + h)),
            inner,
            inner,
            inner,
            pl.BlockSpec((1, 8, rows), lambda h: (low + h, 0, 0)),
            pl.BlockSpec((1, rows), lambda h: (0, 0)),
            pl.BlockSpec((ext, 1), lambda h: (0, 0)),
        ]
        + [pl.BlockSpec((2, s.shape[1], 2 * HD), lambda h: (0, 0, low + h)) for s in starts]
        + [
            pl.BlockSpec((ext - own, 2 * HD), lambda h, t=t: (0, t * pairs + low + h))
            for t in range(len(more))
        ]
        + [pl.BlockSpec(memory_space=pl.ANY)] * len(into),
        out_specs=[inner, pl.BlockSpec((2, ext, 2 * HD), lambda h: (0, 0, low + h))]
        + [pl.BlockSpec((2, HALF, 2 * HD), lambda h: (0, 0, low + h))] * (1 - len(starts)),
        out_shape=[
            jax.ShapeDtypeStruct((rows, width), jnp.bfloat16),
            jax.ShapeDtypeStruct((2, ext, width), jnp.float32),
        ]
        + [jax.ShapeDtypeStruct((2, HALF, width), jnp.bfloat16)] * (1 - len(starts)),
        input_output_aliases={11 + len(starts) + len(more) + i: i for i in range(len(into))},
        scratch_shapes=distances(plan) + [pltpu.VMEM((ext, 2 * HD), jnp.bfloat16)] * len(more),
        compiler_params=pltpu.CompilerParams(vmem_limit_bytes=VMEM_LIMIT),
        cost_estimate=SHORT,
    )(
        chip, slopes, queries, keys_values, keys_values, attended, grad_if, grad_else, lse,
        seg_row, tag_col, *starts, *more, *into,
    )


def norm_parts(values, gain_vec, offset):
    centred = values - jnp.mean(values, axis=-1, keepdims=True)
    variance = jnp.mean(centred * centred, axis=-1, keepdims=True)
    inverse = lax.rsqrt(variance + EPSILON)
    normed = centred * inverse
    return (normed * gain_vec + offset, normed, inverse)


def project_kernel(
    place_numbers, spot, x_ref, *refs
):
    pieces = refs[:8]
    vec_ref, w_ref, out_ref, local_ref, reach_ref, kv_ref, send_ref, weight = refs[8:]
    core, chip = spot[0], spot[1]
    fill_weight(place_numbers, pieces, weight)
    half = out_ref.shape[1]
    rows = local_ref.shape[0]
    w_ref[...] = weight[:, : 3 * half]
    out_ref[...] = weight[:, 3 * half : 4 * half]
    vec = weight[:, 4 * half :].astype(jnp.float32).T[:VECTORS, :]
    vec_ref[...] = vec
    projected = dot_nn(x_ref[...], weight[:, : 3 * half])

    def bias(i):
        return jnp.where(core == 0, vec[i : i + 1, :half], vec[i : i + 1, half:])

    queries = (projected[:, :half] + bias(0)).astype(jnp.bfloat16)
    first = chip == 0
    local_ref[...] = jnp.where(first, queries[:rows], queries[rows:])
    reach_ref[...] = jnp.where(first, queries[rows:], queries[:rows])
    keys = projected[:, half : 2 * half].astype(jnp.bfloat16)
    values = (projected[:, 2 * half :] + bias(1)).astype(jnp.bfloat16)
    kv_ref[:, :half] = keys
    kv_ref[:, half:] = values
    send_ref[:, :half] = jnp.where(first, keys[rows:], keys[:rows])
    send_ref[:, half:] = jnp.where(first, values[rows:], values[:rows])


def project(numbers, spot, x, pieces):
    all_rows, width = x.shape
    half = width // 2
    rows = all_rows // 2
    whole = pl.BlockSpec(memory_space=pltpu.VMEM)
    smem = pl.BlockSpec(memory_space=pltpu.SMEM)
    low = jnp.bfloat16
    return pl.pallas_call(
        project_kernel,
        in_specs=[smem, smem] + [whole] * 9,
        out_specs=[whole] * 7,
        out_shape=[
            jax.ShapeDtypeStruct((VECTORS, width), jnp.float32),
            jax.ShapeDtypeStruct((width, 3 * half), low),
            jax.ShapeDtypeStruct((width, half), low),
            jax.ShapeDtypeStruct((rows, half), low),
            jax.ShapeDtypeStruct((rows, half), low),
            jax.ShapeDtypeStruct((all_rows, width), low),
            jax.ShapeDtypeStruct((rows, width), low),
        ],
        scratch_shapes=[pltpu.VMEM((width, pieces[0].shape[1]), low)],
        compiler_params=pltpu.CompilerParams(vmem_limit_bytes=VMEM_LIMIT),
        cost_estimate=SHORT,
    )(numbers, spot, x, *pieces)


def first_norm_kernel(
    core, vec_ref, attended_ref, mine_ref, other_ref, x_ref,
    norm_ref, normed_ref, inverse_ref, low_ref, w_ref,
):
    half = mine_ref.shape[1]
    rows = norm_ref.shape[0]
    first = core[0] == 0

    @pl.when(pl.program_id(0) == 0)
    def _():
        w_ref[:, :half] = jnp.where(first, mine_ref[...], other_ref[...])
        w_ref[:, half:] = jnp.where(first, other_ref[...], mine_ref[...])

    at = pl.multiple_of(core[0] * rows * pl.num_programs(0) + pl.program_id(0) * rows, rows)
    branch = dot_nn(attended_ref[pl.ds(at, rows), :], w_ref[...]) + vec_ref[2:3, :]
    norm, normed, inverse = norm_parts(
        x_ref[...].astype(jnp.float32) + branch, vec_ref[4:5, :], vec_ref[5:6, :]
    )
    norm_ref[...] = norm
    normed_ref[...] = normed
    inverse_ref[...] = inverse
    low_ref[...] = norm.astype(jnp.bfloat16)


def first_norm_of(core, vec, attended, mine, other, x):
    rows, width = x.shape
    steps = 2
    block = pl.BlockSpec((rows // steps, width), lambda i: (i, 0))

    def all_of(a):
        return pl.BlockSpec(a.shape, lambda i: (0, 0))

    return pl.pallas_call(
        first_norm_kernel,
        grid=(steps,),
        in_specs=[pl.BlockSpec(memory_space=pltpu.SMEM)]
        + [all_of(a) for a in (vec, attended, mine, other)]
        + [block],
        out_specs=[
            block, block, pl.BlockSpec((rows // steps, 1), lambda i: (i, 0)), block,
            pl.BlockSpec((width, width), lambda i: (0, 0)),
        ],
        out_shape=[
            jax.ShapeDtypeStruct((rows, width), jnp.float32),
            jax.ShapeDtypeStruct((rows, width), jnp.float32),
            jax.ShapeDtypeStruct((rows, 1), jnp.float32),
            jax.ShapeDtypeStruct((rows, width), jnp.bfloat16),
            jax.ShapeDtypeStruct((width, width), jnp.bfloat16),
        ],
        compiler_params=pltpu.CompilerParams(vmem_limit_bytes=VMEM_LIMIT),
        cost_estimate=SHORT,
    )(core, vec, attended, mine, other, x)


def norm_back(upstream, normed, inverse, gain_vec):
    scaled = upstream * gain_vec
    row_inner = (
        scaled
        - jnp.mean(scaled, axis=-1, keepdims=True)
        - normed * jnp.mean(scaled * normed, axis=-1, keepdims=True)
    )
    return row_inner * inverse


def last_grads_kernel(
    spot, x_ref, local_ref, reach_ref, dkv_ref, beyond_ref, out_w_ref, attn_ref, ffn_ref,
    last_ref, grad_ref,
):
    core, chip = spot[0], spot[1]
    first = chip == 0
    rows, half = local_ref.shape
    grad_ref[:rows, :half] = jnp.where(first, local_ref[...], reach_ref[...])
    grad_ref[rows:, :half] = jnp.where(first, reach_ref[...], local_ref[...])
    for t in range(2):
        got = beyond_ref[t].astype(jnp.float32)
        part = slice((t + 1) * half, (t + 2) * half)
        top = dkv_ref[t, :rows, :] + jnp.where(first, 0.0, got)
        low = dkv_ref[t, rows:, :] + jnp.where(first, got, 0.0)
        grad_ref[:rows, part] = top.astype(jnp.bfloat16)
        grad_ref[rows:, part] = low.astype(jnp.bfloat16)
    grads = grad_ref[...]
    last_ref[0, :, : 3 * half] = dot_tn(x_ref[...], grads).astype(jnp.bfloat16)
    last_ref[0, :, 3 * half : 4 * half] = out_w_ref[...]
    sums = [
        jnp.sum(grads[:, i * half : (i + 1) * half].astype(jnp.float32), axis=0, keepdims=True)
        for i in (0, 2)
    ]
    nothing = jnp.zeros_like(sums[0])
    vectors = [
        jnp.where(
            core == 0, jnp.concatenate([s, nothing], axis=1), jnp.concatenate([nothing, s], axis=1)
        )
        for s in sums
    ]
    vectors += [attn_ref[2:3, :], ffn_ref[2:3, :], attn_ref[0:2, :], ffn_ref[0:2, :]]
    vectors.append(jnp.zeros((128 - VECTORS, 2 * half), jnp.float32))
    last_ref[0, :, 4 * half :] = jnp.concatenate(vectors, axis=0).T.astype(jnp.bfloat16)


def last_grads(spot, x, dq_local, dq_reach, dkv, beyond, grad_w_out, attn_sums, ffn_sums):
    all_rows, width = x.shape
    half = width // 2
    whole = pl.BlockSpec(memory_space=pltpu.VMEM)
    return pl.pallas_call(
        last_grads_kernel,
        in_specs=[pl.BlockSpec(memory_space=pltpu.SMEM)] + [whole] * 8,
        out_specs=[whole] * 2,
        out_shape=[
            jax.ShapeDtypeStruct((1, width, 4 * half + 128), jnp.bfloat16),
            jax.ShapeDtypeStruct((all_rows, 3 * half), jnp.bfloat16),
        ],
        compiler_params=pltpu.CompilerParams(vmem_limit_bytes=VMEM_LIMIT),
        cost_estimate=SHORT,
    )(spot, x, dq_local, dq_reach, dkv, beyond, grad_w_out, attn_sums, ffn_sums)


def finish_kernel(core, mine_ref, other_ref, *outs):
    first = core[0] == 0
    half = outs[0].shape[1] // 2
    for i, out in enumerate(outs[:4]):
        part = slice(i * half, (i + 1) * half)
        mine, other = mine_ref[:, part].astype(jnp.float32), other_ref[:, part].astype(jnp.float32)
        out[:, :half] = jnp.where(first, mine, other)
        out[:, half:] = jnp.where(first, other, mine)
    mine, other = mine_ref[:, 4 * half :], other_ref[:, 4 * half :]
    vectors = (mine.astype(jnp.float32) + other.astype(jnp.float32)).T
    for i, out in enumerate(outs[4:]):
        out[...] = vectors[i : i + 1, :]


def finish(core, mine, other):
    rows, columns = mine.shape
    width = (columns - 128) // 2
    whole = pl.BlockSpec(memory_space=pltpu.VMEM)
    results = pl.pallas_call(
        finish_kernel,
        in_specs=[pl.BlockSpec(memory_space=pltpu.SMEM)] + [whole] * 2,
        out_specs=[whole] * (4 + VECTORS),
        out_shape=[jax.ShapeDtypeStruct((rows, width), jnp.float32)] * 4
        + [jax.ShapeDtypeStruct((1, rows), jnp.float32)] * VECTORS,
        cost_estimate=SHORT,
    )(core, mine, other)
    return results[:4], results[4:]


def add_sums(step, sums_ref, *columns):
    rows = [jnp.sum(value, axis=0, keepdims=True) for value in columns]
    rows.append(jnp.zeros((8 - len(rows), sums_ref.shape[1]), jnp.float32))
    add_up(step, sums_ref, jnp.concatenate(rows, axis=0))


def second_norm_kernel(
    vec_ref, norm_ref, part_ref, sent_ref, cot_ref, out_ref, grad_ref, low_ref, sums_ref
):
    step = pl.program_id(0)
    bias, gain, shift = vec_ref[3:4, :], vec_ref[6:7, :], vec_ref[7:8, :]
    value = norm_ref[...] + part_ref[...] + sent_ref[...].astype(jnp.float32) + bias
    result, normed, inverse = norm_parts(value, gain, shift)
    out_ref[...] = result.astype(jnp.bfloat16)
    upstream = cot_ref[...].astype(jnp.float32)
    grad = norm_back(upstream, normed, inverse, gain)
    grad_ref[...] = grad
    low_ref[...] = grad.astype(jnp.bfloat16)
    add_sums(step, sums_ref, upstream * normed, upstream, grad)


def second_norm(vec, first_norm, part, sent, cotangent):
    rows, width = part.shape
    block = pl.BlockSpec((rows // 2, width), lambda i: (i, 0))
    eight = pl.BlockSpec((8, width), lambda i: (0, 0))
    return pl.pallas_call(
        second_norm_kernel,
        grid=(2,),
        in_specs=[eight] + [block] * 4,
        out_specs=[block] * 3 + [eight],
        out_shape=[
            jax.ShapeDtypeStruct((rows, width), jnp.bfloat16),
            jax.ShapeDtypeStruct((rows, width), jnp.float32),
            jax.ShapeDtypeStruct((rows, width), jnp.bfloat16),
            jax.ShapeDtypeStruct((8, width), jnp.float32),
        ],
        compiler_params=pltpu.CompilerParams(vmem_limit_bytes=VMEM_LIMIT),
        cost_estimate=SHORT,
    )(vec, first_norm, part, sent, cotangent)


def first_norm_back_kernel(
    core, vec_ref, w_ref, up_ref, part_ref, sent_ref, normed_ref, inverse_ref,
    grad_ref, low_mine, low_theirs, back_mine, back_theirs, sums_ref,
):
    step = pl.program_id(0)
    half = low_mine.shape[1]
    upstream = up_ref[...] + part_ref[...] + sent_ref[...].astype(jnp.float32)
    normed = normed_ref[...]
    grad = norm_back(upstream, normed, inverse_ref[...], vec_ref[4:5, :])
    grad_ref[...] = grad
    low = grad.astype(jnp.bfloat16)
    back = dot_nt(low, w_ref[...]).astype(jnp.bfloat16)
    first = core[0] == 0
    for value, mine, theirs in ((low, low_mine, low_theirs), (back, back_mine, back_theirs)):
        left, right = value[:, :half], value[:, half:]
        mine[...] = jnp.where(first, left, right)
        theirs[...] = jnp.where(first, right, left)
    add_sums(step, sums_ref, upstream * normed, upstream, grad)


def first_norm_back(core, vec, w_out, grad_second, part, sent, normed, inverse):
    rows, width = part.shape
    steps = 2
    block = pl.BlockSpec((rows // steps, width), lambda i: (i, 0))
    halves = pl.BlockSpec((rows // steps, width // 2), lambda i: (i, 0))
    eight = pl.BlockSpec((8, width), lambda i: (0, 0))
    return pl.pallas_call(
        first_norm_back_kernel,
        grid=(steps,),
        in_specs=[
            pl.BlockSpec(memory_space=pltpu.SMEM),
            eight,
            pl.BlockSpec((width, width), lambda i: (0, 0)),
        ]
        + [block] * 4
        + [pl.BlockSpec((rows // steps, 1), lambda i: (i, 0))],
        out_specs=[block] + [halves] * 4 + [eight],
        out_shape=[jax.ShapeDtypeStruct((rows, width), jnp.float32)]
        + [jax.ShapeDtypeStruct((rows, width // 2), jnp.bfloat16)] * 4
        + [jax.ShapeDtypeStruct((8, width), jnp.float32)],
        compiler_params=pltpu.CompilerParams(vmem_limit_bytes=VMEM_LIMIT),
        cost_estimate=SHORT,
    )(core, vec, w_out, grad_second, part, sent, normed, inverse)


def lay_out_kernel(core, mine_ref, other_ref, up_ref, gate_ref, down_ref):
    first = core[0] == 0
    count, shard_rows, width = mine_ref.shape
    groups = count // 3
    shards = width // shard_rows

    def both(i):
        mine, other = mine_ref[i].astype(jnp.float32), other_ref[i].astype(jnp.float32)
        return jnp.where(first, mine, other), jnp.where(first, other, mine)

    for g in range(groups):
        for c, value in enumerate(both(2 * groups + g)):
            at = (c * groups + g) * shard_rows
            down_ref[at : at + shard_rows, :] = value
        for t, out in ((0, up_ref), (1, gate_ref)):
            for c, value in enumerate(both(2 * g + t)):
                for s in range(shards):
                    at = ((s * 2 + c) * groups + g) * shard_rows
                    out[:, at : at + shard_rows] = value[:, s * shard_rows : (s + 1) * shard_rows]


def lay_out(core, mine, other):
    count, shard_rows, width = mine.shape
    columns = count // 3 * 2 * width
    whole = pl.BlockSpec(memory_space=pltpu.VMEM)
    return pl.pallas_call(
        lay_out_kernel,
        in_specs=[pl.BlockSpec(memory_space=pltpu.SMEM)] + [whole] * 2,
        out_specs=[whole] * 3,
        out_shape=[
            jax.ShapeDtypeStruct((shard_rows, columns), jnp.float32),
            jax.ShapeDtypeStruct((shard_rows, columns), jnp.float32),
            jax.ShapeDtypeStruct((count // 3 * 2 * shard_rows, width), jnp.float32),
        ],
        compiler_params=pltpu.CompilerParams(vmem_limit_bytes=VMEM_LIMIT),
        cost_estimate=SHORT,
    )(core, mine, other)


def phi_parts(v):
    cdf = 0.5 * (1.0 + lax.erf(v * math.sqrt(0.5)))
    density = jnp.exp(-0.5 * v * v) * (1.0 / math.sqrt(2.0 * math.pi))
    return cdf, cdf + v * density


def fill_weight(numbers, pieces, weight):
    rows = pieces[0].shape[0]
    for i, piece in enumerate(pieces):
        weight[pl.ds(pl.multiple_of(numbers[i] * rows, rows), rows), :] = piece[...]


def add_up(step, total, out):
    @pl.when(step == 0)
    def _():
        total[...] = out

    @pl.when(step > 0)
    def _():
        total[...] += out


def ffn_fwd_kernel(numbers, own_ref, other_ref, *refs):
    ups, gates, downs = refs[:8], refs[8:16], refs[16:24]
    hid_ref, act_ref, slope_ref, part_ref, send_ref = refs[24:29]
    x_all, up_w, gate_w, down_w, total = refs[29:]
    step = pl.program_id(0)
    rows = own_ref.shape[0]

    @pl.when(step == 0)
    def _():
        x_all[:rows, :] = own_ref[...]
        x_all[rows:, :] = other_ref[...]

    fill_weight(numbers, ups, up_w)
    fill_weight(numbers, gates, gate_w)
    fill_weight(numbers, downs, down_w)
    columns = up_w.shape[1]
    piece = columns // 3
    for i in range(3):
        part = slice(i * piece, (i + 1) * piece)
        x = x_all[...]
        up = dot_nn(x, up_w[:, part])
        gate = dot_nn(x, gate_w[:, part])
        cdf, derivative = phi_parts(gate)
        act = gate * cdf
        hidden = (act * up).astype(jnp.bfloat16)
        hid_ref[:, part] = hidden
        act_ref[:, part] = act.astype(jnp.bfloat16)
        slope_ref[:, part] = (derivative * up).astype(jnp.bfloat16)
    add_up(step, total, dot_nn(hid_ref[...], down_w[...]))

    @pl.when(step == pl.num_programs(0) - 1)
    def _():
        part_ref[...] = total[:rows, :]
        send_ref[...] = total[rows:, :].astype(jnp.bfloat16)


def piece_specs(rows, width, columns):
    steps = columns // width
    return [
        pl.BlockSpec((rows, width), lambda f, t=t: (0, t * steps + f))
        for t in range(3)
        for i in range(8)
    ]


def ffn_forward(own, other, pieces, numbers, columns):
    rows, width = own.shape
    steps = columns // width
    wide = pl.BlockSpec((2 * rows, width), lambda f: (0, f))
    whole = pl.BlockSpec((rows, width), lambda f: (0, 0))
    return pl.pallas_call(
        ffn_fwd_kernel,
        grid=(steps,),
        in_specs=[pl.BlockSpec(memory_space=pltpu.SMEM), whole, whole]
        + piece_specs(pieces[0].shape[0], width, columns),
        out_specs=[wide, wide, wide, whole, whole],
        out_shape=[jax.ShapeDtypeStruct((2 * rows, columns), jnp.bfloat16)] * 3
        + [
            jax.ShapeDtypeStruct((rows, width), jnp.float32),
            jax.ShapeDtypeStruct((rows, width), jnp.bfloat16),
        ],
        scratch_shapes=[
            pltpu.VMEM((2 * rows, width), jnp.bfloat16),
            pltpu.VMEM((width, width), jnp.bfloat16),
            pltpu.VMEM((width, width), jnp.bfloat16),
            pltpu.VMEM((width, width), jnp.bfloat16),
            pltpu.VMEM((2 * rows, width), jnp.float32),
        ],
        compiler_params=pltpu.CompilerParams(vmem_limit_bytes=VMEM_LIMIT),
        cost_estimate=SHORT,
    )(numbers, own, other, *(pieces * 3))


def down_grad_kernel(group, branch_ref, branch_other_ref, hid_ref, grad_ref):
    rows = branch_ref.shape[0]
    total = dot_tn(hid_ref[:rows, :], branch_ref[...])
    grad_ref[...] = (total + dot_tn(hid_ref[rows:, :], branch_other_ref[...])).astype(jnp.bfloat16)


def down_grad(group, branch, branch_other, hidden):
    rows, width = branch.shape
    whole = pl.BlockSpec((rows, width), lambda i, group: (0, 0))
    return pl.pallas_call(
        down_grad_kernel,
        grid_spec=pltpu.PrefetchScalarGridSpec(
            num_scalar_prefetch=1,
            grid=(1,),
            in_specs=[
                whole, whole, pl.BlockSpec((2 * rows, width), lambda i, group: (0, group[0])),
            ],
            out_specs=pl.BlockSpec((width, width), lambda i, group: (0, 0)),
        ),
        out_shape=jax.ShapeDtypeStruct((width, width), jnp.bfloat16),
        compiler_params=pltpu.CompilerParams(vmem_limit_bytes=VMEM_LIMIT),
        cost_estimate=SHORT,
    )(group, branch, branch_other, hidden)


def add_last_kernel(all_ref, keep_ref, got_ref, out_ref):
    out_ref[0] = keep_ref[...] + got_ref[...]


def add_last(grads, keep, got):
    last = grads.shape[0] - 1
    whole = pl.BlockSpec(memory_space=pltpu.VMEM)
    return pl.pallas_call(
        add_last_kernel,
        grid=(1,),
        in_specs=[pl.BlockSpec(memory_space=pl.ANY), whole, whole],
        out_specs=pl.BlockSpec((1,) + grads.shape[1:], lambda i: (last, 0, 0)),
        out_shape=jax.ShapeDtypeStruct(grads.shape, grads.dtype),
        input_output_aliases={0: 0},
        compiler_params=pltpu.CompilerParams(vmem_limit_bytes=VMEM_LIMIT),
        cost_estimate=SHORT,
    )(grads, keep, got)


def ffn_bwd_kernel(numbers, own_ref, other_ref, branch_ref, branch_other_ref, act_ref, slope_ref, *refs):
    ups, gates, downs = refs[:8], refs[8:16], refs[16:24]
    grad_ref, part_ref, send_ref = refs[24:27]
    x_all, branch_all, up_w, gate_w, down_w, total = refs[27:]
    step = pl.program_id(0)
    rows = own_ref.shape[0]

    @pl.when(step == 0)
    def _():
        x_all[:rows, :] = own_ref[...]
        x_all[rows:, :] = other_ref[...]
        branch_all[:rows, :] = branch_ref[...]
        branch_all[rows:, :] = branch_other_ref[...]

    fill_weight(numbers, ups, up_w)
    fill_weight(numbers, gates, gate_w)
    fill_weight(numbers, downs, down_w)
    x = x_all[...]
    outs = []
    piece = up_w.shape[1] // 3
    for i in range(3):
        part = slice(i * piece, (i + 1) * piece)
        d_hidden = dot_nt(branch_all[...], down_w[part, :])
        d_up = (d_hidden * act_ref[:, part].astype(jnp.float32)).astype(jnp.bfloat16)
        d_gate = (d_hidden * slope_ref[:, part].astype(jnp.float32)).astype(jnp.bfloat16)
        outs.append(dot_nt(d_up, up_w[:, part]) + dot_nt(d_gate, gate_w[:, part]))
        grad_ref[0, :, part] = dot_tn(x, d_up).astype(jnp.bfloat16)
        grad_ref[1, :, part] = dot_tn(x, d_gate).astype(jnp.bfloat16)
    add_up(step, total, outs[0] + outs[1] + outs[2])

    @pl.when(step == pl.num_programs(0) - 1)
    def _():
        part_ref[...] = total[:rows, :]
        send_ref[...] = total[rows:, :].astype(jnp.bfloat16)


def ffn_backward(own, other, branch, branch_other, act, slope, pieces, numbers, columns):
    rows, width = own.shape
    steps = columns // width
    wide = pl.BlockSpec((2 * rows, width), lambda f: (0, f))
    whole = pl.BlockSpec((rows, width), lambda f: (0, 0))
    return pl.pallas_call(
        ffn_bwd_kernel,
        grid=(steps,),
        in_specs=[pl.BlockSpec(memory_space=pltpu.SMEM)]
        + [whole] * 4
        + [wide] * 2
        + piece_specs(pieces[0].shape[0], width, columns),
        out_specs=[
            pl.BlockSpec((2, width, width), lambda f: (f, 0, 0)),
            whole,
            whole,
        ],
        out_shape=[
            jax.ShapeDtypeStruct((2 * steps + 1, width, width), jnp.bfloat16),
            jax.ShapeDtypeStruct((rows, width), jnp.float32),
            jax.ShapeDtypeStruct((rows, width), jnp.bfloat16),
        ],
        scratch_shapes=[
            pltpu.VMEM((2 * rows, width), jnp.bfloat16),
            pltpu.VMEM((2 * rows, width), jnp.bfloat16),
            pltpu.VMEM((width, width), jnp.bfloat16),
            pltpu.VMEM((width, width), jnp.bfloat16),
            pltpu.VMEM((width, width), jnp.bfloat16),
            pltpu.VMEM((2 * rows, width), jnp.float32),
        ],
        compiler_params=pltpu.CompilerParams(vmem_limit_bytes=VMEM_LIMIT),
        cost_estimate=SHORT,
    )(numbers, own, other, branch, branch_other, act, slope, *(pieces * 3))


def pack_kernel(core, up_ref, gate_ref, down_ref, out_ref):
    first = core[0] == 0
    shard_rows = up_ref.shape[0]
    width = down_ref.shape[1]
    shards = width // shard_rows
    groups = down_ref.shape[0] // shard_rows // 2
    at = 0
    for ref in (up_ref, gate_ref):
        for g in range(groups):
            for s in range(shards):
                left = (s * 2 * groups + g) * shard_rows
                right = left + groups * shard_rows
                out_ref[:, at : at + shard_rows] = jnp.where(
                    first, ref[:, left : left + shard_rows], ref[:, right : right + shard_rows]
                )
                at += shard_rows
    for g in range(groups):
        top = g * shard_rows
        low = top + groups * shard_rows
        out_ref[:, at : at + width] = jnp.where(
            first, down_ref[top : top + shard_rows, :], down_ref[low : low + shard_rows, :]
        )
        at += width


def pack(core, up, gate, down):
    shard_rows = up.shape[0]
    width = down.shape[1]
    whole = pl.BlockSpec(memory_space=pltpu.VMEM)
    return pl.pallas_call(
        pack_kernel,
        in_specs=[pl.BlockSpec(memory_space=pltpu.SMEM)] + [whole] * 3,
        out_specs=whole,
        out_shape=jax.ShapeDtypeStruct(
            (shard_rows, up.shape[1] + down.shape[0] // shard_rows // 2 * width), jnp.bfloat16
        ),
        compiler_params=pltpu.CompilerParams(vmem_limit_bytes=VMEM_LIMIT),
        cost_estimate=SHORT,
    )(core, up, gate, down)


def pack_first_kernel(core, *refs):
    first = core[0] == 0
    half = refs[0].shape[1] // 2
    out_ref = refs[-1]
    for i, ref in enumerate(refs[:4]):
        out_ref[:, i * half : (i + 1) * half] = jnp.where(first, ref[:, :half], ref[:, half:])
    out_ref[:, 4 * half :] = refs[4][...]


def pack_first(core, matrices, vectors):
    rows, width = matrices[0].shape
    whole = pl.BlockSpec(memory_space=pltpu.VMEM)
    return pl.pallas_call(
        pack_first_kernel,
        in_specs=[pl.BlockSpec(memory_space=pltpu.SMEM)] + [whole] * 5,
        out_specs=whole,
        out_shape=jax.ShapeDtypeStruct((rows, 2 * width + vectors.shape[1]), jnp.bfloat16),
        cost_estimate=SHORT,
    )(core, *matrices, vectors)


def on_device(
    tokens, segments, padding,
    w_query, w_key, w_value, w_out, w_up, w_gate, w_down,
    bias_query, bias_value, bias_out, bias_down, gain_attn, shift_attn, gain_ffn, shift_ffn,
    cotangent,
):
    tuned = lax.axis_size("ctx") == 4 and lax.axis_size("fsdp") == 8
    row_gather, row_reduce = (Gather, Reduce) if tuned else (PlainGather, PlainReduce)
    core = lax.axis_index("ctx") % 2
    chip = lax.axis_index("ctx") // 2
    chip_ref = chip[None].astype(jnp.int32)
    core_ref = core[None].astype(jnp.int32)
    inputs = tokens[0]
    rows, width = inputs.shape
    half = width // 2
    half_ff = FF // 2

    def cut(value, which, count, axis):
        return lax.dynamic_slice_in_dim(value, which * count, count, axis)

    def share(mine, theirs, axis):
        return ordered(core, mine, over_core(theirs), axis)

    vectors = jnp.stack(
        (bias_query, bias_value, bias_out, bias_down, gain_attn, shift_attn, gain_ffn, shift_ffn), axis=1
    )
    vectors = jnp.pad(vectors, ((0, 0), (0, 128 - VECTORS)))
    first = row_gather(pack_first(core_ref, (w_query, w_key, w_value, w_out), vectors))
    second = row_gather(pack(core_ref, w_up, w_gate, w_down))
    first.first()

    own_numbers = jnp.stack((segments[0], jnp.where(padding[0] == 1, -1, segments[0])))
    numbers = share(own_numbers, own_numbers, 1)
    slopes = cut(head_slopes(H), core, H // 2, 0)
    (numbers,) = first.join(numbers)
    tags = numbers[1]
    seg_row = numbers[0][None, :]
    if tuned:
        tags_send = jnp.where(chip == 0, tags[rows:], tags[:rows]) + 2
        first.second()
        beyond = over_x(tags_send)
        beyond, second.own = first.join(beyond, second.own)
        beyond = beyond - 2
        tags_reach = ordered(chip, tags, beyond, 0)[:, None]
        tags_local = tags[:, None]
        seg_local = cut(seg_row, chip, rows, 1)
        seg_reach = cut(seg_row, 1 - chip, rows, 1)
    else:
        tag_low = from_previous_chip(tags[rows:] + 2) - 2
        tag_high = from_next_chip(tags[:rows] + 2) - 2
        tags_wide = jnp.concatenate([tag_low, tags, tag_high])[:, None]
    first.third()
    inputs_all = share(inputs, inputs, 0)
    (inputs_all,) = first.join(inputs_all)
    (second.own,) = first.fourth(second.own)
    second.first_z()
    (second.own,) = first.join(second.own)
    second.first_y()

    spot = jnp.stack((core, chip if tuned else jnp.zeros_like(chip))).astype(jnp.int32)
    vec, full_qkv, out_half, queries_local, queries_reach, keys_values, beyond = project(
        first.numbers(), spot, inputs_all, first.pieces()
    )
    out_other = over_core(out_half)
    if tuned:
        queries_local, queries_reach, keys_values, beyond = second.join(
            queries_local, queries_reach, keys_values, beyond
        )
        beyond = over_x(beyond)
        second.second()
        attended_local, lse_local = attention_forward(
            local_blocks, chip_ref, queries_local, keys_values, seg_local, tags_local, slopes
        )
        attended_local, lse_local, beyond = second.join(attended_local, lse_local, beyond)
        keys_values, kv_beyond = second.third(keys_values, beyond)
        attended_reach, lse_reach = attention_forward(
            reach_blocks, chip_ref, queries_reach, keys_values, seg_reach, tags_reach, slopes, kv_beyond
        )
        attended_own = ordered(chip, attended_local, attended_reach, 0)
        (attended_own,) = second.join(attended_own)
        (attended_own,) = second.fourth(attended_own)
    else:
        queries = jnp.concatenate([queries_local, queries_reach], axis=0)
        kv_low = from_previous_chip(keys_values[rows:])
        kv_high = from_next_chip(keys_values[:rows])
        kv_wide = jnp.concatenate([kv_low, keys_values, kv_high], axis=0)
        spans = [(i * rows, i * rows + rows + 2 * HALF) for i in range(2)]
        forward_parts = [
            attention_forward(
                reach_blocks, chip_ref, queries[i * rows : (i + 1) * rows], kv_wide[low:high],
                seg_row[:, i * rows : (i + 1) * rows], tags_wide[low:high], slopes,
            )
            for i, (low, high) in enumerate(spans)
        ]
        attended_own = jnp.concatenate([part[0] for part in forward_parts], axis=0)
    attended_all = share(attended_own, attended_own, 1)
    first_norm, first_normed, first_inverse, own_low, full_out = first_norm_of(
        core_ref, vec, attended_all, out_half, out_other, inputs
    )
    other_low = over_core(own_low)
    if tuned:
        own_low, other_low = second.join(own_low, other_low)
    pieces = second.pieces()
    places = second.numbers()
    hidden, act, slope, ffn_part, ffn_send = ffn_forward(own_low, other_low, pieces, places, half_ff)
    layer_out, grad_second, own_branch, ffn_sums = second_norm(
        vec, first_norm, ffn_part, over_core(ffn_send), cotangent[0]
    )
    branch_other = over_core(own_branch)
    group = chip_ref if tuned else jnp.zeros_like(chip_ref)
    down_send = down_grad(1 - group, own_branch, branch_other, hidden)
    if tuned:
        down_send, own_branch, branch_other = tie(down_send, own_branch, branch_other)
        down_got = over_x(down_send)
    down_keep = down_grad(group, own_branch, branch_other, hidden)
    down_keep, own_branch, branch_other = tie(down_keep, own_branch, branch_other)
    grad_weights, normed_part, normed_send = ffn_backward(
        own_low, other_low, own_branch, branch_other, act, slope, pieces, places, half_ff
    )
    if tuned:
        grad_weights, normed_send, down_got = tie(grad_weights, normed_send, down_got)
        grad_weights = add_last(grad_weights, down_keep, down_got)
    else:
        grad_weights = jnp.concatenate([grad_weights[:-1], down_keep[None], down_send[None]])
    reduce_ffn = row_reduce(grad_weights)
    (normed_send,) = reduce_ffn.first(normed_send)
    grad_first, low_mine, low_theirs, back_mine, back_theirs, attn_sums = first_norm_back(
        core_ref, vec, full_out, grad_second, normed_part, over_core(normed_send),
        first_normed, first_inverse,
    )
    back_other = over_core(back_theirs)
    low_other = over_core(low_theirs)

    if tuned:
        back_ref = jnp.stack((chip, core == chip)).astype(jnp.int32)
        def reach_part(low, count, into):
            return attention_backward(
                reach_blocks, back_ref, queries_reach, keys_values, attended_reach, back_other, back_mine,
                lse_reach, seg_reach, tags_reach, slopes, None, low, count, into, kv_beyond,
            )

        low_all = ordered(core, low_mine, low_other, 0)
        pairs = half // (2 * HD)
        reached = reduce_ffn.join(*reach_part(0, 1, ()))
        reached = reduce_ffn.second(*reached)
        dq_reach, dkv_reach, beyond = reach_part(1, pairs - 1, tuple(reached))
        dq_reach, dkv_reach, beyond, low_all = tie(dq_reach, dkv_reach, beyond, low_all)
        beyond = over_x(beyond)
        grad_w_out = dot_tn(attended_all, low_all)
        dq_reach, dkv_reach, grad_w_out = reduce_ffn.join(dq_reach, dkv_reach, grad_w_out)
        dq_reach, dkv_reach, grad_w_out = reduce_ffn.third(dq_reach, dkv_reach, grad_w_out)
        dq_local, dkv_local = attention_backward(
            local_blocks, back_ref, queries_local, keys_values, attended_local,
            back_mine, back_other, lse_local, seg_local, tags_local, slopes, dkv_reach,
        )
        dq_local, dkv_local, beyond = reduce_ffn.join(dq_local, dkv_local, beyond)
        reduce_ffn.fourth()
    else:
        grad_attended = ordered(core, back_mine, back_other, 0)
        back_ref = jnp.ones((2,), jnp.int32)
        backward_parts = [
            attention_backward(
                reach_blocks, back_ref, queries[i * rows : (i + 1) * rows], kv_wide[low:high],
                forward_parts[i][0], grad_attended[i * rows : (i + 1) * rows],
                grad_attended[i * rows : (i + 1) * rows], forward_parts[i][1],
                seg_row[:, i * rows : (i + 1) * rows], tags_wide[low:high], slopes, None,
            )
            for i, (low, high) in enumerate(spans)
        ]
        dq_local, dq_reach = [part[0] for part in backward_parts]
        reach_0, reach_1 = [part[1] for part in backward_parts]
        from_next = from_next_chip(reach_0[:, :HALF].astype(jnp.bfloat16)).astype(jnp.float32)
        from_previous = from_previous_chip(reach_1[:, rows + HALF :].astype(jnp.bfloat16)).astype(jnp.float32)
        centre = jnp.pad(reach_0[:, HALF:], ((0, 0), (0, 2 * rows - reach_0.shape[1] + HALF), (0, 0)))
        centre = centre + jnp.pad(
            reach_1[:, : rows + HALF], ((0, 0), (2 * rows - rows - HALF, 0), (0, 0))
        )
        centre = centre.at[:, 2 * rows - HALF :].add(from_next)
        dkv_local = centre.at[:, :HALF].add(from_previous)
        beyond = jnp.zeros_like(from_next, dtype=jnp.bfloat16)
        grad_w_out = dot_tn(attended_all, ordered(core, low_mine, low_other, 0))
    grad_last, grad_qkv = last_grads(
        spot, inputs_all, dq_local, dq_reach, dkv_local, beyond, grad_w_out.astype(jnp.bfloat16),
        attn_sums, ffn_sums,
    )
    last = row_reduce(grad_last)
    last.first()
    reduce_ffn.join()
    last.join()
    last.second()
    input_part = dot_nt(grad_qkv, full_qkv)
    grad_inputs = (
        grad_first
        + cut(input_part, core, rows, 0)
        + over_core(cut(input_part, 1 - core, rows, 0).astype(jnp.bfloat16)).astype(jnp.float32)
    )
    ffn_mine = reduce_ffn.result()
    if tuned:
        got = over_x(ffn_mine)
        ffn_mine = jnp.concatenate(
            [ffn_mine[:-1] + got[:-1], ordered(chip, ffn_mine[-1:], got[-1:], 0)], axis=0
        )
    else:
        ffn_mine = chips_sum(ffn_mine)
    (grad_inputs,) = last.join(grad_inputs)
    last.third()
    last.join()
    last.fourth()
    grad_up, grad_gate, grad_down = lay_out(core_ref, ffn_mine, over_core(ffn_mine))
    if tuned:
        grad_up, grad_gate, grad_down = last.join(grad_up, grad_gate, grad_down)
    last_mine = chips_sum(last.result())[0]
    last_rows, vector_rows = finish(core_ref, last_mine, over_core(last_mine))

    return (
        layer_out[None],
        grad_inputs[None],
        *last_rows,
        grad_up,
        grad_gate,
        grad_down,
    ) + tuple(row[0] for row in vector_rows)


def solution(mesh):
    rows_spec = P("fsdp", "ctx", None)
    in_specs = (
        (rows_spec, P("fsdp", "ctx"), P("fsdp", "ctx"))
        + (P("fsdp", None),) * 7
        + (P("fsdp"),) * VECTORS
        + (rows_spec,)
    )
    out_specs = (rows_spec, rows_spec) + (P("fsdp", None),) * 7 + (P("fsdp"),) * VECTORS
    return jax.shard_map(
        on_device, mesh=mesh, in_specs=in_specs, out_specs=out_specs, check_vma=False
    )
```

```python
import math
import jax
import jax.numpy as jnp
from jax import lax
from jax.experimental import pallas as pl
from jax.experimental.pallas import tpu as pltpu
from jax.sharding import PartitionSpec as P

H = 12
HD = 64
FF = 3072
HALF = 512
EPSILON = 1e-06
VECTORS = 8
QB = 256
ROW_BLOCK = 1024
SPAN = QB + 2 * HALF
BIG = 1e30
MIB = 1024 * 1024
SHORT = pl.CostEstimate(flops=1024, bytes_accessed=1024, transcendentals=0)

Z_SWAP = ((0, 1), (1, 0), (2, 3), (3, 2))
Z_MID = ((1, 2), (2, 1))
Z_OUT = ((1, 0), (2, 3))
Z_IN = ((0, 1), (3, 2))


def dot_nn(a, b):
    return lax.dot_general(a, b, (((1,), (0,)), ((), ())), preferred_element_type=jnp.float32)


def dot_nt(a, b):
    return lax.dot_general(a, b, (((1,), (1,)), ((), ())), preferred_element_type=jnp.float32)


def dot_tn(a, b):
    return lax.dot_general(a, b, (((0,), (0,)), ((), ())), preferred_element_type=jnp.float32)


def tie(*values):
    return lax.optimization_barrier(values)


def head_slopes(number):
    power_two = 2 ** int(math.floor(math.log2(number)))
    first_part = [2.0 ** (-8.0 * (position + 1) / power_two) for position in range(power_two)]
    extra_part = [
        2.0 ** (-8.0 * (2 * position + 1) / (2 * power_two))
        for position in range(number - power_two)
    ]
    return jnp.array(first_part + extra_part, dtype=jnp.float32)


def over_core(x):
    count = lax.axis_size("ctx")
    return lax.ppermute(x, "ctx", [(i, i ^ 1) for i in range(count)])


def from_previous_chip(x):
    count = lax.axis_size("ctx")
    return lax.ppermute(x, "ctx", [(i, i + 2) for i in range(count - 2)])


def from_next_chip(x):
    count = lax.axis_size("ctx")
    return lax.ppermute(x, "ctx", [(i + 2, i) for i in range(count - 2)])


def over_x(x):
    return lax.ppermute(x, "ctx", [(i, i ^ 2) for i in range(4)])


def over_y(x):
    return lax.ppermute(x, "fsdp", [(i, i ^ 1) for i in range(8)])


def over_z(x, moves):
    return lax.ppermute(
        x, "fsdp", [(2 * a + y, 2 * b + y) for a, b in moves for y in range(2)]
    )


def ordered(core, own, other, axis):
    return jnp.where(
        core == 0,
        jnp.concatenate([own, other], axis=axis),
        jnp.concatenate([other, own], axis=axis),
    )


def shard_number(k, dy):
    me = lax.axis_index("fsdp")
    return me ^ (2 * k + dy)


class Chain:
    live = ()

    def join(self, *values):
        held = tie(*[getattr(self, name) for name in self.live], *values)
        for name, value in zip(self.live, held):
            setattr(self, name, value)
        return held[len(self.live) :]


class Gather(Chain):
    def __init__(self, piece):
        self.own = piece

    def first_z(self):
        self.a = over_z(self.own, Z_SWAP)
        self.b = over_z(self.own, Z_MID)

    def first_y(self):
        self.y0 = over_y(self.own)
        self.live = ("y0", "a", "b")

    def first(self):
        self.first_z()
        self.first_y()

    def second(self, *values):
        self.a, self.b, *values = tie(self.a, self.b, *values)
        self.c = over_z(self.a, Z_MID)
        self.d = over_z(self.b, Z_OUT)
        self.ya = over_y(self.a)
        self.live = ("c", "d", "ya")
        return values

    def third(self, *values):
        self.z2, *values = tie(self.c + self.d, *values)
        self.e = over_z(self.c, Z_OUT)
        self.yz2 = over_y(self.z2)
        self.live = ("e", "yz2")
        return values

    def fourth(self, *values):
        self.z3, *values = tie(self.b + self.e, *values)
        self.yz3 = over_y(self.z3)
        self.live = ("yz3",)
        return values

    def pieces(self):
        return [self.own, self.a, self.z2, self.z3, self.y0, self.ya, self.yz2, self.yz3]

    def numbers(self):
        return jnp.stack([shard_number(k, dy) for dy in range(2) for k in range(4)])


class Reduce(Chain):
    def __init__(self, pieces):
        self.pieces = pieces

    def part(self, k, dy):
        return self.pieces[4 * dy + k]

    def first(self, *values):
        send, *values = tie(self.part(3, 1), *values)
        self.y = over_y(send)
        self.live = ("y",)
        return values

    def second(self, *values):
        self.q3, send, *values = tie(self.part(3, 0) + self.y, self.part(2, 1), *values)
        self.y = over_y(send)
        self.e = over_z(self.q3, Z_IN)
        self.live = ("y", "e")
        return values

    def third(self, *values):
        q2 = self.part(2, 0) + self.y
        self.q2, on, send, *values = tie(q2, q2 + self.e, self.part(1, 1), *values)
        self.y = over_y(send)
        self.d = over_z(self.q2, Z_IN)
        self.c = over_z(on, Z_MID)
        self.live = ("y", "d", "c")
        return values

    def fourth(self, *values):
        on_b, on_a, send, *values = tie(
            self.q3 + self.d, self.part(1, 0) + self.y + self.c, self.part(0, 1), *values
        )
        self.y = over_y(send)
        self.b = over_z(on_b, Z_MID)
        self.a = over_z(on_a, Z_SWAP)
        self.live = ("y", "b", "a")
        return values

    def result(self):
        return self.part(0, 0) + self.y + self.a + self.b


class PlainGather(Chain):
    def __init__(self, piece):
        self.own = piece

    def first(self, *values):
        return values

    first_z = first_y = second = third = fourth = first

    def pieces(self):
        whole = lax.all_gather(self.own, "fsdp", axis=0, tiled=True)
        rows = whole.shape[0] // 8
        return [whole[i * rows : (i + 1) * rows] for i in range(8)]

    def numbers(self):
        return jnp.arange(8, dtype=jnp.int32)


class PlainReduce(Chain):
    def __init__(self, pieces):
        self.full = jnp.concatenate(pieces, axis=1)

    def first(self, *values):
        return values

    second = third = fourth = first

    def result(self):
        return lax.psum_scatter(self.full, "fsdp", scatter_dimension=1, tiled=True)


def chips_sum(total):
    count = lax.axis_size("ctx")
    if count == 4:
        return total + over_x(total)
    core = lax.axis_index("ctx") % 2
    slots = jnp.stack(
        [jnp.where(core == i, total, jnp.zeros_like(total)) for i in range(2)]
    )
    return lax.dynamic_index_in_dim(lax.psum(slots, "ctx"), core, 0, keepdims=False)


def local_blocks(chip):
    return (
        (pl.multiple_of(chip * QB, QB), pl.multiple_of(chip * QB, QB), HALF + QB, chip * HALF),
        (pl.multiple_of((1 - chip) * QB, QB), 0, 2 * HALF, QB + chip * QB),
    )


def reach_blocks(chip):
    return ((0, 0, SPAN, HALF), (QB, QB, SPAN, HALF))


def rows_at(start, count):
    return pl.ds(start, count)


def both_chips(chip, local_ref, beyond_ref, all_ref):
    own = local_ref.shape[0]
    count = beyond_ref.shape[0]
    all_ref[rows_at(pl.multiple_of(chip * count, count), own), :] = local_ref[...]
    all_ref[rows_at(pl.multiple_of((1 - chip) * own, count), count), :] = beyond_ref[...]


def fill_distance(dist, block, seg_ref, tag_ref):
    q_at, k_at, span, shift = block
    key_pos = lax.broadcasted_iota(jnp.int32, (span, QB), 0)
    row_pos = lax.broadcasted_iota(jnp.int32, (span, QB), 1) + shift
    gap = jnp.abs(key_pos - row_pos)
    same = tag_ref[rows_at(k_at, span), :] == seg_ref[:, rows_at(q_at, QB)]
    kept = ((gap <= HALF) & same) | (gap == 0)
    dist[...] = jnp.where(kept, gap.astype(jnp.float32), BIG)


def attn_fwd_kernel(
    plan, chip, slopes, q_ref, k_ref, v_ref, seg_ref, tag_ref, k_else, v_else, out_ref, lse_ref, *dists
):
    pair = pl.program_id(0)
    blocks = plan(chip[0])
    if k_else is not None:
        *dists, k_all, v_all = dists
        both_chips(chip[0], k_ref, k_else, k_all)
        both_chips(chip[0], v_ref, v_else, v_all)
        k_ref, v_ref = k_all, v_all

    @pl.when(pair == 0)
    def _():
        for dist, block in zip(dists, blocks):
            fill_distance(dist, block, seg_ref, tag_ref)

    lane = lax.broadcasted_iota(jnp.int32, (QB, 2 * HD), 1)
    work = [(dist, block, a) for dist, block in zip(dists, blocks) for a in range(2)]

    def raw_scores(item):
        dist, (q_at, k_at, span, shift), a = item
        q = q_ref[rows_at(q_at, QB), :]
        mine = (lane >= HD) if a else (lane < HD)
        q_a = jnp.where(mine, q, jnp.zeros_like(q)) * jnp.asarray(1.0 / math.sqrt(HD), q.dtype)
        return dot_nt(k_ref[rows_at(k_at, span), :], q_a)

    ahead = raw_scores(work[0])
    parts = []
    for i, (dist, (q_at, k_at, span, shift), a) in enumerate(work):
        raw = ahead
        if i + 1 < len(work):
            ahead = raw_scores(work[i + 1])
        if a == 0:
            v_t = v_ref[rows_at(k_at, span), :].T
            parts = []
        s = raw - slopes[2 * pair + a] * dist[...]
        top = jnp.max(s, axis=0, keepdims=True)
        p = jnp.exp(s - top)
        total = jnp.sum(p, axis=0, keepdims=True)
        o_t = dot_nn(v_t[a * HD : (a + 1) * HD, :], p.astype(jnp.bfloat16))
        parts.append(o_t * (1.0 / total))
        lse_ref[0, a : a + 1, rows_at(q_at, QB)] = top + jnp.log(total)
        if a == 1:
            out_ref[rows_at(q_at, QB), :] = jnp.concatenate(parts, axis=0).T.astype(jnp.bfloat16)


def distances(plan):
    return [pltpu.VMEM((block[2], QB), jnp.float32) for block in plan(0)]


def attention_forward(plan, chip, queries, keys_values, seg_row, tag_col, slopes, beyond=None):
    rows, width = queries.shape
    ext = tag_col.shape[0]
    own = keys_values.shape[0]
    more = () if beyond is None else (beyond, beyond)
    pairs = width // (2 * HD)

    def body(*refs):
        if beyond is None:
            refs = refs[:7] + (None, None) + refs[7:]
        attn_fwd_kernel(plan, *refs)

    return pl.pallas_call(
        body,
        grid=(pairs,),
        in_specs=[
            pl.BlockSpec(memory_space=pltpu.SMEM),
            pl.BlockSpec(memory_space=pltpu.SMEM),
            pl.BlockSpec((rows, 2 * HD), lambda h: (0, h)),
            pl.BlockSpec((own, 2 * HD), lambda h: (0, h)),
            pl.BlockSpec((own, 2 * HD), lambda h: (0, pairs + h)),
            pl.BlockSpec((1, rows), lambda h: (0, 0)),
            pl.BlockSpec((ext, 1), lambda h: (0, 0)),
        ]
        + [
            pl.BlockSpec((ext - own, 2 * HD), lambda h, t=t: (0, t * pairs + h))
            for t in range(len(more))
        ],
        out_specs=[
            pl.BlockSpec((rows, 2 * HD), lambda h: (0, h)),
            pl.BlockSpec((1, 8, rows), lambda h: (h, 0, 0)),
        ],
        out_shape=[
            jax.ShapeDtypeStruct((rows, width), jnp.bfloat16),
            jax.ShapeDtypeStruct((pairs, 8, rows), jnp.float32),
        ],
        scratch_shapes=distances(plan) + [pltpu.VMEM((ext, 2 * HD), jnp.bfloat16)] * len(more),
        compiler_params=pltpu.CompilerParams(vmem_limit_bytes=56 * MIB),
        cost_estimate=SHORT,
    )(chip, slopes, queries, keys_values, keys_values, seg_row, tag_col, *more)


def attn_bwd_kernel(
    plan, low, chip, slopes, q_ref, k_ref, v_ref, o_ref, do_ref, do_else_ref, lse_ref, seg_ref, tag_ref, start_ref,
    k_else, v_else, dq_ref, dkv_ref, beyond_ref, *dists,
):
    step = pl.program_id(0)
    pair = step + low
    blocks = plan(chip[0])
    if k_else is not None:
        *dists, k_all, v_all = dists
        both_chips(chip[0], k_ref, k_else, k_all)
        both_chips(chip[0], v_ref, v_else, v_all)
        k_ref, v_ref = k_all, v_all

    @pl.when(step == 0)
    def _():
        for dist, block in zip(dists, blocks):
            fill_distance(dist, block, seg_ref, tag_ref)

    lane = lax.broadcasted_iota(jnp.int32, (QB, 2 * HD), 1)
    scale = 1.0 / math.sqrt(HD)
    if start_ref is None:
        dkv_ref[...] = jnp.zeros_like(dkv_ref)
    else:
        count = dkv_ref.shape[1]
        dkv_ref[...] = start_ref[:, rows_at(pl.multiple_of(chip[0] * HALF, HALF), count), :]
    for dist, (q_at, k_at, span, shift) in zip(dists, blocks):
        q = q_ref[rows_at(q_at, QB), :] * jnp.asarray(scale, jnp.bfloat16)
        do = jnp.where(chip[1] == 1, do_ref[rows_at(q_at, QB), :], do_else_ref[rows_at(q_at, QB), :])
        k = k_ref[rows_at(k_at, span), :]
        v = v_ref[rows_at(k_at, span), :]
        k_t = k.T
        mixed_t = (do.astype(jnp.float32) * o_ref[rows_at(q_at, QB), :].astype(jnp.float32)).T
        parts = []
        ps = []
        dss = []
        qs = []
        dos = []
        for a in range(2):
            mine = (lane >= HD) if a else (lane < HD)
            q_a = jnp.where(mine, q, jnp.zeros_like(q))
            do_a = jnp.where(mine, do, jnp.zeros_like(do))
            delta = jnp.sum(mixed_t[a * HD : (a + 1) * HD, :], axis=0, keepdims=True)
            s = dot_nt(k, q_a) - slopes[2 * pair + a] * dist[...]
            p = jnp.exp(s - lse_ref[0, a : a + 1, rows_at(q_at, QB)])
            dp = dot_nt(v, do_a)
            ds = (p * (dp - delta)).astype(jnp.bfloat16)
            parts.append(dot_nn(k_t[a * HD : (a + 1) * HD, :], ds) * scale)
            ps.append(p.astype(jnp.bfloat16))
            dss.append(ds)
            qs.append(q_a)
            dos.append(do_a)
        dq_ref[rows_at(q_at, QB), :] = jnp.concatenate(parts, axis=0).T.astype(jnp.bfloat16)
        dkv_ref[0, rows_at(k_at, span), :] += dot_nn(
            jnp.concatenate(dss, axis=1), jnp.concatenate(qs, axis=0)
        )
        dkv_ref[1, rows_at(k_at, span), :] += dot_nn(
            jnp.concatenate(ps, axis=1), jnp.concatenate(dos, axis=0)
        )
    if beyond_ref is not None:
        other = pl.multiple_of((1 - chip[0]) * 2 * HALF, HALF)
        beyond_ref[...] = dkv_ref[:, rows_at(other, HALF), :].astype(jnp.bfloat16)


def attention_backward(
    plan, chip, queries, keys_values, attended, grad_if, grad_else, lse, seg_row, tag_col, slopes, start,
    low=0, count=None, into=(), beyond=None,
):
    rows, width = queries.shape
    ext = tag_col.shape[0]
    own = keys_values.shape[0]
    more = () if beyond is None else (beyond, beyond)
    pairs = width // (2 * HD)
    count = pairs if count is None else count
    inner = pl.BlockSpec((rows, 2 * HD), lambda h: (0, low + h))
    starts = () if start is None else (start,)

    def body(*refs):
        refs = list(refs)
        fixed, refs = refs[:11], refs[11:]
        begin = refs.pop(0) if starts else None
        others = [refs.pop(0) for _ in more] or [None, None]
        refs = refs[len(into) :]
        outs, refs = refs[: 3 - len(starts)], refs[3 - len(starts) :]
        outs += [None] * len(starts)
        attn_bwd_kernel(plan, low, *fixed, begin, *others, *outs, *refs)

    return pl.pallas_call(
        body,
        grid=(count,),
        in_specs=[
            pl.BlockSpec(memory_space=pltpu.SMEM),
            pl.BlockSpec(memory_space=pltpu.SMEM),
            inner,
            pl.BlockSpec((own, 2 * HD), lambda h: (0, low + h)),
            pl.BlockSpec((own, 2 * HD), lambda h: (0, pairs + low + h)),
            inner,
            inner,
            inner,
            pl.BlockSpec((1, 8, rows), lambda h: (low + h, 0, 0)),
            pl.BlockSpec((1, rows), lambda h: (0, 0)),
            pl.BlockSpec((ext, 1), lambda h: (0, 0)),
        ]
        + [pl.BlockSpec((2, s.shape[1], 2 * HD), lambda h: (0, 0, low + h)) for s in starts]
        + [
            pl.BlockSpec((ext - own, 2 * HD), lambda h, t=t: (0, t * pairs + low + h))
            for t in range(len(more))
        ]
        + [pl.BlockSpec(memory_space=pl.ANY)] * len(into),
        out_specs=[inner, pl.BlockSpec((2, ext, 2 * HD), lambda h: (0, 0, low + h))]
        + [pl.BlockSpec((2, HALF, 2 * HD), lambda h: (0, 0, low + h))] * (1 - len(starts)),
        out_shape=[
            jax.ShapeDtypeStruct((rows, width), jnp.bfloat16),
            jax.ShapeDtypeStruct((2, ext, width), jnp.float32),
        ]
        + [jax.ShapeDtypeStruct((2, HALF, width), jnp.bfloat16)] * (1 - len(starts)),
        input_output_aliases={11 + len(starts) + len(more) + i: i for i in range(len(into))},
        scratch_shapes=distances(plan) + [pltpu.VMEM((ext, 2 * HD), jnp.bfloat16)] * len(more),
        compiler_params=pltpu.CompilerParams(vmem_limit_bytes=56 * MIB),
        cost_estimate=SHORT,
    )(
        chip, slopes, queries, keys_values, keys_values, attended, grad_if, grad_else, lse,
        seg_row, tag_col, *starts, *more, *into,
    )


def norm_parts(values, gain_vec, offset):
    centred = values - jnp.mean(values, axis=-1, keepdims=True)
    variance = jnp.mean(centred * centred, axis=-1, keepdims=True)
    inverse = lax.rsqrt(variance + EPSILON)
    normed = centred * inverse
    return (normed * gain_vec + offset, normed, inverse)


def project_kernel(
    place_numbers, spot, x_ref, *refs
):
    pieces = refs[:8]
    vec_ref, w_ref, out_ref, local_ref, reach_ref, kv_ref, send_ref, weight = refs[8:]
    core, chip = spot[0], spot[1]
    fill_weight(place_numbers, pieces, weight)
    half = out_ref.shape[1]
    rows = local_ref.shape[0]
    w_ref[...] = weight[:, : 3 * half]
    out_ref[...] = weight[:, 3 * half : 4 * half]
    vec = weight[:, 4 * half :].astype(jnp.float32).T[:VECTORS, :]
    vec_ref[...] = vec
    projected = dot_nn(x_ref[...], weight[:, : 3 * half])

    def bias(i):
        return jnp.where(core == 0, vec[i : i + 1, :half], vec[i : i + 1, half:])

    queries = (projected[:, :half] + bias(0)).astype(jnp.bfloat16)
    first = chip == 0
    local_ref[...] = jnp.where(first, queries[:rows], queries[rows:])
    reach_ref[...] = jnp.where(first, queries[rows:], queries[:rows])
    keys = projected[:, half : 2 * half].astype(jnp.bfloat16)
    values = (projected[:, 2 * half :] + bias(1)).astype(jnp.bfloat16)
    kv_ref[:, :half] = keys
    kv_ref[:, half:] = values
    send_ref[:, :half] = jnp.where(first, keys[rows:], keys[:rows])
    send_ref[:, half:] = jnp.where(first, values[rows:], values[:rows])


def project(numbers, spot, x, pieces):
    all_rows, width = x.shape
    half = width // 2
    rows = all_rows // 2
    whole = pl.BlockSpec(memory_space=pltpu.VMEM)
    smem = pl.BlockSpec(memory_space=pltpu.SMEM)
    low = jnp.bfloat16
    return pl.pallas_call(
        project_kernel,
        in_specs=[smem, smem] + [whole] * 9,
        out_specs=[whole] * 7,
        out_shape=[
            jax.ShapeDtypeStruct((VECTORS, width), jnp.float32),
            jax.ShapeDtypeStruct((width, 3 * half), low),
            jax.ShapeDtypeStruct((width, half), low),
            jax.ShapeDtypeStruct((rows, half), low),
            jax.ShapeDtypeStruct((rows, half), low),
            jax.ShapeDtypeStruct((all_rows, width), low),
            jax.ShapeDtypeStruct((rows, width), low),
        ],
        scratch_shapes=[pltpu.VMEM((width, pieces[0].shape[1]), low)],
        compiler_params=pltpu.CompilerParams(vmem_limit_bytes=56 * MIB),
        cost_estimate=SHORT,
    )(numbers, spot, x, *pieces)


def first_norm_kernel(
    core, vec_ref, attended_ref, mine_ref, other_ref, x_ref,
    norm_ref, normed_ref, inverse_ref, low_ref, w_ref,
):
    half = mine_ref.shape[1]
    rows = norm_ref.shape[0]
    first = core[0] == 0

    @pl.when(pl.program_id(0) == 0)
    def _():
        w_ref[:, :half] = jnp.where(first, mine_ref[...], other_ref[...])
        w_ref[:, half:] = jnp.where(first, other_ref[...], mine_ref[...])

    at = pl.multiple_of(core[0] * rows * pl.num_programs(0) + pl.program_id(0) * rows, rows)
    branch = dot_nn(attended_ref[pl.ds(at, rows), :], w_ref[...]) + vec_ref[2:3, :]
    norm, normed, inverse = norm_parts(
        x_ref[...].astype(jnp.float32) + branch, vec_ref[4:5, :], vec_ref[5:6, :]
    )
    norm_ref[...] = norm
    normed_ref[...] = normed
    inverse_ref[...] = inverse
    low_ref[...] = norm.astype(jnp.bfloat16)


def first_norm_of(core, vec, attended, mine, other, x):
    rows, width = x.shape
    steps = 2
    block = pl.BlockSpec((rows // steps, width), lambda i: (i, 0))

    def all_of(a):
        return pl.BlockSpec(a.shape, lambda i: (0, 0))

    return pl.pallas_call(
        first_norm_kernel,
        grid=(steps,),
        in_specs=[pl.BlockSpec(memory_space=pltpu.SMEM)]
        + [all_of(a) for a in (vec, attended, mine, other)]
        + [block],
        out_specs=[
            block, block, pl.BlockSpec((rows // steps, 1), lambda i: (i, 0)), block,
            pl.BlockSpec((width, width), lambda i: (0, 0)),
        ],
        out_shape=[
            jax.ShapeDtypeStruct((rows, width), jnp.float32),
            jax.ShapeDtypeStruct((rows, width), jnp.float32),
            jax.ShapeDtypeStruct((rows, 1), jnp.float32),
            jax.ShapeDtypeStruct((rows, width), jnp.bfloat16),
            jax.ShapeDtypeStruct((width, width), jnp.bfloat16),
        ],
        compiler_params=pltpu.CompilerParams(vmem_limit_bytes=56 * MIB),
        cost_estimate=SHORT,
    )(core, vec, attended, mine, other, x)


def norm_back(upstream, normed, inverse, gain_vec):
    scaled = upstream * gain_vec
    row_inner = (
        scaled
        - jnp.mean(scaled, axis=-1, keepdims=True)
        - normed * jnp.mean(scaled * normed, axis=-1, keepdims=True)
    )
    return row_inner * inverse


def last_grads_kernel(
    numbers, spot, x_ref, local_ref, reach_ref, dkv_ref, beyond_ref, out_w_ref, attn_ref, ffn_ref, *refs
):
    *pieces, grad_ref, last_ref = refs
    core, chip = spot[0], spot[1]
    first = chip == 0
    rows, half = local_ref.shape
    grad_ref[:rows, :half] = jnp.where(first, local_ref[...], reach_ref[...])
    grad_ref[rows:, :half] = jnp.where(first, reach_ref[...], local_ref[...])
    for t in range(2):
        got = beyond_ref[t].astype(jnp.float32)
        part = slice((t + 1) * half, (t + 2) * half)
        top = dkv_ref[t, :rows, :] + jnp.where(first, 0.0, got)
        low = dkv_ref[t, rows:, :] + jnp.where(first, got, 0.0)
        grad_ref[:rows, part] = top.astype(jnp.bfloat16)
        grad_ref[rows:, part] = low.astype(jnp.bfloat16)
    grads = grad_ref[...]
    last_ref[:, : 3 * half] = dot_tn(x_ref[...], grads).astype(jnp.bfloat16)
    last_ref[:, 3 * half : 4 * half] = out_w_ref[...]
    sums = [
        jnp.sum(grads[:, i * half : (i + 1) * half].astype(jnp.float32), axis=0, keepdims=True)
        for i in (0, 2)
    ]
    nothing = jnp.zeros_like(sums[0])
    vectors = [
        jnp.where(
            core == 0, jnp.concatenate([s, nothing], axis=1), jnp.concatenate([nothing, s], axis=1)
        )
        for s in sums
    ]
    vectors += [attn_ref[2:3, :], ffn_ref[2:3, :], attn_ref[0:2, :], ffn_ref[0:2, :]]
    vectors.append(jnp.zeros((128 - VECTORS, 2 * half), jnp.float32))
    last_ref[:, 4 * half :] = jnp.concatenate(vectors, axis=0).T.astype(jnp.bfloat16)
    for i, piece in enumerate(pieces):
        piece[0] = last_ref[shard_rows(numbers, i, piece), :]


def last_grads(numbers, spot, x, dq_local, dq_reach, dkv, beyond, grad_w_out, attn_sums, ffn_sums):
    all_rows, width = x.shape
    half = width // 2
    whole = pl.BlockSpec(memory_space=pltpu.VMEM)
    return pl.pallas_call(
        last_grads_kernel,
        in_specs=[pl.BlockSpec(memory_space=pltpu.SMEM)] * 2 + [whole] * 8,
        out_specs=[whole] * 9,
        out_shape=[jax.ShapeDtypeStruct((1, width // 8, 4 * half + 128), jnp.bfloat16)] * 8
        + [jax.ShapeDtypeStruct((all_rows, 3 * half), jnp.bfloat16)],
        scratch_shapes=[pltpu.VMEM((width, 4 * half + 128), jnp.bfloat16)],
        compiler_params=pltpu.CompilerParams(vmem_limit_bytes=30 * MIB),
        cost_estimate=SHORT,
    )(numbers, spot, x, dq_local, dq_reach, dkv, beyond, grad_w_out, attn_sums, ffn_sums)


def finish_kernel(core, mine_ref, other_ref, *outs):
    first = core[0] == 0
    half = outs[0].shape[1] // 2
    for i, out in enumerate(outs[:4]):
        part = slice(i * half, (i + 1) * half)
        mine, other = mine_ref[:, part].astype(jnp.float32), other_ref[:, part].astype(jnp.float32)
        out[:, :half] = jnp.where(first, mine, other)
        out[:, half:] = jnp.where(first, other, mine)
    mine, other = mine_ref[:, 4 * half :], other_ref[:, 4 * half :]
    vectors = (mine.astype(jnp.float32) + other.astype(jnp.float32)).T
    for i, out in enumerate(outs[4:]):
        out[...] = vectors[i : i + 1, :]


def finish(core, mine, other):
    rows, columns = mine.shape
    width = (columns - 128) // 2
    whole = pl.BlockSpec(memory_space=pltpu.VMEM)
    results = pl.pallas_call(
        finish_kernel,
        in_specs=[pl.BlockSpec(memory_space=pltpu.SMEM)] + [whole] * 2,
        out_specs=[whole] * (4 + VECTORS),
        out_shape=[jax.ShapeDtypeStruct((rows, width), jnp.float32)] * 4
        + [jax.ShapeDtypeStruct((1, rows), jnp.float32)] * VECTORS,
        cost_estimate=SHORT,
    )(core, mine, other)
    return results[:4], results[4:]


def add_sums(step, sums_ref, *columns):
    rows = [jnp.sum(value, axis=0, keepdims=True) for value in columns]
    rows.append(jnp.zeros((8 - len(rows), sums_ref.shape[1]), jnp.float32))
    add_up(step, sums_ref, jnp.concatenate(rows, axis=0))


def second_norm_kernel(
    vec_ref, norm_ref, part_ref, sent_ref, cot_ref, out_ref, grad_ref, low_ref, sums_ref
):
    step = pl.program_id(0)
    bias, gain, shift = vec_ref[3:4, :], vec_ref[6:7, :], vec_ref[7:8, :]
    value = norm_ref[...] + part_ref[...] + sent_ref[...].astype(jnp.float32) + bias
    result, normed, inverse = norm_parts(value, gain, shift)
    out_ref[...] = result.astype(jnp.bfloat16)
    upstream = cot_ref[...].astype(jnp.float32)
    grad = norm_back(upstream, normed, inverse, gain)
    grad_ref[...] = grad
    low_ref[...] = grad.astype(jnp.bfloat16)
    add_sums(step, sums_ref, upstream * normed, upstream, grad)


def second_norm(vec, first_norm, part, sent, cotangent):
    rows, width = part.shape
    block = pl.BlockSpec((rows // 2, width), lambda i: (i, 0))
    eight = pl.BlockSpec((8, width), lambda i: (0, 0))
    return pl.pallas_call(
        second_norm_kernel,
        grid=(2,),
        in_specs=[eight] + [block] * 4,
        out_specs=[block] * 3 + [eight],
        out_shape=[
            jax.ShapeDtypeStruct((rows, width), jnp.bfloat16),
            jax.ShapeDtypeStruct((rows, width), jnp.float32),
            jax.ShapeDtypeStruct((rows, width), jnp.bfloat16),
            jax.ShapeDtypeStruct((8, width), jnp.float32),
        ],
        compiler_params=pltpu.CompilerParams(vmem_limit_bytes=14 * MIB),
        cost_estimate=SHORT,
    )(vec, first_norm, part, sent, cotangent)


def first_norm_back_kernel(
    core, vec_ref, w_ref, up_ref, part_ref, sent_ref, normed_ref, inverse_ref,
    grad_ref, low_mine, low_theirs, back_mine, back_theirs, sums_ref,
):
    step = pl.program_id(0)
    half = low_mine.shape[1]
    upstream = up_ref[...] + part_ref[...] + sent_ref[...].astype(jnp.float32)
    normed = normed_ref[...]
    grad = norm_back(upstream, normed, inverse_ref[...], vec_ref[4:5, :])
    grad_ref[...] = grad
    low = grad.astype(jnp.bfloat16)
    back = dot_nt(low, w_ref[...]).astype(jnp.bfloat16)
    first = core[0] == 0
    for value, mine, theirs in ((low, low_mine, low_theirs), (back, back_mine, back_theirs)):
        left, right = value[:, :half], value[:, half:]
        mine[...] = jnp.where(first, left, right)
        theirs[...] = jnp.where(first, right, left)
    add_sums(step, sums_ref, upstream * normed, upstream, grad)


def first_norm_back(core, vec, w_out, grad_second, part, sent, normed, inverse):
    rows, width = part.shape
    steps = 2
    block = pl.BlockSpec((rows // steps, width), lambda i: (i, 0))
    halves = pl.BlockSpec((rows // steps, width // 2), lambda i: (i, 0))
    eight = pl.BlockSpec((8, width), lambda i: (0, 0))
    return pl.pallas_call(
        first_norm_back_kernel,
        grid=(steps,),
        in_specs=[
            pl.BlockSpec(memory_space=pltpu.SMEM),
            eight,
            pl.BlockSpec((width, width), lambda i: (0, 0)),
        ]
        + [block] * 4
        + [pl.BlockSpec((rows // steps, 1), lambda i: (i, 0))],
        out_specs=[block] + [halves] * 4 + [eight],
        out_shape=[jax.ShapeDtypeStruct((rows, width), jnp.float32)]
        + [jax.ShapeDtypeStruct((rows, width // 2), jnp.bfloat16)] * 4
        + [jax.ShapeDtypeStruct((8, width), jnp.float32)],
        compiler_params=pltpu.CompilerParams(vmem_limit_bytes=18 * MIB),
        cost_estimate=SHORT,
    )(core, vec, w_out, grad_second, part, sent, normed, inverse)


def lay_out_kernel(core, mine_ref, other_ref, up_ref, gate_ref, down_ref):
    first = core[0] == 0
    count, shard_rows, width = mine_ref.shape
    groups = count // 3
    shards = width // shard_rows

    def both(i):
        mine, other = mine_ref[i].astype(jnp.float32), other_ref[i].astype(jnp.float32)
        return jnp.where(first, mine, other), jnp.where(first, other, mine)

    for g in range(groups):
        for c, value in enumerate(both(2 * groups + g)):
            at = (c * groups + g) * shard_rows
            down_ref[at : at + shard_rows, :] = value
        for t, out in ((0, up_ref), (1, gate_ref)):
            for c, value in enumerate(both(2 * g + t)):
                for s in range(shards):
                    at = ((s * 2 + c) * groups + g) * shard_rows
                    out[:, at : at + shard_rows] = value[:, s * shard_rows : (s + 1) * shard_rows]


def lay_out(core, mine, other):
    count, shard_rows, width = mine.shape
    columns = count // 3 * 2 * width
    whole = pl.BlockSpec(memory_space=pltpu.VMEM)
    return pl.pallas_call(
        lay_out_kernel,
        in_specs=[pl.BlockSpec(memory_space=pltpu.SMEM)] + [whole] * 2,
        out_specs=[whole] * 3,
        out_shape=[
            jax.ShapeDtypeStruct((shard_rows, columns), jnp.float32),
            jax.ShapeDtypeStruct((shard_rows, columns), jnp.float32),
            jax.ShapeDtypeStruct((count // 3 * 2 * shard_rows, width), jnp.float32),
        ],
        compiler_params=pltpu.CompilerParams(vmem_limit_bytes=14 * MIB),
        cost_estimate=SHORT,
    )(core, mine, other)


def phi_parts(v):
    cdf = 0.5 * (1.0 + lax.erf(v * math.sqrt(0.5)))
    density = jnp.exp(-0.5 * v * v) * (1.0 / math.sqrt(2.0 * math.pi))
    return cdf, cdf + v * density


def shard_rows(numbers, i, piece):
    rows = piece.shape[-2]
    return pl.ds(pl.multiple_of(numbers[i] * rows, rows), rows)


def fill_weight(numbers, pieces, weight):
    for i, piece in enumerate(pieces):
        weight[shard_rows(numbers, i, piece), :] = piece[...]


def add_up(step, total, out):
    @pl.when(step == 0)
    def _():
        total[...] = out

    @pl.when(step > 0)
    def _():
        total[...] += out


def ffn_fwd_kernel(numbers, own_ref, other_ref, *refs):
    ups, gates, downs = refs[:8], refs[8:16], refs[16:24]
    hid_ref, act_ref, slope_ref, part_ref, send_ref = refs[24:29]
    x_all, up_w, gate_w, down_w, total = refs[29:]
    step = pl.program_id(0)
    rows = own_ref.shape[0]

    @pl.when(step == 0)
    def _():
        x_all[:rows, :] = own_ref[...]
        x_all[rows:, :] = other_ref[...]

    fill_weight(numbers, ups, up_w)
    fill_weight(numbers, gates, gate_w)
    fill_weight(numbers, downs, down_w)
    columns = up_w.shape[1]
    piece = columns // 3
    for i in range(3):
        part = slice(i * piece, (i + 1) * piece)
        x = x_all[...]
        up = dot_nn(x, up_w[:, part])
        gate = dot_nn(x, gate_w[:, part])
        cdf, derivative = phi_parts(gate)
        act = gate * cdf
        hidden = (act * up).astype(jnp.bfloat16)
        hid_ref[:, part] = hidden
        act_ref[:, part] = act.astype(jnp.bfloat16)
        slope_ref[:, part] = (derivative * up).astype(jnp.bfloat16)
    add_up(step, total, dot_nn(hid_ref[...], down_w[...]))

    @pl.when(step == pl.num_programs(0) - 1)
    def _():
        part_ref[...] = total[:rows, :]
        send_ref[...] = total[rows:, :].astype(jnp.bfloat16)


def piece_specs(rows, width, columns):
    steps = columns // width
    return [
        pl.BlockSpec((rows, width), lambda f, t=t: (0, t * steps + f))
        for t in range(3)
        for i in range(8)
    ]


def ffn_forward(own, other, pieces, numbers, columns):
    rows, width = own.shape
    steps = columns // width
    wide = pl.BlockSpec((2 * rows, width), lambda f: (0, f))
    whole = pl.BlockSpec((rows, width), lambda f: (0, 0))
    return pl.pallas_call(
        ffn_fwd_kernel,
        grid=(steps,),
        in_specs=[pl.BlockSpec(memory_space=pltpu.SMEM), whole, whole]
        + piece_specs(pieces[0].shape[0], width, columns),
        out_specs=[wide, wide, wide, whole, whole],
        out_shape=[jax.ShapeDtypeStruct((2 * rows, columns), jnp.bfloat16)] * 3
        + [
            jax.ShapeDtypeStruct((rows, width), jnp.float32),
            jax.ShapeDtypeStruct((rows, width), jnp.bfloat16),
        ],
        scratch_shapes=[
            pltpu.VMEM((2 * rows, width), jnp.bfloat16),
            pltpu.VMEM((width, width), jnp.bfloat16),
            pltpu.VMEM((width, width), jnp.bfloat16),
            pltpu.VMEM((width, width), jnp.bfloat16),
            pltpu.VMEM((2 * rows, width), jnp.float32),
        ],
        compiler_params=pltpu.CompilerParams(vmem_limit_bytes=56 * MIB),
        cost_estimate=SHORT,
    )(numbers, own, other, *(pieces * 3))


def down_grad_kernel(group, branch_ref, branch_other_ref, hid_ref, grad_ref):
    rows = branch_ref.shape[0]
    total = dot_tn(hid_ref[:rows, :], branch_ref[...])
    grad_ref[...] = (total + dot_tn(hid_ref[rows:, :], branch_other_ref[...])).astype(jnp.bfloat16)


def down_grad(group, branch, branch_other, hidden):
    rows, width = branch.shape
    whole = pl.BlockSpec((rows, width), lambda i, group: (0, 0))
    return pl.pallas_call(
        down_grad_kernel,
        grid_spec=pltpu.PrefetchScalarGridSpec(
            num_scalar_prefetch=1,
            grid=(1,),
            in_specs=[
                whole, whole, pl.BlockSpec((2 * rows, width), lambda i, group: (0, group[0])),
            ],
            out_specs=pl.BlockSpec((width, width), lambda i, group: (0, 0)),
        ),
        out_shape=jax.ShapeDtypeStruct((width, width), jnp.bfloat16),
        compiler_params=pltpu.CompilerParams(vmem_limit_bytes=18 * MIB),
        cost_estimate=SHORT,
    )(group, branch, branch_other, hidden)


def add_last_kernel(numbers, *refs):
    keep_ref, got_ref = refs[8:10]
    for i, out_ref in enumerate(refs[10:]):
        shard = shard_rows(numbers, i, out_ref)
        out_ref[0] = keep_ref[shard, :] + got_ref[shard, :]


def add_last(numbers, pieces, keep, got):
    units, rows, width = pieces[0].shape
    whole = pl.BlockSpec(memory_space=pltpu.VMEM)
    return pl.pallas_call(
        add_last_kernel,
        grid=(1,),
        in_specs=[pl.BlockSpec(memory_space=pltpu.SMEM)]
        + [pl.BlockSpec(memory_space=pl.ANY)] * 8
        + [whole, whole],
        out_specs=[pl.BlockSpec((1, rows, width), lambda i: (units - 1, 0, 0))] * 8,
        out_shape=[jax.ShapeDtypeStruct(pieces[0].shape, pieces[0].dtype)] * 8,
        input_output_aliases={1 + i: i for i in range(8)},
        compiler_params=pltpu.CompilerParams(vmem_limit_bytes=56 * MIB),
        cost_estimate=SHORT,
    )(numbers, *pieces, keep, got)


def ffn_bwd_kernel(numbers, own_ref, other_ref, branch_ref, branch_other_ref, act_ref, slope_ref, *refs):
    ups, gates, downs = refs[:8], refs[8:16], refs[16:24]
    grad_refs, part_ref, send_ref = refs[24:32], refs[32], refs[33]
    x_all, branch_all, up_w, gate_w, down_w, total, up_grad, gate_grad = refs[34:]
    step = pl.program_id(0)
    rows = own_ref.shape[0]

    @pl.when(step == 0)
    def _():
        x_all[:rows, :] = own_ref[...]
        x_all[rows:, :] = other_ref[...]
        branch_all[:rows, :] = branch_ref[...]
        branch_all[rows:, :] = branch_other_ref[...]

    fill_weight(numbers, ups, up_w)
    fill_weight(numbers, gates, gate_w)
    fill_weight(numbers, downs, down_w)
    x = x_all[...]
    outs = []
    piece = up_w.shape[1] // 3
    for i in range(3):
        part = slice(i * piece, (i + 1) * piece)
        d_hidden = dot_nt(branch_all[...], down_w[part, :])
        d_up = (d_hidden * act_ref[:, part].astype(jnp.float32)).astype(jnp.bfloat16)
        d_gate = (d_hidden * slope_ref[:, part].astype(jnp.float32)).astype(jnp.bfloat16)
        outs.append(dot_nt(d_up, up_w[:, part]) + dot_nt(d_gate, gate_w[:, part]))
        up_grad[:, part] = dot_tn(x, d_up).astype(jnp.bfloat16)
        gate_grad[:, part] = dot_tn(x, d_gate).astype(jnp.bfloat16)
    for i, grad_ref in enumerate(grad_refs):
        shard = shard_rows(numbers, i, grad_ref)
        grad_ref[0] = up_grad[shard, :]
        grad_ref[1] = gate_grad[shard, :]
    add_up(step, total, outs[0] + outs[1] + outs[2])

    @pl.when(step == pl.num_programs(0) - 1)
    def _():
        part_ref[...] = total[:rows, :]
        send_ref[...] = total[rows:, :].astype(jnp.bfloat16)


def ffn_backward(own, other, branch, branch_other, act, slope, pieces, numbers, columns):
    rows, width = own.shape
    steps = columns // width
    wide = pl.BlockSpec((2 * rows, width), lambda f: (0, f))
    whole = pl.BlockSpec((rows, width), lambda f: (0, 0))
    return pl.pallas_call(
        ffn_bwd_kernel,
        grid=(steps,),
        in_specs=[pl.BlockSpec(memory_space=pltpu.SMEM)]
        + [whole] * 4
        + [wide] * 2
        + piece_specs(pieces[0].shape[0], width, columns),
        out_specs=[
            *[pl.BlockSpec((2, width // 8, width), lambda f: (f, 0, 0))] * 8,
            whole,
            whole,
        ],
        out_shape=[
            *[jax.ShapeDtypeStruct((2 * steps + 1, width // 8, width), jnp.bfloat16)] * 8,
            jax.ShapeDtypeStruct((rows, width), jnp.float32),
            jax.ShapeDtypeStruct((rows, width), jnp.bfloat16),
        ],
        scratch_shapes=[
            pltpu.VMEM((2 * rows, width), jnp.bfloat16),
            pltpu.VMEM((2 * rows, width), jnp.bfloat16),
            pltpu.VMEM((width, width), jnp.bfloat16),
            pltpu.VMEM((width, width), jnp.bfloat16),
            pltpu.VMEM((width, width), jnp.bfloat16),
            pltpu.VMEM((2 * rows, width), jnp.float32),
            pltpu.VMEM((width, width), jnp.bfloat16),
            pltpu.VMEM((width, width), jnp.bfloat16),
        ],
        compiler_params=pltpu.CompilerParams(vmem_limit_bytes=56 * MIB),
        cost_estimate=SHORT,
    )(numbers, own, other, branch, branch_other, act, slope, *(pieces * 3))


def pack_kernel(core, up_ref, gate_ref, down_ref, out_ref):
    first = core[0] == 0
    shard_rows = up_ref.shape[0]
    width = down_ref.shape[1]
    shards = width // shard_rows
    groups = down_ref.shape[0] // shard_rows // 2
    at = 0
    for ref in (up_ref, gate_ref):
        for g in range(groups):
            for s in range(shards):
                left = (s * 2 * groups + g) * shard_rows
                right = left + groups * shard_rows
                out_ref[:, at : at + shard_rows] = jnp.where(
                    first, ref[:, left : left + shard_rows], ref[:, right : right + shard_rows]
                )
                at += shard_rows
    for g in range(groups):
        top = g * shard_rows
        low = top + groups * shard_rows
        out_ref[:, at : at + width] = jnp.where(
            first, down_ref[top : top + shard_rows, :], down_ref[low : low + shard_rows, :]
        )
        at += width


def pack(core, up, gate, down):
    shard_rows = up.shape[0]
    width = down.shape[1]
    whole = pl.BlockSpec(memory_space=pltpu.VMEM)
    return pl.pallas_call(
        pack_kernel,
        in_specs=[pl.BlockSpec(memory_space=pltpu.SMEM)] + [whole] * 3,
        out_specs=whole,
        out_shape=jax.ShapeDtypeStruct(
            (shard_rows, up.shape[1] + down.shape[0] // shard_rows // 2 * width), jnp.bfloat16
        ),
        compiler_params=pltpu.CompilerParams(vmem_limit_bytes=56 * MIB),
        cost_estimate=SHORT,
    )(core, up, gate, down)


def pack_first_kernel(core, *refs):
    first = core[0] == 0
    half = refs[0].shape[1] // 2
    out_ref = refs[-1]
    for i, ref in enumerate(refs[:4]):
        out_ref[:, i * half : (i + 1) * half] = jnp.where(first, ref[:, :half], ref[:, half:])
    out_ref[:, 4 * half :] = refs[4][...]


def pack_first(core, matrices, vectors):
    rows, width = matrices[0].shape
    whole = pl.BlockSpec(memory_space=pltpu.VMEM)
    return pl.pallas_call(
        pack_first_kernel,
        in_specs=[pl.BlockSpec(memory_space=pltpu.SMEM)] + [whole] * 5,
        out_specs=whole,
        out_shape=jax.ShapeDtypeStruct((rows, 2 * width + vectors.shape[1]), jnp.bfloat16),
        cost_estimate=SHORT,
    )(core, *matrices, vectors)


def on_device(
    tokens, segments, padding,
    w_query, w_key, w_value, w_out, w_up, w_gate, w_down,
    bias_query, bias_value, bias_out, bias_down, gain_attn, shift_attn, gain_ffn, shift_ffn,
    cotangent,
):
    tuned = lax.axis_size("ctx") == 4 and lax.axis_size("fsdp") == 8
    row_gather, row_reduce = (Gather, Reduce) if tuned else (PlainGather, PlainReduce)
    core = lax.axis_index("ctx") % 2
    chip = lax.axis_index("ctx") // 2
    chip_ref = chip[None].astype(jnp.int32)
    core_ref = core[None].astype(jnp.int32)
    inputs = tokens[0]
    rows, width = inputs.shape
    half = width // 2
    half_ff = FF // 2

    def cut(value, which, count, axis):
        return lax.dynamic_slice_in_dim(value, which * count, count, axis)

    def share(mine, theirs, axis):
        return ordered(core, mine, over_core(theirs), axis)

    vectors = jnp.stack(
        (bias_query, bias_value, bias_out, bias_down, gain_attn, shift_attn, gain_ffn, shift_ffn), axis=1
    )
    vectors = jnp.pad(vectors, ((0, 0), (0, 128 - VECTORS)))
    first = row_gather(pack_first(core_ref, (w_query, w_key, w_value, w_out), vectors))
    second = row_gather(pack(core_ref, w_up, w_gate, w_down))
    first.first()

    own_numbers = jnp.stack((segments[0], jnp.where(padding[0] == 1, -1, segments[0])))
    numbers = share(own_numbers, own_numbers, 1)
    slopes = cut(head_slopes(H), core, H // 2, 0)
    (numbers,) = first.join(numbers)
    tags = numbers[1]
    seg_row = numbers[0][None, :]
    if tuned:
        tags_send = jnp.where(chip == 0, tags[rows:], tags[:rows]) + 2
        first.second()
        beyond = over_x(tags_send)
        beyond, second.own = first.join(beyond, second.own)
        beyond = beyond - 2
        tags_reach = ordered(chip, tags, beyond, 0)[:, None]
        tags_local = tags[:, None]
        seg_local = cut(seg_row, chip, rows, 1)
        seg_reach = cut(seg_row, 1 - chip, rows, 1)
    else:
        tag_low = from_previous_chip(tags[rows:] + 2) - 2
        tag_high = from_next_chip(tags[:rows] + 2) - 2
        tags_wide = jnp.concatenate([tag_low, tags, tag_high])[:, None]
    first.third()
    inputs_all = share(inputs, inputs, 0)
    (inputs_all,) = first.join(inputs_all)
    (second.own,) = first.fourth(second.own)
    second.first_z()
    (second.own,) = first.join(second.own)
    second.first_y()

    spot = jnp.stack((core, chip if tuned else jnp.zeros_like(chip))).astype(jnp.int32)
    vec, full_qkv, out_half, queries_local, queries_reach, keys_values, beyond = project(
        first.numbers(), spot, inputs_all, first.pieces()
    )
    out_other = over_core(out_half)
    if tuned:
        queries_local, queries_reach, keys_values, beyond = second.join(
            queries_local, queries_reach, keys_values, beyond
        )
        beyond = over_x(beyond)
        second.second()
        attended_local, lse_local = attention_forward(
            local_blocks, chip_ref, queries_local, keys_values, seg_local, tags_local, slopes
        )
        attended_local, lse_local, beyond = second.join(attended_local, lse_local, beyond)
        keys_values, kv_beyond = second.third(keys_values, beyond)
        attended_reach, lse_reach = attention_forward(
            reach_blocks, chip_ref, queries_reach, keys_values, seg_reach, tags_reach, slopes, kv_beyond
        )
        attended_own = ordered(chip, attended_local, attended_reach, 0)
        (attended_own,) = second.join(attended_own)
        (attended_own,) = second.fourth(attended_own)
    else:
        queries = jnp.concatenate([queries_local, queries_reach], axis=0)
        kv_low = from_previous_chip(keys_values[rows:])
        kv_high = from_next_chip(keys_values[:rows])
        kv_wide = jnp.concatenate([kv_low, keys_values, kv_high], axis=0)
        spans = [(i * rows, i * rows + rows + 2 * HALF) for i in range(2)]
        forward_parts = [
            attention_forward(
                reach_blocks, chip_ref, queries[i * rows : (i + 1) * rows], kv_wide[low:high],
                seg_row[:, i * rows : (i + 1) * rows], tags_wide[low:high], slopes,
            )
            for i, (low, high) in enumerate(spans)
        ]
        attended_own = jnp.concatenate([part[0] for part in forward_parts], axis=0)
    attended_all = share(attended_own, attended_own, 1)
    first_norm, first_normed, first_inverse, own_low, full_out = first_norm_of(
        core_ref, vec, attended_all, out_half, out_other, inputs
    )
    other_low = over_core(own_low)
    if tuned:
        own_low, other_low = second.join(own_low, other_low)
    pieces = second.pieces()
    places = second.numbers()
    hidden, act, slope, ffn_part, ffn_send = ffn_forward(own_low, other_low, pieces, places, half_ff)
    layer_out, grad_second, own_branch, ffn_sums = second_norm(
        vec, first_norm, ffn_part, over_core(ffn_send), cotangent[0]
    )
    branch_other = over_core(own_branch)
    group = chip_ref if tuned else jnp.zeros_like(chip_ref)
    down_send = down_grad(1 - group, own_branch, branch_other, hidden)
    if tuned:
        down_send, own_branch, branch_other = tie(down_send, own_branch, branch_other)
        down_got = over_x(down_send)
    down_keep = down_grad(group, own_branch, branch_other, hidden)
    down_keep, own_branch, branch_other = tie(down_keep, own_branch, branch_other)
    *grad_pieces, normed_part, normed_send = ffn_backward(
        own_low, other_low, own_branch, branch_other, act, slope, pieces, places, half_ff
    )
    if tuned:
        normed_send, down_got, *grad_pieces = tie(normed_send, down_got, *grad_pieces)
        grad_pieces = add_last(places, grad_pieces, down_keep, down_got)
    else:
        shard_rows = width // 8
        grad_pieces = [
            jnp.concatenate(
                [piece[:-1], down_keep[None, i * shard_rows : (i + 1) * shard_rows],
                 down_send[None, i * shard_rows : (i + 1) * shard_rows]]
            )
            for i, piece in enumerate(grad_pieces)
        ]
    reduce_ffn = row_reduce(grad_pieces)
    (normed_send,) = reduce_ffn.first(normed_send)
    grad_first, low_mine, low_theirs, back_mine, back_theirs, attn_sums = first_norm_back(
        core_ref, vec, full_out, grad_second, normed_part, over_core(normed_send),
        first_normed, first_inverse,
    )
    back_other = over_core(back_theirs)
    low_other = over_core(low_theirs)

    if tuned:
        back_ref = jnp.stack((chip, core == chip)).astype(jnp.int32)
        def reach_part(low, count, into):
            return attention_backward(
                reach_blocks, back_ref, queries_reach, keys_values, attended_reach, back_other, back_mine,
                lse_reach, seg_reach, tags_reach, slopes, None, low, count, into, kv_beyond,
            )

        low_all = ordered(core, low_mine, low_other, 0)
        pairs = half // (2 * HD)
        reached = reduce_ffn.join(*reach_part(0, 1, ()))
        reached = reduce_ffn.second(*reached)
        dq_reach, dkv_reach, beyond = reach_part(1, pairs - 1, tuple(reached))
        dq_reach, dkv_reach, beyond, low_all = tie(dq_reach, dkv_reach, beyond, low_all)
        beyond = over_x(beyond)
        grad_w_out = dot_tn(attended_all, low_all)
        dq_reach, dkv_reach, grad_w_out = reduce_ffn.join(dq_reach, dkv_reach, grad_w_out)
        dq_reach, dkv_reach, grad_w_out = reduce_ffn.third(dq_reach, dkv_reach, grad_w_out)
        dq_local, dkv_local = attention_backward(
            local_blocks, back_ref, queries_local, keys_values, attended_local,
            back_mine, back_other, lse_local, seg_local, tags_local, slopes, dkv_reach,
        )
        dq_local, dkv_local, beyond = reduce_ffn.join(dq_local, dkv_local, beyond)
        reduce_ffn.fourth()
    else:
        grad_attended = ordered(core, back_mine, back_other, 0)
        back_ref = jnp.ones((2,), jnp.int32)
        backward_parts = [
            attention_backward(
                reach_blocks, back_ref, queries[i * rows : (i + 1) * rows], kv_wide[low:high],
                forward_parts[i][0], grad_attended[i * rows : (i + 1) * rows],
                grad_attended[i * rows : (i + 1) * rows], forward_parts[i][1],
                seg_row[:, i * rows : (i + 1) * rows], tags_wide[low:high], slopes, None,
            )
            for i, (low, high) in enumerate(spans)
        ]
        dq_local, dq_reach = [part[0] for part in backward_parts]
        reach_0, reach_1 = [part[1] for part in backward_parts]
        from_next = from_next_chip(reach_0[:, :HALF].astype(jnp.bfloat16)).astype(jnp.float32)
        from_previous = from_previous_chip(reach_1[:, rows + HALF :].astype(jnp.bfloat16)).astype(jnp.float32)
        centre = jnp.pad(reach_0[:, HALF:], ((0, 0), (0, 2 * rows - reach_0.shape[1] + HALF), (0, 0)))
        centre = centre + jnp.pad(
            reach_1[:, : rows + HALF], ((0, 0), (2 * rows - rows - HALF, 0), (0, 0))
        )
        centre = centre.at[:, 2 * rows - HALF :].add(from_next)
        dkv_local = centre.at[:, :HALF].add(from_previous)
        beyond = jnp.zeros_like(from_next, dtype=jnp.bfloat16)
        grad_w_out = dot_tn(attended_all, ordered(core, low_mine, low_other, 0))
    *grad_last, grad_qkv = last_grads(
        places, spot, inputs_all, dq_local, dq_reach, dkv_local, beyond, grad_w_out.astype(jnp.bfloat16),
        attn_sums, ffn_sums,
    )
    last = row_reduce(grad_last)
    last.first()
    reduce_ffn.join()
    last.join()
    last.second()
    input_part = dot_nt(grad_qkv, full_qkv)
    grad_inputs = (
        grad_first
        + cut(input_part, core, rows, 0)
        + over_core(cut(input_part, 1 - core, rows, 0).astype(jnp.bfloat16)).astype(jnp.float32)
    )
    ffn_mine = reduce_ffn.result()
    if tuned:
        got = over_x(ffn_mine)
        ffn_mine = jnp.concatenate(
            [ffn_mine[:-1] + got[:-1], ordered(chip, ffn_mine[-1:], got[-1:], 0)], axis=0
        )
    else:
        ffn_mine = chips_sum(ffn_mine)
    (grad_inputs,) = last.join(grad_inputs)
    last.third()
    last.join()
    last.fourth()
    grad_up, grad_gate, grad_down = lay_out(core_ref, ffn_mine, over_core(ffn_mine))
    if tuned:
        grad_up, grad_gate, grad_down = last.join(grad_up, grad_gate, grad_down)
    last_mine = chips_sum(last.result())[0]
    last_rows, vector_rows = finish(core_ref, last_mine, over_core(last_mine))

    return (
        layer_out[None],
        grad_inputs[None],
        *last_rows,
        grad_up,
        grad_gate,
        grad_down,
    ) + tuple(row[0] for row in vector_rows)


def solution(mesh):
    rows_spec = P("fsdp", "ctx", None)
    in_specs = (
        (rows_spec, P("fsdp", "ctx"), P("fsdp", "ctx"))
        + (P("fsdp", None),) * 7
        + (P("fsdp"),) * VECTORS
        + (rows_spec,)
    )
    out_specs = (rows_spec, rows_spec) + (P("fsdp", None),) * 7 + (P("fsdp"),) * VECTORS
    return jax.shard_map(
        on_device, mesh=mesh, in_specs=in_specs, out_specs=out_specs, check_vma=False
    )
```

```python
import math
import jax
import jax.numpy as jnp
from jax import lax
from jax.experimental import pallas as pl
from jax.experimental.pallas import tpu as pltpu
from jax.sharding import PartitionSpec as P

H = 12
HD = 64
FF = 3072
HALF = 512
EPSILON = 1e-06
VECTORS = 8
QB = 256
ROW_BLOCK = 1024
SPAN = QB + 2 * HALF
BIG = 1e30
MIB = 1024 * 1024
SHORT = pl.CostEstimate(flops=1024, bytes_accessed=1024, transcendentals=0)

Z_SWAP = ((0, 1), (1, 0), (2, 3), (3, 2))
Z_MID = ((1, 2), (2, 1))
Z_OUT = ((1, 0), (2, 3))
Z_IN = ((0, 1), (3, 2))


def dot_nn(a, b):
    return lax.dot_general(a, b, (((1,), (0,)), ((), ())), preferred_element_type=jnp.float32)


def dot_nt(a, b):
    return lax.dot_general(a, b, (((1,), (1,)), ((), ())), preferred_element_type=jnp.float32)


def dot_tn(a, b):
    return lax.dot_general(a, b, (((0,), (0,)), ((), ())), preferred_element_type=jnp.float32)


def tie(*values):
    return lax.optimization_barrier(values)


def head_slopes(number):
    power_two = 2 ** int(math.floor(math.log2(number)))
    first_part = [2.0 ** (-8.0 * (position + 1) / power_two) for position in range(power_two)]
    extra_part = [
        2.0 ** (-8.0 * (2 * position + 1) / (2 * power_two))
        for position in range(number - power_two)
    ]
    return jnp.array(first_part + extra_part, dtype=jnp.float32)


def over_core(x):
    count = lax.axis_size("ctx")
    return lax.ppermute(x, "ctx", [(i, i ^ 1) for i in range(count)])


def from_previous_chip(x):
    count = lax.axis_size("ctx")
    return lax.ppermute(x, "ctx", [(i, i + 2) for i in range(count - 2)])


def from_next_chip(x):
    count = lax.axis_size("ctx")
    return lax.ppermute(x, "ctx", [(i + 2, i) for i in range(count - 2)])


def over_x(x):
    return lax.ppermute(x, "ctx", [(i, i ^ 2) for i in range(4)])


def over_y(x):
    return lax.ppermute(x, "fsdp", [(i, i ^ 1) for i in range(8)])


def over_z(x, moves):
    return lax.ppermute(
        x, "fsdp", [(2 * a + y, 2 * b + y) for a, b in moves for y in range(2)]
    )


def ordered(core, own, other, axis):
    return jnp.where(
        core == 0,
        jnp.concatenate([own, other], axis=axis),
        jnp.concatenate([other, own], axis=axis),
    )


def shard_number(k, dy):
    me = lax.axis_index("fsdp")
    return me ^ (2 * k + dy)


class Chain:
    live = ()

    def join(self, *values):
        held = tie(*[getattr(self, name) for name in self.live], *values)
        for name, value in zip(self.live, held):
            setattr(self, name, value)
        return held[len(self.live) :]


class Gather(Chain):
    def __init__(self, piece):
        self.own = piece

    def first_z(self):
        self.a = over_z(self.own, Z_SWAP)
        self.b = over_z(self.own, Z_MID)

    def first_y(self):
        self.y0 = over_y(self.own)
        self.live = ("y0", "a", "b")

    def first(self):
        self.first_z()
        self.first_y()

    def second(self, *values):
        self.a, self.b, *values = tie(self.a, self.b, *values)
        self.c = over_z(self.a, Z_MID)
        self.d = over_z(self.b, Z_OUT)
        self.ya = over_y(self.a)
        self.live = ("c", "d", "ya")
        return values

    def third(self, *values):
        self.z2, *values = tie(self.c + self.d, *values)
        self.e = over_z(self.c, Z_OUT)
        self.yz2 = over_y(self.z2)
        self.live = ("e", "yz2")
        return values

    def fourth(self, *values):
        self.z3, *values = tie(self.b + self.e, *values)
        self.yz3 = over_y(self.z3)
        self.live = ("yz3",)
        return values

    def pieces(self):
        return [self.own, self.a, self.z2, self.z3, self.y0, self.ya, self.yz2, self.yz3]

    def numbers(self):
        return jnp.stack([shard_number(k, dy) for dy in range(2) for k in range(4)])


class Reduce(Chain):
    def __init__(self, pieces):
        self.pieces = pieces

    def part(self, k, dy):
        return self.pieces[4 * dy + k]

    def first(self, *values):
        send, *values = tie(self.part(3, 1), *values)
        self.y = over_y(send)
        self.live = ("y",)
        return values

    def second(self, *values):
        self.q3, send, *values = tie(self.part(3, 0) + self.y, self.part(2, 1), *values)
        self.y = over_y(send)
        self.e = over_z(self.q3, Z_IN)
        self.live = ("y", "e")
        return values

    def third(self, *values):
        q2 = self.part(2, 0) + self.y
        self.q2, on, send, *values = tie(q2, q2 + self.e, self.part(1, 1), *values)
        self.y = over_y(send)
        self.d = over_z(self.q2, Z_IN)
        self.c = over_z(on, Z_MID)
        self.live = ("y", "d", "c")
        return values

    def fourth(self, *values):
        on_b, on_a, send, *values = tie(
            self.q3 + self.d, self.part(1, 0) + self.y + self.c, self.part(0, 1), *values
        )
        self.y = over_y(send)
        self.b = over_z(on_b, Z_MID)
        self.a = over_z(on_a, Z_SWAP)
        self.live = ("y", "b", "a")
        return values

    def result(self):
        return self.part(0, 0) + self.y + self.a + self.b


class LateReduce(Reduce):
    def fourth(self, *values):
        on_b, on_a, *values = tie(
            self.q3 + self.d, self.part(1, 0) + self.y + self.c, *values
        )
        self.b = over_z(on_b, Z_MID)
        self.a = over_z(on_a, Z_SWAP)
        return values

    def last_y(self, *values):
        send, *values = tie(self.part(0, 1), *values)
        self.y = over_y(send)
        self.live = ("y", "b", "a")
        return values


class PlainGather(Chain):
    def __init__(self, piece):
        self.own = piece

    def first(self, *values):
        return values

    first_z = first_y = second = third = fourth = first

    def pieces(self):
        whole = lax.all_gather(self.own, "fsdp", axis=0, tiled=True)
        rows = whole.shape[0] // 8
        return [whole[i * rows : (i + 1) * rows] for i in range(8)]

    def numbers(self):
        return jnp.arange(8, dtype=jnp.int32)


class PlainReduce(Chain):
    def __init__(self, pieces):
        self.full = jnp.concatenate(pieces, axis=1)

    def first(self, *values):
        return values

    second = third = fourth = first

    def result(self):
        return lax.psum_scatter(self.full, "fsdp", scatter_dimension=1, tiled=True)


def chips_sum(total):
    count = lax.axis_size("ctx")
    if count == 4:
        return total + over_x(total)
    core = lax.axis_index("ctx") % 2
    slots = jnp.stack(
        [jnp.where(core == i, total, jnp.zeros_like(total)) for i in range(2)]
    )
    return lax.dynamic_index_in_dim(lax.psum(slots, "ctx"), core, 0, keepdims=False)


def local_blocks(chip):
    return (
        (pl.multiple_of(chip * QB, QB), pl.multiple_of(chip * QB, QB), HALF + QB, chip * HALF),
        (pl.multiple_of((1 - chip) * QB, QB), 0, 2 * HALF, QB + chip * QB),
    )


def reach_blocks(chip):
    return ((0, 0, SPAN, HALF), (QB, QB, SPAN, HALF))


def rows_at(start, count):
    return pl.ds(start, count)


def both_chips(chip, local_ref, beyond_ref, all_ref):
    own = local_ref.shape[0]
    count = beyond_ref.shape[0]
    all_ref[rows_at(pl.multiple_of(chip * count, count), own), :] = local_ref[...]
    all_ref[rows_at(pl.multiple_of((1 - chip) * own, count), count), :] = beyond_ref[...]


def fill_distance(dist, block, seg_ref, tag_ref):
    q_at, k_at, span, shift = block
    key_pos = lax.broadcasted_iota(jnp.int32, (span, QB), 0)
    row_pos = lax.broadcasted_iota(jnp.int32, (span, QB), 1) + shift
    gap = jnp.abs(key_pos - row_pos)
    same = tag_ref[rows_at(k_at, span), :] == seg_ref[:, rows_at(q_at, QB)]
    kept = ((gap <= HALF) & same) | (gap == 0)
    dist[...] = jnp.where(kept, gap.astype(jnp.float32), BIG)


def attn_fwd_kernel(
    plan, chip, slopes, q_ref, k_ref, v_ref, seg_ref, tag_ref, k_else, v_else, out_ref, lse_ref, *dists
):
    pair = pl.program_id(0)
    blocks = plan(chip[0])
    if k_else is not None:
        *dists, k_all, v_all = dists
        both_chips(chip[0], k_ref, k_else, k_all)
        both_chips(chip[0], v_ref, v_else, v_all)
        k_ref, v_ref = k_all, v_all

    @pl.when(pair == 0)
    def _():
        for dist, block in zip(dists, blocks):
            fill_distance(dist, block, seg_ref, tag_ref)

    lane = lax.broadcasted_iota(jnp.int32, (QB, 2 * HD), 1)
    work = [(dist, block, a) for dist, block in zip(dists, blocks) for a in range(2)]

    def raw_scores(item):
        dist, (q_at, k_at, span, shift), a = item
        q = q_ref[rows_at(q_at, QB), :]
        mine = (lane >= HD) if a else (lane < HD)
        q_a = jnp.where(mine, q, jnp.zeros_like(q)) * jnp.asarray(1.0 / math.sqrt(HD), q.dtype)
        return dot_nt(k_ref[rows_at(k_at, span), :], q_a)

    ahead = raw_scores(work[0])
    parts = []
    for i, (dist, (q_at, k_at, span, shift), a) in enumerate(work):
        raw = ahead
        if i + 1 < len(work):
            ahead = raw_scores(work[i + 1])
        if a == 0:
            v_t = v_ref[rows_at(k_at, span), :].T
            parts = []
        s = raw - slopes[2 * pair + a] * dist[...]
        top = jnp.max(s, axis=0, keepdims=True)
        p = jnp.exp(s - top)
        total = jnp.sum(p, axis=0, keepdims=True)
        o_t = dot_nn(v_t[a * HD : (a + 1) * HD, :], p.astype(jnp.bfloat16))
        parts.append(o_t * (1.0 / total))
        lse_ref[0, a : a + 1, rows_at(q_at, QB)] = top + jnp.log(total)
        if a == 1:
            out_ref[rows_at(q_at, QB), :] = jnp.concatenate(parts, axis=0).T.astype(jnp.bfloat16)


def distances(plan):
    return [pltpu.VMEM((block[2], QB), jnp.float32) for block in plan(0)]


def attention_forward(plan, chip, queries, keys_values, seg_row, tag_col, slopes, beyond=None):
    rows, width = queries.shape
    ext = tag_col.shape[0]
    own = keys_values.shape[0]
    more = () if beyond is None else (beyond, beyond)
    pairs = width // (2 * HD)

    def body(*refs):
        if beyond is None:
            refs = refs[:7] + (None, None) + refs[7:]
        attn_fwd_kernel(plan, *refs)

    return pl.pallas_call(
        body,
        grid=(pairs,),
        in_specs=[
            pl.BlockSpec(memory_space=pltpu.SMEM),
            pl.BlockSpec(memory_space=pltpu.SMEM),
            pl.BlockSpec((rows, 2 * HD), lambda h: (0, h)),
            pl.BlockSpec((own, 2 * HD), lambda h: (0, h)),
            pl.BlockSpec((own, 2 * HD), lambda h: (0, pairs + h)),
            pl.BlockSpec((1, rows), lambda h: (0, 0)),
            pl.BlockSpec((ext, 1), lambda h: (0, 0)),
        ]
        + [
            pl.BlockSpec((ext - own, 2 * HD), lambda h, t=t: (0, t * pairs + h))
            for t in range(len(more))
        ],
        out_specs=[
            pl.BlockSpec((rows, 2 * HD), lambda h: (0, h)),
            pl.BlockSpec((1, 8, rows), lambda h: (h, 0, 0)),
        ],
        out_shape=[
            jax.ShapeDtypeStruct((rows, width), jnp.bfloat16),
            jax.ShapeDtypeStruct((pairs, 8, rows), jnp.float32),
        ],
        scratch_shapes=distances(plan) + [pltpu.VMEM((ext, 2 * HD), jnp.bfloat16)] * len(more),
        compiler_params=pltpu.CompilerParams(vmem_limit_bytes=56 * MIB),
        cost_estimate=SHORT,
    )(chip, slopes, queries, keys_values, keys_values, seg_row, tag_col, *more)


def attn_bwd_kernel(
    plan, low, chip, slopes, q_ref, k_ref, v_ref, o_ref, do_ref, do_else_ref, lse_ref, seg_ref, tag_ref, start_ref,
    k_else, v_else, dq_ref, dkv_ref, beyond_ref, *dists,
):
    step = pl.program_id(0)
    pair = step + low
    blocks = plan(chip[0])
    if k_else is not None:
        *dists, k_all, v_all = dists
        both_chips(chip[0], k_ref, k_else, k_all)
        both_chips(chip[0], v_ref, v_else, v_all)
        k_ref, v_ref = k_all, v_all

    @pl.when(step == 0)
    def _():
        for dist, block in zip(dists, blocks):
            fill_distance(dist, block, seg_ref, tag_ref)

    lane = lax.broadcasted_iota(jnp.int32, (QB, 2 * HD), 1)
    scale = 1.0 / math.sqrt(HD)
    if start_ref is None:
        dkv_ref[...] = jnp.zeros_like(dkv_ref)
    else:
        count = dkv_ref.shape[1]
        dkv_ref[...] = start_ref[:, rows_at(pl.multiple_of(chip[0] * HALF, HALF), count), :]
    for dist, (q_at, k_at, span, shift) in zip(dists, blocks):
        q = q_ref[rows_at(q_at, QB), :] * jnp.asarray(scale, jnp.bfloat16)
        do = jnp.where(chip[1] == 1, do_ref[rows_at(q_at, QB), :], do_else_ref[rows_at(q_at, QB), :])
        k = k_ref[rows_at(k_at, span), :]
        v = v_ref[rows_at(k_at, span), :]
        k_t = k.T
        mixed_t = (do.astype(jnp.float32) * o_ref[rows_at(q_at, QB), :].astype(jnp.float32)).T
        parts = []
        ps = []
        dss = []
        qs = []
        dos = []
        for a in range(2):
            mine = (lane >= HD) if a else (lane < HD)
            q_a = jnp.where(mine, q, jnp.zeros_like(q))
            do_a = jnp.where(mine, do, jnp.zeros_like(do))
            delta = jnp.sum(mixed_t[a * HD : (a + 1) * HD, :], axis=0, keepdims=True)
            s = dot_nt(k, q_a) - slopes[2 * pair + a] * dist[...]
            p = jnp.exp(s - lse_ref[0, a : a + 1, rows_at(q_at, QB)])
            dp = dot_nt(v, do_a)
            ds = (p * (dp - delta)).astype(jnp.bfloat16)
            parts.append(dot_nn(k_t[a * HD : (a + 1) * HD, :], ds) * scale)
            ps.append(p.astype(jnp.bfloat16))
            dss.append(ds)
            qs.append(q_a)
            dos.append(do_a)
        dq_ref[rows_at(q_at, QB), :] = jnp.concatenate(parts, axis=0).T.astype(jnp.bfloat16)
        dkv_ref[0, rows_at(k_at, span), :] += dot_nn(
            jnp.concatenate(dss, axis=1), jnp.concatenate(qs, axis=0)
        )
        dkv_ref[1, rows_at(k_at, span), :] += dot_nn(
            jnp.concatenate(ps, axis=1), jnp.concatenate(dos, axis=0)
        )
    if beyond_ref is not None:
        other = pl.multiple_of((1 - chip[0]) * 2 * HALF, HALF)
        beyond_ref[...] = dkv_ref[:, rows_at(other, HALF), :].astype(jnp.bfloat16)


def attention_backward(
    plan, chip, queries, keys_values, attended, grad_if, grad_else, lse, seg_row, tag_col, slopes, start,
    low=0, count=None, into=(), beyond=None,
):
    rows, width = queries.shape
    ext = tag_col.shape[0]
    own = keys_values.shape[0]
    more = () if beyond is None else (beyond, beyond)
    pairs = width // (2 * HD)
    count = pairs if count is None else count
    inner = pl.BlockSpec((rows, 2 * HD), lambda h: (0, low + h))
    starts = () if start is None else (start,)

    def body(*refs):
        refs = list(refs)
        fixed, refs = refs[:11], refs[11:]
        begin = refs.pop(0) if starts else None
        others = [refs.pop(0) for _ in more] or [None, None]
        refs = refs[len(into) :]
        outs, refs = refs[: 3 - len(starts)], refs[3 - len(starts) :]
        outs += [None] * len(starts)
        attn_bwd_kernel(plan, low, *fixed, begin, *others, *outs, *refs)

    return pl.pallas_call(
        body,
        grid=(count,),
        in_specs=[
            pl.BlockSpec(memory_space=pltpu.SMEM),
            pl.BlockSpec(memory_space=pltpu.SMEM),
            inner,
            pl.BlockSpec((own, 2 * HD), lambda h: (0, low + h)),
            pl.BlockSpec((own, 2 * HD), lambda h: (0, pairs + low + h)),
            inner,
            inner,
            inner,
            pl.BlockSpec((1, 8, rows), lambda h: (low + h, 0, 0)),
            pl.BlockSpec((1, rows), lambda h: (0, 0)),
            pl.BlockSpec((ext, 1), lambda h: (0, 0)),
        ]
        + [pl.BlockSpec((2, s.shape[1], 2 * HD), lambda h: (0, 0, low + h)) for s in starts]
        + [
            pl.BlockSpec((ext - own, 2 * HD), lambda h, t=t: (0, t * pairs + low + h))
            for t in range(len(more))
        ]
        + [pl.BlockSpec(memory_space=pl.ANY)] * len(into),
        out_specs=[inner, pl.BlockSpec((2, ext, 2 * HD), lambda h: (0, 0, low + h))]
        + [pl.BlockSpec((2, HALF, 2 * HD), lambda h: (0, 0, low + h))] * (1 - len(starts)),
        out_shape=[
            jax.ShapeDtypeStruct((rows, width), jnp.bfloat16),
            jax.ShapeDtypeStruct((2, ext, width), jnp.float32),
        ]
        + [jax.ShapeDtypeStruct((2, HALF, width), jnp.bfloat16)] * (1 - len(starts)),
        input_output_aliases={11 + len(starts) + len(more) + i: i for i in range(len(into))},
        scratch_shapes=distances(plan) + [pltpu.VMEM((ext, 2 * HD), jnp.bfloat16)] * len(more),
        compiler_params=pltpu.CompilerParams(vmem_limit_bytes=56 * MIB),
        cost_estimate=SHORT,
    )(
        chip, slopes, queries, keys_values, keys_values, attended, grad_if, grad_else, lse,
        seg_row, tag_col, *starts, *more, *into,
    )


def norm_parts(values, gain_vec, offset):
    centred = values - jnp.mean(values, axis=-1, keepdims=True)
    variance = jnp.mean(centred * centred, axis=-1, keepdims=True)
    inverse = lax.rsqrt(variance + EPSILON)
    normed = centred * inverse
    return (normed * gain_vec + offset, normed, inverse)


def project_kernel(
    place_numbers, spot, x_ref, *refs
):
    pieces = refs[:8]
    vec_ref, w_ref, out_ref, local_ref, reach_ref, kv_ref, send_ref, weight = refs[8:]
    core, chip = spot[0], spot[1]
    fill_weight(place_numbers, pieces, weight)
    half = out_ref.shape[1]
    rows = local_ref.shape[0]
    w_ref[...] = weight[:, : 3 * half]
    out_ref[...] = weight[:, 3 * half : 4 * half]
    vec = weight[:, 4 * half :].astype(jnp.float32).T[:VECTORS, :]
    vec_ref[...] = vec
    projected = dot_nn(x_ref[...], weight[:, : 3 * half])

    def bias(i):
        return jnp.where(core == 0, vec[i : i + 1, :half], vec[i : i + 1, half:])

    queries = (projected[:, :half] + bias(0)).astype(jnp.bfloat16)
    first = chip == 0
    local_ref[...] = jnp.where(first, queries[:rows], queries[rows:])
    reach_ref[...] = jnp.where(first, queries[rows:], queries[:rows])
    keys = projected[:, half : 2 * half].astype(jnp.bfloat16)
    values = (projected[:, 2 * half :] + bias(1)).astype(jnp.bfloat16)
    kv_ref[:, :half] = keys
    kv_ref[:, half:] = values
    send_ref[:, :half] = jnp.where(first, keys[rows:], keys[:rows])
    send_ref[:, half:] = jnp.where(first, values[rows:], values[:rows])


def project(numbers, spot, x, pieces):
    all_rows, width = x.shape
    half = width // 2
    rows = all_rows // 2
    whole = pl.BlockSpec(memory_space=pltpu.VMEM)
    smem = pl.BlockSpec(memory_space=pltpu.SMEM)
    low = jnp.bfloat16
    return pl.pallas_call(
        project_kernel,
        in_specs=[smem, smem] + [whole] * 9,
        out_specs=[whole] * 7,
        out_shape=[
            jax.ShapeDtypeStruct((VECTORS, width), jnp.float32),
            jax.ShapeDtypeStruct((width, 3 * half), low),
            jax.ShapeDtypeStruct((width, half), low),
            jax.ShapeDtypeStruct((rows, half), low),
            jax.ShapeDtypeStruct((rows, half), low),
            jax.ShapeDtypeStruct((all_rows, width), low),
            jax.ShapeDtypeStruct((rows, width), low),
        ],
        scratch_shapes=[pltpu.VMEM((width, pieces[0].shape[1]), low)],
        compiler_params=pltpu.CompilerParams(vmem_limit_bytes=56 * MIB),
        cost_estimate=SHORT,
    )(numbers, spot, x, *pieces)


def first_norm_kernel(
    core, vec_ref, attended_ref, mine_ref, other_ref, x_ref,
    norm_ref, normed_ref, inverse_ref, low_ref, w_ref,
):
    half = mine_ref.shape[1]
    rows = norm_ref.shape[0]
    first = core[0] == 0

    @pl.when(pl.program_id(0) == 0)
    def _():
        w_ref[:, :half] = jnp.where(first, mine_ref[...], other_ref[...])
        w_ref[:, half:] = jnp.where(first, other_ref[...], mine_ref[...])

    at = pl.multiple_of(core[0] * rows * pl.num_programs(0) + pl.program_id(0) * rows, rows)
    branch = dot_nn(attended_ref[pl.ds(at, rows), :], w_ref[...]) + vec_ref[2:3, :]
    norm, normed, inverse = norm_parts(
        x_ref[...].astype(jnp.float32) + branch, vec_ref[4:5, :], vec_ref[5:6, :]
    )
    norm_ref[...] = norm
    normed_ref[...] = normed
    inverse_ref[...] = inverse
    low_ref[...] = norm.astype(jnp.bfloat16)


def first_norm_of(core, vec, attended, mine, other, x):
    rows, width = x.shape
    steps = 2
    block = pl.BlockSpec((rows // steps, width), lambda i: (i, 0))

    def all_of(a):
        return pl.BlockSpec(a.shape, lambda i: (0, 0))

    return pl.pallas_call(
        first_norm_kernel,
        grid=(steps,),
        in_specs=[pl.BlockSpec(memory_space=pltpu.SMEM)]
        + [all_of(a) for a in (vec, attended, mine, other)]
        + [block],
        out_specs=[
            block, block, pl.BlockSpec((rows // steps, 1), lambda i: (i, 0)), block,
            pl.BlockSpec((width, width), lambda i: (0, 0)),
        ],
        out_shape=[
            jax.ShapeDtypeStruct((rows, width), jnp.float32),
            jax.ShapeDtypeStruct((rows, width), jnp.float32),
            jax.ShapeDtypeStruct((rows, 1), jnp.float32),
            jax.ShapeDtypeStruct((rows, width), jnp.bfloat16),
            jax.ShapeDtypeStruct((width, width), jnp.bfloat16),
        ],
        compiler_params=pltpu.CompilerParams(vmem_limit_bytes=56 * MIB),
        cost_estimate=SHORT,
    )(core, vec, attended, mine, other, x)


def norm_back(upstream, normed, inverse, gain_vec):
    scaled = upstream * gain_vec
    row_inner = (
        scaled
        - jnp.mean(scaled, axis=-1, keepdims=True)
        - normed * jnp.mean(scaled * normed, axis=-1, keepdims=True)
    )
    return row_inner * inverse


def last_grads_kernel(
    numbers, spot, x_ref, local_ref, reach_ref, dkv_ref, beyond_ref, out_w_ref, attn_ref, ffn_ref, *refs
):
    *pieces, grad_ref, last_ref = refs
    core, chip = spot[0], spot[1]
    first = chip == 0
    rows, half = local_ref.shape
    grad_ref[:rows, :half] = jnp.where(first, local_ref[...], reach_ref[...])
    grad_ref[rows:, :half] = jnp.where(first, reach_ref[...], local_ref[...])
    for t in range(2):
        got = beyond_ref[t].astype(jnp.float32)
        part = slice((t + 1) * half, (t + 2) * half)
        top = dkv_ref[t, :rows, :] + jnp.where(first, 0.0, got)
        low = dkv_ref[t, rows:, :] + jnp.where(first, got, 0.0)
        grad_ref[:rows, part] = top.astype(jnp.bfloat16)
        grad_ref[rows:, part] = low.astype(jnp.bfloat16)
    grads = grad_ref[...]
    last_ref[:, : 3 * half] = dot_tn(x_ref[...], grads).astype(jnp.bfloat16)
    last_ref[:, 3 * half : 4 * half] = out_w_ref[...]
    sums = [
        jnp.sum(grads[:, i * half : (i + 1) * half].astype(jnp.float32), axis=0, keepdims=True)
        for i in (0, 2)
    ]
    nothing = jnp.zeros_like(sums[0])
    vectors = [
        jnp.where(
            core == 0, jnp.concatenate([s, nothing], axis=1), jnp.concatenate([nothing, s], axis=1)
        )
        for s in sums
    ]
    vectors += [attn_ref[2:3, :], ffn_ref[2:3, :], attn_ref[0:2, :], ffn_ref[0:2, :]]
    vectors.append(jnp.zeros((128 - VECTORS, 2 * half), jnp.float32))
    last_ref[:, 4 * half :] = jnp.concatenate(vectors, axis=0).T.astype(jnp.bfloat16)
    for i, piece in enumerate(pieces):
        piece[0] = last_ref[shard_rows(numbers, i, piece), :]


def last_grads(numbers, spot, x, dq_local, dq_reach, dkv, beyond, grad_w_out, attn_sums, ffn_sums):
    all_rows, width = x.shape
    half = width // 2
    whole = pl.BlockSpec(memory_space=pltpu.VMEM)
    return pl.pallas_call(
        last_grads_kernel,
        in_specs=[pl.BlockSpec(memory_space=pltpu.SMEM)] * 2 + [whole] * 8,
        out_specs=[whole] * 9,
        out_shape=[jax.ShapeDtypeStruct((1, width // 8, 4 * half + 128), jnp.bfloat16)] * 8
        + [jax.ShapeDtypeStruct((all_rows, 3 * half), jnp.bfloat16)],
        scratch_shapes=[pltpu.VMEM((width, 4 * half + 128), jnp.bfloat16)],
        compiler_params=pltpu.CompilerParams(vmem_limit_bytes=30 * MIB),
        cost_estimate=SHORT,
    )(numbers, spot, x, dq_local, dq_reach, dkv, beyond, grad_w_out, attn_sums, ffn_sums)


def finish_kernel(core, mine_ref, other_ref, *outs):
    first = core[0] == 0
    half = outs[0].shape[1] // 2
    for i, out in enumerate(outs[:4]):
        part = slice(i * half, (i + 1) * half)
        mine, other = mine_ref[:, part].astype(jnp.float32), other_ref[:, part].astype(jnp.float32)
        out[:, :half] = jnp.where(first, mine, other)
        out[:, half:] = jnp.where(first, other, mine)
    mine, other = mine_ref[:, 4 * half :], other_ref[:, 4 * half :]
    vectors = (mine.astype(jnp.float32) + other.astype(jnp.float32)).T
    for i, out in enumerate(outs[4:]):
        out[...] = vectors[i : i + 1, :]


def finish(core, mine, other):
    rows, columns = mine.shape
    width = (columns - 128) // 2
    whole = pl.BlockSpec(memory_space=pltpu.VMEM)
    results = pl.pallas_call(
        finish_kernel,
        in_specs=[pl.BlockSpec(memory_space=pltpu.SMEM)] + [whole] * 2,
        out_specs=[whole] * (4 + VECTORS),
        out_shape=[jax.ShapeDtypeStruct((rows, width), jnp.float32)] * 4
        + [jax.ShapeDtypeStruct((1, rows), jnp.float32)] * VECTORS,
        cost_estimate=SHORT,
    )(core, mine, other)
    return results[:4], results[4:]


def add_sums(step, sums_ref, *columns):
    rows = [jnp.sum(value, axis=0, keepdims=True) for value in columns]
    rows.append(jnp.zeros((8 - len(rows), sums_ref.shape[1]), jnp.float32))
    add_up(step, sums_ref, jnp.concatenate(rows, axis=0))


def second_norm_kernel(
    vec_ref, norm_ref, part_ref, sent_ref, cot_ref, out_ref, grad_ref, low_ref, sums_ref
):
    step = pl.program_id(0)
    bias, gain, shift = vec_ref[3:4, :], vec_ref[6:7, :], vec_ref[7:8, :]
    value = norm_ref[...] + part_ref[...] + sent_ref[...].astype(jnp.float32) + bias
    result, normed, inverse = norm_parts(value, gain, shift)
    out_ref[...] = result.astype(jnp.bfloat16)
    upstream = cot_ref[...].astype(jnp.float32)
    grad = norm_back(upstream, normed, inverse, gain)
    grad_ref[...] = grad
    low_ref[...] = grad.astype(jnp.bfloat16)
    add_sums(step, sums_ref, upstream * normed, upstream, grad)


def second_norm(vec, first_norm, part, sent, cotangent):
    rows, width = part.shape
    block = pl.BlockSpec((rows // 2, width), lambda i: (i, 0))
    eight = pl.BlockSpec((8, width), lambda i: (0, 0))
    return pl.pallas_call(
        second_norm_kernel,
        grid=(2,),
        in_specs=[eight] + [block] * 4,
        out_specs=[block] * 3 + [eight],
        out_shape=[
            jax.ShapeDtypeStruct((rows, width), jnp.bfloat16),
            jax.ShapeDtypeStruct((rows, width), jnp.float32),
            jax.ShapeDtypeStruct((rows, width), jnp.bfloat16),
            jax.ShapeDtypeStruct((8, width), jnp.float32),
        ],
        compiler_params=pltpu.CompilerParams(vmem_limit_bytes=14 * MIB),
        cost_estimate=SHORT,
    )(vec, first_norm, part, sent, cotangent)


def first_norm_back_kernel(
    core, vec_ref, w_ref, up_ref, part_ref, sent_ref, normed_ref, inverse_ref,
    grad_ref, low_mine, low_theirs, back_mine, back_theirs, sums_ref,
):
    step = pl.program_id(0)
    half = low_mine.shape[1]
    upstream = up_ref[...] + part_ref[...] + sent_ref[...].astype(jnp.float32)
    normed = normed_ref[...]
    grad = norm_back(upstream, normed, inverse_ref[...], vec_ref[4:5, :])
    grad_ref[...] = grad
    low = grad.astype(jnp.bfloat16)
    back = dot_nt(low, w_ref[...]).astype(jnp.bfloat16)
    first = core[0] == 0
    for value, mine, theirs in ((low, low_mine, low_theirs), (back, back_mine, back_theirs)):
        left, right = value[:, :half], value[:, half:]
        mine[...] = jnp.where(first, left, right)
        theirs[...] = jnp.where(first, right, left)
    add_sums(step, sums_ref, upstream * normed, upstream, grad)


def first_norm_back(core, vec, w_out, grad_second, part, sent, normed, inverse):
    rows, width = part.shape
    steps = 2
    block = pl.BlockSpec((rows // steps, width), lambda i: (i, 0))
    halves = pl.BlockSpec((rows // steps, width // 2), lambda i: (i, 0))
    eight = pl.BlockSpec((8, width), lambda i: (0, 0))
    return pl.pallas_call(
        first_norm_back_kernel,
        grid=(steps,),
        in_specs=[
            pl.BlockSpec(memory_space=pltpu.SMEM),
            eight,
            pl.BlockSpec((width, width), lambda i: (0, 0)),
        ]
        + [block] * 4
        + [pl.BlockSpec((rows // steps, 1), lambda i: (i, 0))],
        out_specs=[block] + [halves] * 4 + [eight],
        out_shape=[jax.ShapeDtypeStruct((rows, width), jnp.float32)]
        + [jax.ShapeDtypeStruct((rows, width // 2), jnp.bfloat16)] * 4
        + [jax.ShapeDtypeStruct((8, width), jnp.float32)],
        compiler_params=pltpu.CompilerParams(vmem_limit_bytes=18 * MIB),
        cost_estimate=SHORT,
    )(core, vec, w_out, grad_second, part, sent, normed, inverse)


def lay_out_kernel(core, mine_ref, other_ref, up_ref, gate_ref, down_ref):
    first = core[0] == 0
    count, shard_rows, width = mine_ref.shape
    groups = count // 3
    shards = width // shard_rows

    def both(i):
        mine, other = mine_ref[i].astype(jnp.float32), other_ref[i].astype(jnp.float32)
        return jnp.where(first, mine, other), jnp.where(first, other, mine)

    for g in range(groups):
        for c, value in enumerate(both(2 * groups + g)):
            at = (c * groups + g) * shard_rows
            down_ref[at : at + shard_rows, :] = value
        for t, out in ((0, up_ref), (1, gate_ref)):
            for c, value in enumerate(both(2 * g + t)):
                for s in range(shards):
                    at = ((s * 2 + c) * groups + g) * shard_rows
                    out[:, at : at + shard_rows] = value[:, s * shard_rows : (s + 1) * shard_rows]


def lay_out(core, mine, other):
    count, shard_rows, width = mine.shape
    columns = count // 3 * 2 * width
    whole = pl.BlockSpec(memory_space=pltpu.VMEM)
    return pl.pallas_call(
        lay_out_kernel,
        in_specs=[pl.BlockSpec(memory_space=pltpu.SMEM)] + [whole] * 2,
        out_specs=[whole] * 3,
        out_shape=[
            jax.ShapeDtypeStruct((shard_rows, columns), jnp.float32),
            jax.ShapeDtypeStruct((shard_rows, columns), jnp.float32),
            jax.ShapeDtypeStruct((count // 3 * 2 * shard_rows, width), jnp.float32),
        ],
        compiler_params=pltpu.CompilerParams(vmem_limit_bytes=14 * MIB),
        cost_estimate=SHORT,
    )(core, mine, other)


def phi_parts(v):
    cdf = 0.5 * (1.0 + lax.erf(v * math.sqrt(0.5)))
    density = jnp.exp(-0.5 * v * v) * (1.0 / math.sqrt(2.0 * math.pi))
    return cdf, cdf + v * density


def shard_rows(numbers, i, piece):
    rows = piece.shape[-2]
    return pl.ds(pl.multiple_of(numbers[i] * rows, rows), rows)


def fill_weight(numbers, pieces, weight):
    for i, piece in enumerate(pieces):
        weight[shard_rows(numbers, i, piece), :] = piece[...]


def add_up(step, total, out):
    @pl.when(step == 0)
    def _():
        total[...] = out

    @pl.when(step > 0)
    def _():
        total[...] += out


def ffn_fwd_kernel(numbers, own_ref, other_ref, *refs):
    ups, gates, downs = refs[:8], refs[8:16], refs[16:24]
    hid_ref, act_ref, slope_ref, part_ref, send_ref = refs[24:29]
    x_all, up_w, gate_w, down_w, total = refs[29:]
    step = pl.program_id(0)
    rows = own_ref.shape[0]

    @pl.when(step == 0)
    def _():
        x_all[:rows, :] = own_ref[...]
        x_all[rows:, :] = other_ref[...]

    fill_weight(numbers, ups, up_w)
    fill_weight(numbers, gates, gate_w)
    fill_weight(numbers, downs, down_w)
    columns = up_w.shape[1]
    piece = columns // 3
    for i in range(3):
        part = slice(i * piece, (i + 1) * piece)
        x = x_all[...]
        up = dot_nn(x, up_w[:, part])
        gate = dot_nn(x, gate_w[:, part])
        cdf, derivative = phi_parts(gate)
        act = gate * cdf
        hidden = (act * up).astype(jnp.bfloat16)
        hid_ref[:, part] = hidden
        act_ref[:, part] = act.astype(jnp.bfloat16)
        slope_ref[:, part] = (derivative * up).astype(jnp.bfloat16)
    add_up(step, total, dot_nn(hid_ref[...], down_w[...]))

    @pl.when(step == pl.num_programs(0) - 1)
    def _():
        part_ref[...] = total[:rows, :]
        send_ref[...] = total[rows:, :].astype(jnp.bfloat16)


def piece_specs(rows, width, columns):
    steps = columns // width
    return [
        pl.BlockSpec((rows, width), lambda f, t=t: (0, t * steps + f))
        for t in range(3)
        for i in range(8)
    ]


def ffn_forward(own, other, pieces, numbers, columns):
    rows, width = own.shape
    steps = columns // width
    wide = pl.BlockSpec((2 * rows, width), lambda f: (0, f))
    whole = pl.BlockSpec((rows, width), lambda f: (0, 0))
    return pl.pallas_call(
        ffn_fwd_kernel,
        grid=(steps,),
        in_specs=[pl.BlockSpec(memory_space=pltpu.SMEM), whole, whole]
        + piece_specs(pieces[0].shape[0], width, columns),
        out_specs=[wide, wide, wide, whole, whole],
        out_shape=[jax.ShapeDtypeStruct((2 * rows, columns), jnp.bfloat16)] * 3
        + [
            jax.ShapeDtypeStruct((rows, width), jnp.float32),
            jax.ShapeDtypeStruct((rows, width), jnp.bfloat16),
        ],
        scratch_shapes=[
            pltpu.VMEM((2 * rows, width), jnp.bfloat16),
            pltpu.VMEM((width, width), jnp.bfloat16),
            pltpu.VMEM((width, width), jnp.bfloat16),
            pltpu.VMEM((width, width), jnp.bfloat16),
            pltpu.VMEM((2 * rows, width), jnp.float32),
        ],
        compiler_params=pltpu.CompilerParams(vmem_limit_bytes=56 * MIB),
        cost_estimate=SHORT,
    )(numbers, own, other, *(pieces * 3))


def down_grad_kernel(group, branch_ref, branch_other_ref, hid_ref, grad_ref):
    rows = branch_ref.shape[0]
    total = dot_tn(hid_ref[:rows, :], branch_ref[...])
    grad_ref[...] = (total + dot_tn(hid_ref[rows:, :], branch_other_ref[...])).astype(jnp.bfloat16)


def down_grad(group, branch, branch_other, hidden):
    rows, width = branch.shape
    whole = pl.BlockSpec((rows, width), lambda i, group: (0, 0))
    return pl.pallas_call(
        down_grad_kernel,
        grid_spec=pltpu.PrefetchScalarGridSpec(
            num_scalar_prefetch=1,
            grid=(1,),
            in_specs=[
                whole, whole, pl.BlockSpec((2 * rows, width), lambda i, group: (0, group[0])),
            ],
            out_specs=pl.BlockSpec((width, width), lambda i, group: (0, 0)),
        ),
        out_shape=jax.ShapeDtypeStruct((width, width), jnp.bfloat16),
        compiler_params=pltpu.CompilerParams(vmem_limit_bytes=18 * MIB),
        cost_estimate=SHORT,
    )(group, branch, branch_other, hidden)


def add_last_kernel(numbers, *refs):
    keep_ref, got_ref = refs[8:10]
    for i, out_ref in enumerate(refs[10:]):
        shard = shard_rows(numbers, i, out_ref)
        out_ref[0] = keep_ref[shard, :] + got_ref[shard, :]


def add_last(numbers, pieces, keep, got):
    units, rows, width = pieces[0].shape
    whole = pl.BlockSpec(memory_space=pltpu.VMEM)
    return pl.pallas_call(
        add_last_kernel,
        grid=(1,),
        in_specs=[pl.BlockSpec(memory_space=pltpu.SMEM)]
        + [pl.BlockSpec(memory_space=pl.ANY)] * 8
        + [whole, whole],
        out_specs=[pl.BlockSpec((1, rows, width), lambda i: (units - 1, 0, 0))] * 8,
        out_shape=[jax.ShapeDtypeStruct(pieces[0].shape, pieces[0].dtype)] * 8,
        input_output_aliases={1 + i: i for i in range(8)},
        compiler_params=pltpu.CompilerParams(vmem_limit_bytes=56 * MIB),
        cost_estimate=SHORT,
    )(numbers, *pieces, keep, got)


def ffn_bwd_kernel(numbers, own_ref, other_ref, branch_ref, branch_other_ref, act_ref, slope_ref, *refs):
    ups, gates, downs = refs[:8], refs[8:16], refs[16:24]
    grad_refs, part_ref, send_ref = refs[24:32], refs[32], refs[33]
    x_all, branch_all, up_w, gate_w, down_w, total, up_grad, gate_grad = refs[34:]
    step = pl.program_id(0)
    rows = own_ref.shape[0]

    @pl.when(step == 0)
    def _():
        x_all[:rows, :] = own_ref[...]
        x_all[rows:, :] = other_ref[...]
        branch_all[:rows, :] = branch_ref[...]
        branch_all[rows:, :] = branch_other_ref[...]

    fill_weight(numbers, ups, up_w)
    fill_weight(numbers, gates, gate_w)
    fill_weight(numbers, downs, down_w)
    x = x_all[...]
    outs = []
    piece = up_w.shape[1] // 3
    for i in range(3):
        part = slice(i * piece, (i + 1) * piece)
        d_hidden = dot_nt(branch_all[...], down_w[part, :])
        d_up = (d_hidden * act_ref[:, part].astype(jnp.float32)).astype(jnp.bfloat16)
        d_gate = (d_hidden * slope_ref[:, part].astype(jnp.float32)).astype(jnp.bfloat16)
        outs.append(dot_nt(d_up, up_w[:, part]) + dot_nt(d_gate, gate_w[:, part]))
        up_grad[:, part] = dot_tn(x, d_up).astype(jnp.bfloat16)
        gate_grad[:, part] = dot_tn(x, d_gate).astype(jnp.bfloat16)
    for i, grad_ref in enumerate(grad_refs):
        shard = shard_rows(numbers, i, grad_ref)
        grad_ref[0] = up_grad[shard, :]
        grad_ref[1] = gate_grad[shard, :]
    add_up(step, total, outs[0] + outs[1] + outs[2])

    @pl.when(step == pl.num_programs(0) - 1)
    def _():
        part_ref[...] = total[:rows, :]
        send_ref[...] = total[rows:, :].astype(jnp.bfloat16)


def ffn_backward(own, other, branch, branch_other, act, slope, pieces, numbers, columns):
    rows, width = own.shape
    steps = columns // width
    wide = pl.BlockSpec((2 * rows, width), lambda f: (0, f))
    whole = pl.BlockSpec((rows, width), lambda f: (0, 0))
    return pl.pallas_call(
        ffn_bwd_kernel,
        grid=(steps,),
        in_specs=[pl.BlockSpec(memory_space=pltpu.SMEM)]
        + [whole] * 4
        + [wide] * 2
        + piece_specs(pieces[0].shape[0], width, columns),
        out_specs=[
            *[pl.BlockSpec((2, width // 8, width), lambda f: (f, 0, 0))] * 8,
            whole,
            whole,
        ],
        out_shape=[
            *[jax.ShapeDtypeStruct((2 * steps + 1, width // 8, width), jnp.bfloat16)] * 8,
            jax.ShapeDtypeStruct((rows, width), jnp.float32),
            jax.ShapeDtypeStruct((rows, width), jnp.bfloat16),
        ],
        scratch_shapes=[
            pltpu.VMEM((2 * rows, width), jnp.bfloat16),
            pltpu.VMEM((2 * rows, width), jnp.bfloat16),
            pltpu.VMEM((width, width), jnp.bfloat16),
            pltpu.VMEM((width, width), jnp.bfloat16),
            pltpu.VMEM((width, width), jnp.bfloat16),
            pltpu.VMEM((2 * rows, width), jnp.float32),
            pltpu.VMEM((width, width), jnp.bfloat16),
            pltpu.VMEM((width, width), jnp.bfloat16),
        ],
        compiler_params=pltpu.CompilerParams(vmem_limit_bytes=56 * MIB),
        cost_estimate=SHORT,
    )(numbers, own, other, branch, branch_other, act, slope, *(pieces * 3))


def pack_kernel(core, up_ref, gate_ref, down_ref, out_ref):
    first = core[0] == 0
    shard_rows = up_ref.shape[0]
    width = down_ref.shape[1]
    shards = width // shard_rows
    groups = down_ref.shape[0] // shard_rows // 2
    at = 0
    for ref in (up_ref, gate_ref):
        for g in range(groups):
            for s in range(shards):
                left = (s * 2 * groups + g) * shard_rows
                right = left + groups * shard_rows
                out_ref[:, at : at + shard_rows] = jnp.where(
                    first, ref[:, left : left + shard_rows], ref[:, right : right + shard_rows]
                )
                at += shard_rows
    for g in range(groups):
        top = g * shard_rows
        low = top + groups * shard_rows
        out_ref[:, at : at + width] = jnp.where(
            first, down_ref[top : top + shard_rows, :], down_ref[low : low + shard_rows, :]
        )
        at += width


def pack(core, up, gate, down):
    shard_rows = up.shape[0]
    width = down.shape[1]
    whole = pl.BlockSpec(memory_space=pltpu.VMEM)
    return pl.pallas_call(
        pack_kernel,
        in_specs=[pl.BlockSpec(memory_space=pltpu.SMEM)] + [whole] * 3,
        out_specs=whole,
        out_shape=jax.ShapeDtypeStruct(
            (shard_rows, up.shape[1] + down.shape[0] // shard_rows // 2 * width), jnp.bfloat16
        ),
        compiler_params=pltpu.CompilerParams(vmem_limit_bytes=56 * MIB),
        cost_estimate=SHORT,
    )(core, up, gate, down)


def pack_first_kernel(core, *refs):
    first = core[0] == 0
    half = refs[0].shape[1] // 2
    out_ref = refs[-1]
    for i, ref in enumerate(refs[:4]):
        out_ref[:, i * half : (i + 1) * half] = jnp.where(first, ref[:, :half], ref[:, half:])
    out_ref[:, 4 * half :] = refs[4][...]


def pack_first(core, matrices, vectors):
    rows, width = matrices[0].shape
    whole = pl.BlockSpec(memory_space=pltpu.VMEM)
    return pl.pallas_call(
        pack_first_kernel,
        in_specs=[pl.BlockSpec(memory_space=pltpu.SMEM)] + [whole] * 5,
        out_specs=whole,
        out_shape=jax.ShapeDtypeStruct((rows, 2 * width + vectors.shape[1]), jnp.bfloat16),
        cost_estimate=SHORT,
    )(core, *matrices, vectors)


def on_device(
    tokens, segments, padding,
    w_query, w_key, w_value, w_out, w_up, w_gate, w_down,
    bias_query, bias_value, bias_out, bias_down, gain_attn, shift_attn, gain_ffn, shift_ffn,
    cotangent,
):
    tuned = lax.axis_size("ctx") == 4 and lax.axis_size("fsdp") == 8
    row_gather, row_reduce = (Gather, Reduce) if tuned else (PlainGather, PlainReduce)
    core = lax.axis_index("ctx") % 2
    chip = lax.axis_index("ctx") // 2
    chip_ref = chip[None].astype(jnp.int32)
    core_ref = core[None].astype(jnp.int32)
    inputs = tokens[0]
    rows, width = inputs.shape
    half = width // 2
    half_ff = FF // 2

    def cut(value, which, count, axis):
        return lax.dynamic_slice_in_dim(value, which * count, count, axis)

    def share(mine, theirs, axis):
        return ordered(core, mine, over_core(theirs), axis)

    vectors = jnp.stack(
        (bias_query, bias_value, bias_out, bias_down, gain_attn, shift_attn, gain_ffn, shift_ffn), axis=1
    )
    vectors = jnp.pad(vectors, ((0, 0), (0, 128 - VECTORS)))
    first = row_gather(pack_first(core_ref, (w_query, w_key, w_value, w_out), vectors))
    second = row_gather(pack(core_ref, w_up, w_gate, w_down))
    first.first()

    own_numbers = jnp.stack((segments[0], jnp.where(padding[0] == 1, -1, segments[0])))
    numbers = share(own_numbers, own_numbers, 1)
    slopes = cut(head_slopes(H), core, H // 2, 0)
    (numbers,) = first.join(numbers)
    tags = numbers[1]
    seg_row = numbers[0][None, :]
    if tuned:
        tags_send = jnp.where(chip == 0, tags[rows:], tags[:rows]) + 2
        first.second()
        beyond = over_x(tags_send)
        beyond, second.own = first.join(beyond, second.own)
        beyond = beyond - 2
        tags_reach = ordered(chip, tags, beyond, 0)[:, None]
        tags_local = tags[:, None]
        seg_local = cut(seg_row, chip, rows, 1)
        seg_reach = cut(seg_row, 1 - chip, rows, 1)
    else:
        tag_low = from_previous_chip(tags[rows:] + 2) - 2
        tag_high = from_next_chip(tags[:rows] + 2) - 2
        tags_wide = jnp.concatenate([tag_low, tags, tag_high])[:, None]
    first.third()
    inputs_all = share(inputs, inputs, 0)
    (inputs_all,) = first.join(inputs_all)
    (second.own,) = first.fourth(second.own)
    second.first_z()
    (second.own,) = first.join(second.own)
    second.first_y()

    spot = jnp.stack((core, chip if tuned else jnp.zeros_like(chip))).astype(jnp.int32)
    vec, full_qkv, out_half, queries_local, queries_reach, keys_values, beyond = project(
        first.numbers(), spot, inputs_all, first.pieces()
    )
    out_other = over_core(out_half)
    if tuned:
        queries_local, queries_reach, keys_values, beyond = second.join(
            queries_local, queries_reach, keys_values, beyond
        )
        beyond = over_x(beyond)
        second.second()
        attended_local, lse_local = attention_forward(
            local_blocks, chip_ref, queries_local, keys_values, seg_local, tags_local, slopes
        )
        attended_local, lse_local, beyond = second.join(attended_local, lse_local, beyond)
        keys_values, kv_beyond = second.third(keys_values, beyond)
        attended_reach, lse_reach = attention_forward(
            reach_blocks, chip_ref, queries_reach, keys_values, seg_reach, tags_reach, slopes, kv_beyond
        )
        attended_own = ordered(chip, attended_local, attended_reach, 0)
        (attended_own,) = second.join(attended_own)
        (attended_own,) = second.fourth(attended_own)
    else:
        queries = jnp.concatenate([queries_local, queries_reach], axis=0)
        kv_low = from_previous_chip(keys_values[rows:])
        kv_high = from_next_chip(keys_values[:rows])
        kv_wide = jnp.concatenate([kv_low, keys_values, kv_high], axis=0)
        spans = [(i * rows, i * rows + rows + 2 * HALF) for i in range(2)]
        forward_parts = [
            attention_forward(
                reach_blocks, chip_ref, queries[i * rows : (i + 1) * rows], kv_wide[low:high],
                seg_row[:, i * rows : (i + 1) * rows], tags_wide[low:high], slopes,
            )
            for i, (low, high) in enumerate(spans)
        ]
        attended_own = jnp.concatenate([part[0] for part in forward_parts], axis=0)
    attended_all = share(attended_own, attended_own, 1)
    first_norm, first_normed, first_inverse, own_low, full_out = first_norm_of(
        core_ref, vec, attended_all, out_half, out_other, inputs
    )
    other_low = over_core(own_low)
    if tuned:
        own_low, other_low = second.join(own_low, other_low)
    pieces = second.pieces()
    places = second.numbers()
    hidden, act, slope, ffn_part, ffn_send = ffn_forward(own_low, other_low, pieces, places, half_ff)
    layer_out, grad_second, own_branch, ffn_sums = second_norm(
        vec, first_norm, ffn_part, over_core(ffn_send), cotangent[0]
    )
    branch_other = over_core(own_branch)
    group = chip_ref if tuned else jnp.zeros_like(chip_ref)
    down_send = down_grad(1 - group, own_branch, branch_other, hidden)
    if tuned:
        down_send, own_branch, branch_other = tie(down_send, own_branch, branch_other)
        down_got = over_x(down_send)
    down_keep = down_grad(group, own_branch, branch_other, hidden)
    down_keep, own_branch, branch_other = tie(down_keep, own_branch, branch_other)
    *grad_pieces, normed_part, normed_send = ffn_backward(
        own_low, other_low, own_branch, branch_other, act, slope, pieces, places, half_ff
    )
    if tuned:
        normed_send, down_got, *grad_pieces = tie(normed_send, down_got, *grad_pieces)
        grad_pieces = add_last(places, grad_pieces, down_keep, down_got)
    else:
        shard_rows = width // 8
        grad_pieces = [
            jnp.concatenate(
                [piece[:-1], down_keep[None, i * shard_rows : (i + 1) * shard_rows],
                 down_send[None, i * shard_rows : (i + 1) * shard_rows]]
            )
            for i, piece in enumerate(grad_pieces)
        ]
    reduce_ffn = (LateReduce if tuned else PlainReduce)(grad_pieces)
    (normed_send,) = reduce_ffn.first(normed_send)
    grad_first, low_mine, low_theirs, back_mine, back_theirs, attn_sums = first_norm_back(
        core_ref, vec, full_out, grad_second, normed_part, over_core(normed_send),
        first_normed, first_inverse,
    )
    back_other = over_core(back_theirs)
    low_other = over_core(low_theirs)

    if tuned:
        back_ref = jnp.stack((chip, core == chip)).astype(jnp.int32)
        def reach_part(low, count, into):
            return attention_backward(
                reach_blocks, back_ref, queries_reach, keys_values, attended_reach, back_other, back_mine,
                lse_reach, seg_reach, tags_reach, slopes, None, low, count, into, kv_beyond,
            )

        low_all = ordered(core, low_mine, low_other, 0)
        pairs = half // (2 * HD)
        reached = reduce_ffn.join(*reach_part(0, 1, ()))
        reached = reduce_ffn.second(*reached)
        dq_reach, dkv_reach, beyond = reach_part(1, pairs - 1, tuple(reached))
        dq_reach, dkv_reach, beyond, low_all = tie(dq_reach, dkv_reach, beyond, low_all)
        beyond = over_x(beyond)
        grad_w_out = dot_tn(attended_all, low_all)
        dq_reach, dkv_reach, grad_w_out = reduce_ffn.join(dq_reach, dkv_reach, grad_w_out)
        dq_reach, dkv_reach, grad_w_out = reduce_ffn.third(dq_reach, dkv_reach, grad_w_out)
        dq_local, dkv_local = attention_backward(
            local_blocks, back_ref, queries_local, keys_values, attended_local,
            back_mine, back_other, lse_local, seg_local, tags_local, slopes, dkv_reach,
        )
        dq_local, dkv_local, beyond = reduce_ffn.join(dq_local, dkv_local, beyond)
        reduce_ffn.fourth()
    else:
        grad_attended = ordered(core, back_mine, back_other, 0)
        back_ref = jnp.ones((2,), jnp.int32)
        backward_parts = [
            attention_backward(
                reach_blocks, back_ref, queries[i * rows : (i + 1) * rows], kv_wide[low:high],
                forward_parts[i][0], grad_attended[i * rows : (i + 1) * rows],
                grad_attended[i * rows : (i + 1) * rows], forward_parts[i][1],
                seg_row[:, i * rows : (i + 1) * rows], tags_wide[low:high], slopes, None,
            )
            for i, (low, high) in enumerate(spans)
        ]
        dq_local, dq_reach = [part[0] for part in backward_parts]
        reach_0, reach_1 = [part[1] for part in backward_parts]
        from_next = from_next_chip(reach_0[:, :HALF].astype(jnp.bfloat16)).astype(jnp.float32)
        from_previous = from_previous_chip(reach_1[:, rows + HALF :].astype(jnp.bfloat16)).astype(jnp.float32)
        centre = jnp.pad(reach_0[:, HALF:], ((0, 0), (0, 2 * rows - reach_0.shape[1] + HALF), (0, 0)))
        centre = centre + jnp.pad(
            reach_1[:, : rows + HALF], ((0, 0), (2 * rows - rows - HALF, 0), (0, 0))
        )
        centre = centre.at[:, 2 * rows - HALF :].add(from_next)
        dkv_local = centre.at[:, :HALF].add(from_previous)
        beyond = jnp.zeros_like(from_next, dtype=jnp.bfloat16)
        grad_w_out = dot_tn(attended_all, ordered(core, low_mine, low_other, 0))
    *grad_last, grad_qkv = last_grads(
        places, spot, inputs_all, dq_local, dq_reach, dkv_local, beyond, grad_w_out.astype(jnp.bfloat16),
        attn_sums, ffn_sums,
    )
    last = row_reduce(grad_last)
    last.first()
    if tuned:
        reduce_ffn.part(0, 1)
        last.pieces = last.join(*last.pieces)
        last.pieces = reduce_ffn.last_y(*last.pieces)
    last.second()
    input_part = dot_nt(grad_qkv, full_qkv)
    grad_inputs = (
        grad_first
        + cut(input_part, core, rows, 0)
        + over_core(cut(input_part, 1 - core, rows, 0).astype(jnp.bfloat16)).astype(jnp.float32)
    )
    ffn_mine = reduce_ffn.result()
    if tuned:
        got = over_x(ffn_mine)
        ffn_mine = jnp.concatenate(
            [ffn_mine[:-1] + got[:-1], ordered(chip, ffn_mine[-1:], got[-1:], 0)], axis=0
        )
    else:
        ffn_mine = chips_sum(ffn_mine)
    (grad_inputs,) = last.join(grad_inputs)
    last.third()
    last.join()
    last.fourth()
    grad_up, grad_gate, grad_down = lay_out(core_ref, ffn_mine, over_core(ffn_mine))
    if tuned:
        grad_up, grad_gate, grad_down = last.join(grad_up, grad_gate, grad_down)
    last_mine = chips_sum(last.result())[0]
    last_rows, vector_rows = finish(core_ref, last_mine, over_core(last_mine))

    return (
        layer_out[None],
        grad_inputs[None],
        *last_rows,
        grad_up,
        grad_gate,
        grad_down,
    ) + tuple(row[0] for row in vector_rows)


def solution(mesh):
    rows_spec = P("fsdp", "ctx", None)
    in_specs = (
        (rows_spec, P("fsdp", "ctx"), P("fsdp", "ctx"))
        + (P("fsdp", None),) * 7
        + (P("fsdp"),) * VECTORS
        + (rows_spec,)
    )
    out_specs = (rows_spec, rows_spec) + (P("fsdp", None),) * 7 + (P("fsdp"),) * VECTORS
    return jax.shard_map(
        on_device, mesh=mesh, in_specs=in_specs, out_specs=out_specs, check_vma=False
    )
```

```python
import math
import jax
import jax.numpy as jnp
from jax import lax
from jax.experimental import pallas as pl
from jax.experimental.pallas import tpu as pltpu
from jax.sharding import PartitionSpec as P

H = 12
HD = 64
FF = 3072
HALF = 512
EPSILON = 1e-06
VECTORS = 8
QB = 256
ROW_BLOCK = 1024
SPAN = QB + 2 * HALF
BIG = 1e30
MIB = 1024 * 1024
SHORT = pl.CostEstimate(flops=1024, bytes_accessed=1024, transcendentals=0)

Z_SWAP = ((0, 1), (1, 0), (2, 3), (3, 2))
Z_MID = ((1, 2), (2, 1))
Z_OUT = ((1, 0), (2, 3))
Z_IN = ((0, 1), (3, 2))


def dot_nn(a, b):
    return lax.dot_general(a, b, (((1,), (0,)), ((), ())), preferred_element_type=jnp.float32)


def dot_nt(a, b):
    return lax.dot_general(a, b, (((1,), (1,)), ((), ())), preferred_element_type=jnp.float32)


def dot_tn(a, b):
    return lax.dot_general(a, b, (((0,), (0,)), ((), ())), preferred_element_type=jnp.float32)


def tie(*values):
    return lax.optimization_barrier(values)


def head_slopes(number):
    power_two = 2 ** int(math.floor(math.log2(number)))
    first_part = [2.0 ** (-8.0 * (position + 1) / power_two) for position in range(power_two)]
    extra_part = [
        2.0 ** (-8.0 * (2 * position + 1) / (2 * power_two))
        for position in range(number - power_two)
    ]
    return jnp.array(first_part + extra_part, dtype=jnp.float32)


def over_core(x):
    count = lax.axis_size("ctx")
    return lax.ppermute(x, "ctx", [(i, i ^ 1) for i in range(count)])


def from_previous_chip(x):
    count = lax.axis_size("ctx")
    return lax.ppermute(x, "ctx", [(i, i + 2) for i in range(count - 2)])


def from_next_chip(x):
    count = lax.axis_size("ctx")
    return lax.ppermute(x, "ctx", [(i + 2, i) for i in range(count - 2)])


def over_x(x):
    return lax.ppermute(x, "ctx", [(i, i ^ 2) for i in range(4)])


def over_y(x):
    return lax.ppermute(x, "fsdp", [(i, i ^ 1) for i in range(8)])


def over_z(x, moves):
    return lax.ppermute(
        x, "fsdp", [(2 * a + y, 2 * b + y) for a, b in moves for y in range(2)]
    )


def ordered(core, own, other, axis):
    return jnp.where(
        core == 0,
        jnp.concatenate([own, other], axis=axis),
        jnp.concatenate([other, own], axis=axis),
    )


def shard_number(k, dy):
    me = lax.axis_index("fsdp")
    return me ^ (2 * k + dy)


class Chain:
    live = ()

    def join(self, *values):
        held = tie(*[getattr(self, name) for name in self.live], *values)
        for name, value in zip(self.live, held):
            setattr(self, name, value)
        return held[len(self.live) :]


class Gather(Chain):
    def __init__(self, piece):
        self.own = piece

    def first_z(self):
        self.a = over_z(self.own, Z_SWAP)
        self.b = over_z(self.own, Z_MID)

    def first_y(self):
        self.y0 = over_y(self.own)
        self.live = ("y0", "a", "b")

    def first(self):
        self.first_z()
        self.first_y()

    def second(self, *values):
        self.a, self.b, *values = tie(self.a, self.b, *values)
        self.c = over_z(self.a, Z_MID)
        self.d = over_z(self.b, Z_OUT)
        self.ya = over_y(self.a)
        self.live = ("c", "d", "ya")
        return values

    def third(self, *values):
        self.z2, *values = tie(self.c + self.d, *values)
        self.e = over_z(self.c, Z_OUT)
        self.yz2 = over_y(self.z2)
        self.live = ("e", "yz2")
        return values

    def fourth(self, *values):
        self.z3, *values = tie(self.b + self.e, *values)
        self.yz3 = over_y(self.z3)
        self.live = ("yz3",)
        return values

    def pieces(self):
        return [self.own, self.a, self.z2, self.z3, self.y0, self.ya, self.yz2, self.yz3]

    def numbers(self):
        return jnp.stack([shard_number(k, dy) for dy in range(2) for k in range(4)])


class Reduce(Chain):
    def __init__(self, pieces):
        self.pieces = pieces

    def part(self, k, dy):
        return self.pieces[4 * dy + k]

    def first(self, *values):
        send, *values = tie(self.part(3, 1), *values)
        self.y = over_y(send)
        self.live = ("y",)
        return values

    def second(self, *values):
        self.q3, send, *values = tie(self.part(3, 0) + self.y, self.part(2, 1), *values)
        self.y = over_y(send)
        self.e = over_z(self.q3, Z_IN)
        self.live = ("y", "e")
        return values

    def third(self, *values):
        q2 = self.part(2, 0) + self.y
        self.q2, on, send, *values = tie(q2, q2 + self.e, self.part(1, 1), *values)
        self.y = over_y(send)
        self.d = over_z(self.q2, Z_IN)
        self.c = over_z(on, Z_MID)
        self.live = ("y", "d", "c")
        return values

    def fourth(self, *values):
        on_b, on_a, send, *values = tie(
            self.q3 + self.d, self.part(1, 0) + self.y + self.c, self.part(0, 1), *values
        )
        self.y = over_y(send)
        self.b = over_z(on_b, Z_MID)
        self.a = over_z(on_a, Z_SWAP)
        self.live = ("y", "b", "a")
        return values

    def result(self):
        return self.part(0, 0) + self.y + self.a + self.b


class LateReduce(Reduce):
    def fourth(self, *values):
        on_b, on_a, *values = tie(
            self.q3 + self.d, self.part(1, 0) + self.y + self.c, *values
        )
        self.b = over_z(on_b, Z_MID)
        self.a = over_z(on_a, Z_SWAP)
        return values

    def last_y(self, *values):
        send, *values = tie(self.part(0, 1), *values)
        self.y = over_y(send)
        self.live = ("y", "b", "a")
        return values


class PlainGather(Chain):
    def __init__(self, piece):
        self.own = piece

    def first(self, *values):
        return values

    first_z = first_y = second = third = fourth = first

    def pieces(self):
        whole = lax.all_gather(self.own, "fsdp", axis=0, tiled=True)
        rows = whole.shape[0] // 8
        return [whole[i * rows : (i + 1) * rows] for i in range(8)]

    def numbers(self):
        return jnp.arange(8, dtype=jnp.int32)


class PlainReduce(Chain):
    def __init__(self, pieces):
        self.full = jnp.concatenate(pieces, axis=1)

    def first(self, *values):
        return values

    second = third = fourth = first

    def result(self):
        return lax.psum_scatter(self.full, "fsdp", scatter_dimension=1, tiled=True)


def chips_sum(total):
    count = lax.axis_size("ctx")
    if count == 4:
        return total + over_x(total)
    core = lax.axis_index("ctx") % 2
    slots = jnp.stack(
        [jnp.where(core == i, total, jnp.zeros_like(total)) for i in range(2)]
    )
    return lax.dynamic_index_in_dim(lax.psum(slots, "ctx"), core, 0, keepdims=False)


def local_blocks(chip):
    return (
        (pl.multiple_of(chip * QB, QB), pl.multiple_of(chip * QB, QB), HALF + QB, chip * HALF),
        (pl.multiple_of((1 - chip) * QB, QB), 0, 2 * HALF, QB + chip * QB),
    )


def reach_blocks(chip):
    return ((0, 0, SPAN, HALF), (QB, QB, SPAN, HALF))


def rows_at(start, count):
    return pl.ds(start, count)


def both_chips(chip, local_ref, beyond_ref, all_ref):
    own = local_ref.shape[0]
    count = beyond_ref.shape[0]
    all_ref[rows_at(pl.multiple_of(chip * count, count), own), :] = local_ref[...]
    all_ref[rows_at(pl.multiple_of((1 - chip) * own, count), count), :] = beyond_ref[...]


def fill_distance(dist, block, seg_ref, tag_ref):
    q_at, k_at, span, shift = block
    key_pos = lax.broadcasted_iota(jnp.int32, (span, QB), 0)
    row_pos = lax.broadcasted_iota(jnp.int32, (span, QB), 1) + shift
    gap = jnp.abs(key_pos - row_pos)
    same = tag_ref[rows_at(k_at, span), :] == seg_ref[:, rows_at(q_at, QB)]
    kept = ((gap <= HALF) & same) | (gap == 0)
    dist[...] = jnp.where(kept, gap.astype(jnp.float32), BIG)


def attn_fwd_kernel(
    plan, chip, slopes, q_ref, k_ref, v_ref, seg_ref, tag_ref, k_else, v_else, out_ref, lse_ref, *dists
):
    pair = pl.program_id(0)
    blocks = plan(chip[0])
    if k_else is not None:
        *dists, k_all, v_all = dists
        both_chips(chip[0], k_ref, k_else, k_all)
        both_chips(chip[0], v_ref, v_else, v_all)
        k_ref, v_ref = k_all, v_all

    @pl.when(pair == 0)
    def _():
        for dist, block in zip(dists, blocks):
            fill_distance(dist, block, seg_ref, tag_ref)

    lane = lax.broadcasted_iota(jnp.int32, (QB, 2 * HD), 1)
    work = [(dist, block, a) for dist, block in zip(dists, blocks) for a in range(2)]

    def raw_scores(item):
        dist, (q_at, k_at, span, shift), a = item
        q = q_ref[rows_at(q_at, QB), :]
        mine = (lane >= HD) if a else (lane < HD)
        q_a = jnp.where(mine, q, jnp.zeros_like(q)) * jnp.asarray(1.0 / math.sqrt(HD), q.dtype)
        return dot_nt(k_ref[rows_at(k_at, span), :], q_a)

    ahead = raw_scores(work[0])
    parts = []
    for i, (dist, (q_at, k_at, span, shift), a) in enumerate(work):
        raw = ahead
        if i + 1 < len(work):
            ahead = raw_scores(work[i + 1])
        if a == 0:
            v_t = v_ref[rows_at(k_at, span), :].T
            parts = []
        s = raw - slopes[2 * pair + a] * dist[...]
        top = jnp.max(s, axis=0, keepdims=True)
        p = jnp.exp(s - top)
        total = jnp.sum(p, axis=0, keepdims=True)
        o_t = dot_nn(v_t[a * HD : (a + 1) * HD, :], p.astype(jnp.bfloat16))
        parts.append(o_t * (1.0 / total))
        lse_ref[0, a : a + 1, rows_at(q_at, QB)] = top + jnp.log(total)
        if a == 1:
            out_ref[rows_at(q_at, QB), :] = jnp.concatenate(parts, axis=0).T.astype(jnp.bfloat16)


def distances(plan):
    return [pltpu.VMEM((block[2], QB), jnp.float32) for block in plan(0)]


def attention_forward(plan, chip, queries, keys_values, seg_row, tag_col, slopes, beyond=None):
    rows, width = queries.shape
    ext = tag_col.shape[0]
    own = keys_values.shape[0]
    more = () if beyond is None else (beyond, beyond)
    pairs = width // (2 * HD)

    def body(*refs):
        if beyond is None:
            refs = refs[:7] + (None, None) + refs[7:]
        attn_fwd_kernel(plan, *refs)

    return pl.pallas_call(
        body,
        grid=(pairs,),
        in_specs=[
            pl.BlockSpec(memory_space=pltpu.SMEM),
            pl.BlockSpec(memory_space=pltpu.SMEM),
            pl.BlockSpec((rows, 2 * HD), lambda h: (0, h)),
            pl.BlockSpec((own, 2 * HD), lambda h: (0, h)),
            pl.BlockSpec((own, 2 * HD), lambda h: (0, pairs + h)),
            pl.BlockSpec((1, rows), lambda h: (0, 0)),
            pl.BlockSpec((ext, 1), lambda h: (0, 0)),
        ]
        + [
            pl.BlockSpec((ext - own, 2 * HD), lambda h, t=t: (0, t * pairs + h))
            for t in range(len(more))
        ],
        out_specs=[
            pl.BlockSpec((rows, 2 * HD), lambda h: (0, h)),
            pl.BlockSpec((1, 8, rows), lambda h: (h, 0, 0)),
        ],
        out_shape=[
            jax.ShapeDtypeStruct((rows, width), jnp.bfloat16),
            jax.ShapeDtypeStruct((pairs, 8, rows), jnp.float32),
        ],
        scratch_shapes=distances(plan) + [pltpu.VMEM((ext, 2 * HD), jnp.bfloat16)] * len(more),
        compiler_params=pltpu.CompilerParams(vmem_limit_bytes=56 * MIB),
        cost_estimate=SHORT,
    )(chip, slopes, queries, keys_values, keys_values, seg_row, tag_col, *more)


def attn_bwd_kernel(
    plan, low, chip, slopes, q_ref, k_ref, v_ref, o_ref, do_ref, do_else_ref, lse_ref, seg_ref, tag_ref, start_ref,
    k_else, v_else, dq_ref, dkv_ref, beyond_ref, *dists,
):
    step = pl.program_id(0)
    pair = step + low
    blocks = plan(chip[0])
    if k_else is not None:
        *dists, k_all, v_all = dists
        both_chips(chip[0], k_ref, k_else, k_all)
        both_chips(chip[0], v_ref, v_else, v_all)
        k_ref, v_ref = k_all, v_all

    @pl.when(step == 0)
    def _():
        for dist, block in zip(dists, blocks):
            fill_distance(dist, block, seg_ref, tag_ref)

    lane = lax.broadcasted_iota(jnp.int32, (QB, 2 * HD), 1)
    scale = 1.0 / math.sqrt(HD)
    if start_ref is None:
        dkv_ref[...] = jnp.zeros_like(dkv_ref)
    else:
        count = dkv_ref.shape[1]
        dkv_ref[...] = start_ref[:, rows_at(pl.multiple_of(chip[0] * HALF, HALF), count), :]
    for dist, (q_at, k_at, span, shift) in zip(dists, blocks):
        q = q_ref[rows_at(q_at, QB), :] * jnp.asarray(scale, jnp.bfloat16)
        do = jnp.where(chip[1] == 1, do_ref[rows_at(q_at, QB), :], do_else_ref[rows_at(q_at, QB), :])
        k = k_ref[rows_at(k_at, span), :]
        v = v_ref[rows_at(k_at, span), :]
        k_t = k.T
        mixed_t = (do.astype(jnp.float32) * o_ref[rows_at(q_at, QB), :].astype(jnp.float32)).T
        parts = []
        ps = []
        dss = []
        qs = []
        dos = []
        for a in range(2):
            mine = (lane >= HD) if a else (lane < HD)
            q_a = jnp.where(mine, q, jnp.zeros_like(q))
            do_a = jnp.where(mine, do, jnp.zeros_like(do))
            delta = jnp.sum(mixed_t[a * HD : (a + 1) * HD, :], axis=0, keepdims=True)
            s = dot_nt(k, q_a) - slopes[2 * pair + a] * dist[...]
            p = jnp.exp(s - lse_ref[0, a : a + 1, rows_at(q_at, QB)])
            dp = dot_nt(v, do_a)
            ds = (p * (dp - delta)).astype(jnp.bfloat16)
            parts.append(dot_nn(k_t[a * HD : (a + 1) * HD, :], ds) * scale)
            ps.append(p.astype(jnp.bfloat16))
            dss.append(ds)
            qs.append(q_a)
            dos.append(do_a)
        dq_ref[rows_at(q_at, QB), :] = jnp.concatenate(parts, axis=0).T.astype(jnp.bfloat16)
        dkv_ref[0, rows_at(k_at, span), :] += dot_nn(
            jnp.concatenate(dss, axis=1), jnp.concatenate(qs, axis=0)
        )
        dkv_ref[1, rows_at(k_at, span), :] += dot_nn(
            jnp.concatenate(ps, axis=1), jnp.concatenate(dos, axis=0)
        )
    if beyond_ref is not None:
        other = pl.multiple_of((1 - chip[0]) * 2 * HALF, HALF)
        beyond_ref[...] = dkv_ref[:, rows_at(other, HALF), :].astype(jnp.bfloat16)


def attention_backward(
    plan, chip, queries, keys_values, attended, grad_if, grad_else, lse, seg_row, tag_col, slopes, start,
    low=0, count=None, into=(), beyond=None,
):
    rows, width = queries.shape
    ext = tag_col.shape[0]
    own = keys_values.shape[0]
    more = () if beyond is None else (beyond, beyond)
    pairs = width // (2 * HD)
    count = pairs if count is None else count
    inner = pl.BlockSpec((rows, 2 * HD), lambda h: (0, low + h))
    starts = () if start is None else (start,)

    def body(*refs):
        refs = list(refs)
        fixed, refs = refs[:11], refs[11:]
        begin = refs.pop(0) if starts else None
        others = [refs.pop(0) for _ in more] or [None, None]
        refs = refs[len(into) :]
        outs, refs = refs[: 3 - len(starts)], refs[3 - len(starts) :]
        outs += [None] * len(starts)
        attn_bwd_kernel(plan, low, *fixed, begin, *others, *outs, *refs)

    return pl.pallas_call(
        body,
        grid=(count,),
        in_specs=[
            pl.BlockSpec(memory_space=pltpu.SMEM),
            pl.BlockSpec(memory_space=pltpu.SMEM),
            inner,
            pl.BlockSpec((own, 2 * HD), lambda h: (0, low + h)),
            pl.BlockSpec((own, 2 * HD), lambda h: (0, pairs + low + h)),
            inner,
            inner,
            inner,
            pl.BlockSpec((1, 8, rows), lambda h: (low + h, 0, 0)),
            pl.BlockSpec((1, rows), lambda h: (0, 0)),
            pl.BlockSpec((ext, 1), lambda h: (0, 0)),
        ]
        + [pl.BlockSpec((2, s.shape[1], 2 * HD), lambda h: (0, 0, low + h)) for s in starts]
        + [
            pl.BlockSpec((ext - own, 2 * HD), lambda h, t=t: (0, t * pairs + low + h))
            for t in range(len(more))
        ]
        + [pl.BlockSpec(memory_space=pl.ANY)] * len(into),
        out_specs=[inner, pl.BlockSpec((2, ext, 2 * HD), lambda h: (0, 0, low + h))]
        + [pl.BlockSpec((2, HALF, 2 * HD), lambda h: (0, 0, low + h))] * (1 - len(starts)),
        out_shape=[
            jax.ShapeDtypeStruct((rows, width), jnp.bfloat16),
            jax.ShapeDtypeStruct((2, ext, width), jnp.float32),
        ]
        + [jax.ShapeDtypeStruct((2, HALF, width), jnp.bfloat16)] * (1 - len(starts)),
        input_output_aliases={11 + len(starts) + len(more) + i: i for i in range(len(into))},
        scratch_shapes=distances(plan) + [pltpu.VMEM((ext, 2 * HD), jnp.bfloat16)] * len(more),
        compiler_params=pltpu.CompilerParams(vmem_limit_bytes=56 * MIB),
        cost_estimate=SHORT,
    )(
        chip, slopes, queries, keys_values, keys_values, attended, grad_if, grad_else, lse,
        seg_row, tag_col, *starts, *more, *into,
    )


def norm_parts(values, gain_vec, offset):
    centred = values - jnp.mean(values, axis=-1, keepdims=True)
    variance = jnp.mean(centred * centred, axis=-1, keepdims=True)
    inverse = lax.rsqrt(variance + EPSILON)
    normed = centred * inverse
    return (normed * gain_vec + offset, normed, inverse)


def project_kernel(
    place_numbers, spot, x_ref, *refs
):
    pieces = refs[:8]
    vec_ref, w_ref, out_ref, local_ref, reach_ref, kv_ref, send_ref, weight = refs[8:]
    core, chip = spot[0], spot[1]
    fill_weight(place_numbers, pieces, weight)
    half = out_ref.shape[1]
    rows = local_ref.shape[0]
    w_ref[...] = weight[:, : 3 * half]
    out_ref[...] = weight[:, 3 * half : 4 * half]
    vec = weight[:, 4 * half :].astype(jnp.float32).T[:VECTORS, :]
    vec_ref[...] = vec
    projected = dot_nn(x_ref[...], weight[:, : 3 * half])

    def bias(i):
        return jnp.where(core == 0, vec[i : i + 1, :half], vec[i : i + 1, half:])

    queries = (projected[:, :half] + bias(0)).astype(jnp.bfloat16)
    first = chip == 0
    local_ref[...] = jnp.where(first, queries[:rows], queries[rows:])
    reach_ref[...] = jnp.where(first, queries[rows:], queries[:rows])
    keys = projected[:, half : 2 * half].astype(jnp.bfloat16)
    values = (projected[:, 2 * half :] + bias(1)).astype(jnp.bfloat16)
    kv_ref[:, :half] = keys
    kv_ref[:, half:] = values
    send_ref[:, :half] = jnp.where(first, keys[rows:], keys[:rows])
    send_ref[:, half:] = jnp.where(first, values[rows:], values[:rows])


def project(numbers, spot, x, pieces):
    all_rows, width = x.shape
    half = width // 2
    rows = all_rows // 2
    whole = pl.BlockSpec(memory_space=pltpu.VMEM)
    smem = pl.BlockSpec(memory_space=pltpu.SMEM)
    low = jnp.bfloat16
    return pl.pallas_call(
        project_kernel,
        in_specs=[smem, smem] + [whole] * 9,
        out_specs=[whole] * 7,
        out_shape=[
            jax.ShapeDtypeStruct((VECTORS, width), jnp.float32),
            jax.ShapeDtypeStruct((width, 3 * half), low),
            jax.ShapeDtypeStruct((width, half), low),
            jax.ShapeDtypeStruct((rows, half), low),
            jax.ShapeDtypeStruct((rows, half), low),
            jax.ShapeDtypeStruct((all_rows, width), low),
            jax.ShapeDtypeStruct((rows, width), low),
        ],
        scratch_shapes=[pltpu.VMEM((width, pieces[0].shape[1]), low)],
        compiler_params=pltpu.CompilerParams(vmem_limit_bytes=56 * MIB),
        cost_estimate=SHORT,
    )(numbers, spot, x, *pieces)


def first_norm_kernel(
    core, vec_ref, attended_ref, mine_ref, other_ref, x_ref,
    norm_ref, normed_ref, inverse_ref, low_ref, w_ref,
):
    half = mine_ref.shape[1]
    rows = norm_ref.shape[0]
    first = core[0] == 0

    @pl.when(pl.program_id(0) == 0)
    def _():
        w_ref[:, :half] = jnp.where(first, mine_ref[...], other_ref[...])
        w_ref[:, half:] = jnp.where(first, other_ref[...], mine_ref[...])

    at = pl.multiple_of(core[0] * rows * pl.num_programs(0) + pl.program_id(0) * rows, rows)
    branch = dot_nn(attended_ref[pl.ds(at, rows), :], w_ref[...]) + vec_ref[2:3, :]
    norm, normed, inverse = norm_parts(
        x_ref[...].astype(jnp.float32) + branch, vec_ref[4:5, :], vec_ref[5:6, :]
    )
    norm_ref[...] = norm
    normed_ref[...] = normed
    inverse_ref[...] = inverse
    low_ref[...] = norm.astype(jnp.bfloat16)


def first_norm_of(core, vec, attended, mine, other, x):
    rows, width = x.shape
    steps = 2
    block = pl.BlockSpec((rows // steps, width), lambda i: (i, 0))

    def all_of(a):
        return pl.BlockSpec(a.shape, lambda i: (0, 0))

    return pl.pallas_call(
        first_norm_kernel,
        grid=(steps,),
        in_specs=[pl.BlockSpec(memory_space=pltpu.SMEM)]
        + [all_of(a) for a in (vec, attended, mine, other)]
        + [block],
        out_specs=[
            block, block, pl.BlockSpec((rows // steps, 1), lambda i: (i, 0)), block,
            pl.BlockSpec((width, width), lambda i: (0, 0)),
        ],
        out_shape=[
            jax.ShapeDtypeStruct((rows, width), jnp.float32),
            jax.ShapeDtypeStruct((rows, width), jnp.float32),
            jax.ShapeDtypeStruct((rows, 1), jnp.float32),
            jax.ShapeDtypeStruct((rows, width), jnp.bfloat16),
            jax.ShapeDtypeStruct((width, width), jnp.bfloat16),
        ],
        compiler_params=pltpu.CompilerParams(vmem_limit_bytes=56 * MIB),
        cost_estimate=SHORT,
    )(core, vec, attended, mine, other, x)


def norm_back(upstream, normed, inverse, gain_vec):
    scaled = upstream * gain_vec
    row_inner = (
        scaled
        - jnp.mean(scaled, axis=-1, keepdims=True)
        - normed * jnp.mean(scaled * normed, axis=-1, keepdims=True)
    )
    return row_inner * inverse


def last_grads_kernel(
    numbers, spot, x_ref, local_ref, reach_ref, dkv_ref, beyond_ref, out_w_ref, attn_ref, ffn_ref, *refs
):
    *pieces, grad_ref, last_ref = refs
    core, chip = spot[0], spot[1]
    first = chip == 0
    rows, half = local_ref.shape
    grad_ref[:rows, :half] = jnp.where(first, local_ref[...], reach_ref[...])
    grad_ref[rows:, :half] = jnp.where(first, reach_ref[...], local_ref[...])
    for t in range(2):
        got = beyond_ref[t].astype(jnp.float32)
        part = slice((t + 1) * half, (t + 2) * half)
        top = dkv_ref[t, :rows, :] + jnp.where(first, 0.0, got)
        low = dkv_ref[t, rows:, :] + jnp.where(first, got, 0.0)
        grad_ref[:rows, part] = top.astype(jnp.bfloat16)
        grad_ref[rows:, part] = low.astype(jnp.bfloat16)
    grads = grad_ref[...]
    last_ref[:, : 3 * half] = dot_tn(x_ref[...], grads).astype(jnp.bfloat16)
    last_ref[:, 3 * half : 4 * half] = out_w_ref[...]
    sums = [
        jnp.sum(grads[:, i * half : (i + 1) * half].astype(jnp.float32), axis=0, keepdims=True)
        for i in (0, 2)
    ]
    nothing = jnp.zeros_like(sums[0])
    vectors = [
        jnp.where(
            core == 0, jnp.concatenate([s, nothing], axis=1), jnp.concatenate([nothing, s], axis=1)
        )
        for s in sums
    ]
    vectors += [attn_ref[2:3, :], ffn_ref[2:3, :], attn_ref[0:2, :], ffn_ref[0:2, :]]
    vectors.append(jnp.zeros((128 - VECTORS, 2 * half), jnp.float32))
    last_ref[:, 4 * half :] = jnp.concatenate(vectors, axis=0).T.astype(jnp.bfloat16)
    for i, piece in enumerate(pieces):
        piece[0] = last_ref[shard_rows(numbers, i, piece), :]


def last_grads(numbers, spot, x, dq_local, dq_reach, dkv, beyond, grad_w_out, attn_sums, ffn_sums):
    all_rows, width = x.shape
    half = width // 2
    whole = pl.BlockSpec(memory_space=pltpu.VMEM)
    return pl.pallas_call(
        last_grads_kernel,
        in_specs=[pl.BlockSpec(memory_space=pltpu.SMEM)] * 2 + [whole] * 8,
        out_specs=[whole] * 9,
        out_shape=[jax.ShapeDtypeStruct((1, width // 8, 4 * half + 128), jnp.bfloat16)] * 8
        + [jax.ShapeDtypeStruct((all_rows, 3 * half), jnp.bfloat16)],
        scratch_shapes=[pltpu.VMEM((width, 4 * half + 128), jnp.bfloat16)],
        compiler_params=pltpu.CompilerParams(vmem_limit_bytes=30 * MIB),
        cost_estimate=SHORT,
    )(numbers, spot, x, dq_local, dq_reach, dkv, beyond, grad_w_out, attn_sums, ffn_sums)


def input_part_kernel(core, grad_ref, w_ref, own_ref, send_ref):
    rows = own_ref.shape[0]
    for ref, which in ((send_ref, 1 - core[0]), (own_ref, core[0])):
        part = grad_ref[pl.ds(pl.multiple_of(which * rows, rows), rows), :]
        ref[...] = dot_nt(part, w_ref[...]).astype(ref.dtype)


def input_part(core, grads, weights):
    all_rows, columns = grads.shape
    width = weights.shape[0]
    whole = pl.BlockSpec(memory_space=pltpu.VMEM)
    return pl.pallas_call(
        input_part_kernel,
        in_specs=[pl.BlockSpec(memory_space=pltpu.SMEM), whole, whole],
        out_specs=[whole, whole],
        out_shape=[
            jax.ShapeDtypeStruct((all_rows // 2, width), jnp.float32),
            jax.ShapeDtypeStruct((all_rows // 2, width), jnp.bfloat16),
        ],
        compiler_params=pltpu.CompilerParams(vmem_limit_bytes=18 * MIB),
        cost_estimate=SHORT,
    )(core, grads, weights)


def finish_kernel(core, mine_ref, other_ref, *outs):
    first = core[0] == 0
    half = outs[0].shape[1] // 2
    for i, out in enumerate(outs[:4]):
        part = slice(i * half, (i + 1) * half)
        mine, other = mine_ref[:, part].astype(jnp.float32), other_ref[:, part].astype(jnp.float32)
        out[:, :half] = jnp.where(first, mine, other)
        out[:, half:] = jnp.where(first, other, mine)
    mine, other = mine_ref[:, 4 * half :], other_ref[:, 4 * half :]
    vectors = (mine.astype(jnp.float32) + other.astype(jnp.float32)).T
    for i, out in enumerate(outs[4:]):
        out[...] = vectors[i : i + 1, :]


def finish(core, mine, other):
    rows, columns = mine.shape
    width = (columns - 128) // 2
    whole = pl.BlockSpec(memory_space=pltpu.VMEM)
    results = pl.pallas_call(
        finish_kernel,
        in_specs=[pl.BlockSpec(memory_space=pltpu.SMEM)] + [whole] * 2,
        out_specs=[whole] * (4 + VECTORS),
        out_shape=[jax.ShapeDtypeStruct((rows, width), jnp.float32)] * 4
        + [jax.ShapeDtypeStruct((1, rows), jnp.float32)] * VECTORS,
        cost_estimate=SHORT,
    )(core, mine, other)
    return results[:4], results[4:]


def add_sums(step, sums_ref, *columns):
    rows = [jnp.sum(value, axis=0, keepdims=True) for value in columns]
    rows.append(jnp.zeros((8 - len(rows), sums_ref.shape[1]), jnp.float32))
    add_up(step, sums_ref, jnp.concatenate(rows, axis=0))


def second_norm_kernel(
    vec_ref, norm_ref, part_ref, sent_ref, cot_ref, out_ref, grad_ref, low_ref, sums_ref
):
    step = pl.program_id(0)
    bias, gain, shift = vec_ref[3:4, :], vec_ref[6:7, :], vec_ref[7:8, :]
    value = norm_ref[...] + part_ref[...] + sent_ref[...].astype(jnp.float32) + bias
    result, normed, inverse = norm_parts(value, gain, shift)
    out_ref[...] = result.astype(jnp.bfloat16)
    upstream = cot_ref[...].astype(jnp.float32)
    grad = norm_back(upstream, normed, inverse, gain)
    grad_ref[...] = grad
    low_ref[...] = grad.astype(jnp.bfloat16)
    add_sums(step, sums_ref, upstream * normed, upstream, grad)


def second_norm(vec, first_norm, part, sent, cotangent):
    rows, width = part.shape
    block = pl.BlockSpec((rows // 2, width), lambda i: (i, 0))
    eight = pl.BlockSpec((8, width), lambda i: (0, 0))
    return pl.pallas_call(
        second_norm_kernel,
        grid=(2,),
        in_specs=[eight] + [block] * 4,
        out_specs=[block] * 3 + [eight],
        out_shape=[
            jax.ShapeDtypeStruct((rows, width), jnp.bfloat16),
            jax.ShapeDtypeStruct((rows, width), jnp.float32),
            jax.ShapeDtypeStruct((rows, width), jnp.bfloat16),
            jax.ShapeDtypeStruct((8, width), jnp.float32),
        ],
        compiler_params=pltpu.CompilerParams(vmem_limit_bytes=14 * MIB),
        cost_estimate=SHORT,
    )(vec, first_norm, part, sent, cotangent)


def first_norm_back_kernel(
    core, vec_ref, w_ref, up_ref, part_ref, sent_ref, normed_ref, inverse_ref,
    grad_ref, low_mine, low_theirs, back_mine, back_theirs, sums_ref,
):
    step = pl.program_id(0)
    half = low_mine.shape[1]
    upstream = up_ref[...] + part_ref[...] + sent_ref[...].astype(jnp.float32)
    normed = normed_ref[...]
    grad = norm_back(upstream, normed, inverse_ref[...], vec_ref[4:5, :])
    grad_ref[...] = grad
    low = grad.astype(jnp.bfloat16)
    back = dot_nt(low, w_ref[...]).astype(jnp.bfloat16)
    first = core[0] == 0
    for value, mine, theirs in ((low, low_mine, low_theirs), (back, back_mine, back_theirs)):
        left, right = value[:, :half], value[:, half:]
        mine[...] = jnp.where(first, left, right)
        theirs[...] = jnp.where(first, right, left)
    add_sums(step, sums_ref, upstream * normed, upstream, grad)


def first_norm_back(core, vec, w_out, grad_second, part, sent, normed, inverse):
    rows, width = part.shape
    steps = 2
    block = pl.BlockSpec((rows // steps, width), lambda i: (i, 0))
    halves = pl.BlockSpec((rows // steps, width // 2), lambda i: (i, 0))
    eight = pl.BlockSpec((8, width), lambda i: (0, 0))
    return pl.pallas_call(
        first_norm_back_kernel,
        grid=(steps,),
        in_specs=[
            pl.BlockSpec(memory_space=pltpu.SMEM),
            eight,
            pl.BlockSpec((width, width), lambda i: (0, 0)),
        ]
        + [block] * 4
        + [pl.BlockSpec((rows // steps, 1), lambda i: (i, 0))],
        out_specs=[block] + [halves] * 4 + [eight],
        out_shape=[jax.ShapeDtypeStruct((rows, width), jnp.float32)]
        + [jax.ShapeDtypeStruct((rows, width // 2), jnp.bfloat16)] * 4
        + [jax.ShapeDtypeStruct((8, width), jnp.float32)],
        compiler_params=pltpu.CompilerParams(vmem_limit_bytes=18 * MIB),
        cost_estimate=SHORT,
    )(core, vec, w_out, grad_second, part, sent, normed, inverse)


def lay_out_kernel(core, mine_ref, other_ref, up_ref, gate_ref, down_ref):
    first = core[0] == 0
    count, shard_rows, width = mine_ref.shape
    groups = count // 3
    shards = width // shard_rows

    def both(i):
        mine, other = mine_ref[i].astype(jnp.float32), other_ref[i].astype(jnp.float32)
        return jnp.where(first, mine, other), jnp.where(first, other, mine)

    for g in range(groups):
        for c, value in enumerate(both(2 * groups + g)):
            at = (c * groups + g) * shard_rows
            down_ref[at : at + shard_rows, :] = value
        for t, out in ((0, up_ref), (1, gate_ref)):
            for c, value in enumerate(both(2 * g + t)):
                for s in range(shards):
                    at = ((s * 2 + c) * groups + g) * shard_rows
                    out[:, at : at + shard_rows] = value[:, s * shard_rows : (s + 1) * shard_rows]


def lay_out(core, mine, other):
    count, shard_rows, width = mine.shape
    columns = count // 3 * 2 * width
    whole = pl.BlockSpec(memory_space=pltpu.VMEM)
    return pl.pallas_call(
        lay_out_kernel,
        in_specs=[pl.BlockSpec(memory_space=pltpu.SMEM)] + [whole] * 2,
        out_specs=[whole] * 3,
        out_shape=[
            jax.ShapeDtypeStruct((shard_rows, columns), jnp.float32),
            jax.ShapeDtypeStruct((shard_rows, columns), jnp.float32),
            jax.ShapeDtypeStruct((count // 3 * 2 * shard_rows, width), jnp.float32),
        ],
        compiler_params=pltpu.CompilerParams(vmem_limit_bytes=14 * MIB),
        cost_estimate=SHORT,
    )(core, mine, other)


def phi_parts(v):
    cdf = 0.5 * (1.0 + lax.erf(v * math.sqrt(0.5)))
    density = jnp.exp(-0.5 * v * v) * (1.0 / math.sqrt(2.0 * math.pi))
    return cdf, cdf + v * density


def shard_rows(numbers, i, piece):
    rows = piece.shape[-2]
    return pl.ds(pl.multiple_of(numbers[i] * rows, rows), rows)


def fill_weight(numbers, pieces, weight):
    for i, piece in enumerate(pieces):
        weight[shard_rows(numbers, i, piece), :] = piece[...]


def add_up(step, total, out):
    @pl.when(step == 0)
    def _():
        total[...] = out

    @pl.when(step > 0)
    def _():
        total[...] += out


def ffn_fwd_kernel(numbers, own_ref, other_ref, *refs):
    ups, gates, downs = refs[:8], refs[8:16], refs[16:24]
    hid_ref, act_ref, slope_ref, part_ref, send_ref = refs[24:29]
    x_all, up_w, gate_w, down_w, total = refs[29:]
    step = pl.program_id(0)
    rows = own_ref.shape[0]

    @pl.when(step == 0)
    def _():
        x_all[:rows, :] = own_ref[...]
        x_all[rows:, :] = other_ref[...]

    fill_weight(numbers, ups, up_w)
    fill_weight(numbers, gates, gate_w)
    fill_weight(numbers, downs, down_w)
    columns = up_w.shape[1]
    piece = columns // 3
    for i in range(3):
        part = slice(i * piece, (i + 1) * piece)
        x = x_all[...]
        up = dot_nn(x, up_w[:, part])
        gate = dot_nn(x, gate_w[:, part])
        cdf, derivative = phi_parts(gate)
        act = gate * cdf
        hidden = (act * up).astype(jnp.bfloat16)
        hid_ref[:, part] = hidden
        act_ref[:, part] = act.astype(jnp.bfloat16)
        slope_ref[:, part] = (derivative * up).astype(jnp.bfloat16)
    add_up(step, total, dot_nn(hid_ref[...], down_w[...]))

    @pl.when(step == pl.num_programs(0) - 1)
    def _():
        part_ref[...] = total[:rows, :]
        send_ref[...] = total[rows:, :].astype(jnp.bfloat16)


def piece_specs(rows, width, columns):
    steps = columns // width
    return [
        pl.BlockSpec((rows, width), lambda f, t=t: (0, t * steps + f))
        for t in range(3)
        for i in range(8)
    ]


def ffn_forward(own, other, pieces, numbers, columns):
    rows, width = own.shape
    steps = columns // width
    wide = pl.BlockSpec((2 * rows, width), lambda f: (0, f))
    whole = pl.BlockSpec((rows, width), lambda f: (0, 0))
    return pl.pallas_call(
        ffn_fwd_kernel,
        grid=(steps,),
        in_specs=[pl.BlockSpec(memory_space=pltpu.SMEM), whole, whole]
        + piece_specs(pieces[0].shape[0], width, columns),
        out_specs=[wide, wide, wide, whole, whole],
        out_shape=[jax.ShapeDtypeStruct((2 * rows, columns), jnp.bfloat16)] * 3
        + [
            jax.ShapeDtypeStruct((rows, width), jnp.float32),
            jax.ShapeDtypeStruct((rows, width), jnp.bfloat16),
        ],
        scratch_shapes=[
            pltpu.VMEM((2 * rows, width), jnp.bfloat16),
            pltpu.VMEM((width, width), jnp.bfloat16),
            pltpu.VMEM((width, width), jnp.bfloat16),
            pltpu.VMEM((width, width), jnp.bfloat16),
            pltpu.VMEM((2 * rows, width), jnp.float32),
        ],
        compiler_params=pltpu.CompilerParams(vmem_limit_bytes=56 * MIB),
        cost_estimate=SHORT,
    )(numbers, own, other, *(pieces * 3))


def down_grad_kernel(group, branch_ref, branch_other_ref, hid_ref, grad_ref):
    rows = branch_ref.shape[0]
    total = dot_tn(hid_ref[:rows, :], branch_ref[...])
    grad_ref[...] = (total + dot_tn(hid_ref[rows:, :], branch_other_ref[...])).astype(jnp.bfloat16)


def down_grad(group, branch, branch_other, hidden):
    rows, width = branch.shape
    whole = pl.BlockSpec((rows, width), lambda i, group: (0, 0))
    return pl.pallas_call(
        down_grad_kernel,
        grid_spec=pltpu.PrefetchScalarGridSpec(
            num_scalar_prefetch=1,
            grid=(1,),
            in_specs=[
                whole, whole, pl.BlockSpec((2 * rows, width), lambda i, group: (0, group[0])),
            ],
            out_specs=pl.BlockSpec((width, width), lambda i, group: (0, 0)),
        ),
        out_shape=jax.ShapeDtypeStruct((width, width), jnp.bfloat16),
        compiler_params=pltpu.CompilerParams(vmem_limit_bytes=18 * MIB),
        cost_estimate=SHORT,
    )(group, branch, branch_other, hidden)


def add_last_kernel(numbers, *refs):
    keep_ref, got_ref = refs[8:10]
    for i, out_ref in enumerate(refs[10:]):
        shard = shard_rows(numbers, i, out_ref)
        out_ref[0] = keep_ref[shard, :] + got_ref[shard, :]


def add_last(numbers, pieces, keep, got):
    units, rows, width = pieces[0].shape
    whole = pl.BlockSpec(memory_space=pltpu.VMEM)
    return pl.pallas_call(
        add_last_kernel,
        grid=(1,),
        in_specs=[pl.BlockSpec(memory_space=pltpu.SMEM)]
        + [pl.BlockSpec(memory_space=pl.ANY)] * 8
        + [whole, whole],
        out_specs=[pl.BlockSpec((1, rows, width), lambda i: (units - 1, 0, 0))] * 8,
        out_shape=[jax.ShapeDtypeStruct(pieces[0].shape, pieces[0].dtype)] * 8,
        input_output_aliases={1 + i: i for i in range(8)},
        compiler_params=pltpu.CompilerParams(vmem_limit_bytes=56 * MIB),
        cost_estimate=SHORT,
    )(numbers, *pieces, keep, got)


def ffn_bwd_kernel(numbers, own_ref, other_ref, branch_ref, branch_other_ref, act_ref, slope_ref, *refs):
    ups, gates, downs = refs[:8], refs[8:16], refs[16:24]
    grad_refs, part_ref, send_ref = refs[24:32], refs[32], refs[33]
    x_all, branch_all, up_w, gate_w, down_w, total, up_grad, gate_grad = refs[34:]
    step = pl.program_id(0)
    rows = own_ref.shape[0]

    @pl.when(step == 0)
    def _():
        x_all[:rows, :] = own_ref[...]
        x_all[rows:, :] = other_ref[...]
        branch_all[:rows, :] = branch_ref[...]
        branch_all[rows:, :] = branch_other_ref[...]

    fill_weight(numbers, ups, up_w)
    fill_weight(numbers, gates, gate_w)
    fill_weight(numbers, downs, down_w)
    x = x_all[...]
    outs = []
    piece = up_w.shape[1] // 3
    for i in range(3):
        part = slice(i * piece, (i + 1) * piece)
        d_hidden = dot_nt(branch_all[...], down_w[part, :])
        d_up = (d_hidden * act_ref[:, part].astype(jnp.float32)).astype(jnp.bfloat16)
        d_gate = (d_hidden * slope_ref[:, part].astype(jnp.float32)).astype(jnp.bfloat16)
        outs.append(dot_nt(d_up, up_w[:, part]) + dot_nt(d_gate, gate_w[:, part]))
        up_grad[:, part] = dot_tn(x, d_up).astype(jnp.bfloat16)
        gate_grad[:, part] = dot_tn(x, d_gate).astype(jnp.bfloat16)
    for i, grad_ref in enumerate(grad_refs):
        shard = shard_rows(numbers, i, grad_ref)
        grad_ref[0] = up_grad[shard, :]
        grad_ref[1] = gate_grad[shard, :]
    add_up(step, total, outs[0] + outs[1] + outs[2])

    @pl.when(step == pl.num_programs(0) - 1)
    def _():
        part_ref[...] = total[:rows, :]
        send_ref[...] = total[rows:, :].astype(jnp.bfloat16)


def ffn_backward(own, other, branch, branch_other, act, slope, pieces, numbers, columns):
    rows, width = own.shape
    steps = columns // width
    wide = pl.BlockSpec((2 * rows, width), lambda f: (0, f))
    whole = pl.BlockSpec((rows, width), lambda f: (0, 0))
    return pl.pallas_call(
        ffn_bwd_kernel,
        grid=(steps,),
        in_specs=[pl.BlockSpec(memory_space=pltpu.SMEM)]
        + [whole] * 4
        + [wide] * 2
        + piece_specs(pieces[0].shape[0], width, columns),
        out_specs=[
            *[pl.BlockSpec((2, width // 8, width), lambda f: (f, 0, 0))] * 8,
            whole,
            whole,
        ],
        out_shape=[
            *[jax.ShapeDtypeStruct((2 * steps + 1, width // 8, width), jnp.bfloat16)] * 8,
            jax.ShapeDtypeStruct((rows, width), jnp.float32),
            jax.ShapeDtypeStruct((rows, width), jnp.bfloat16),
        ],
        scratch_shapes=[
            pltpu.VMEM((2 * rows, width), jnp.bfloat16),
            pltpu.VMEM((2 * rows, width), jnp.bfloat16),
            pltpu.VMEM((width, width), jnp.bfloat16),
            pltpu.VMEM((width, width), jnp.bfloat16),
            pltpu.VMEM((width, width), jnp.bfloat16),
            pltpu.VMEM((2 * rows, width), jnp.float32),
            pltpu.VMEM((width, width), jnp.bfloat16),
            pltpu.VMEM((width, width), jnp.bfloat16),
        ],
        compiler_params=pltpu.CompilerParams(vmem_limit_bytes=56 * MIB),
        cost_estimate=SHORT,
    )(numbers, own, other, branch, branch_other, act, slope, *(pieces * 3))


def pack_kernel(core, up_ref, gate_ref, down_ref, out_ref):
    first = core[0] == 0
    shard_rows = up_ref.shape[0]
    width = down_ref.shape[1]
    shards = width // shard_rows
    groups = down_ref.shape[0] // shard_rows // 2
    at = 0
    for ref in (up_ref, gate_ref):
        for g in range(groups):
            for s in range(shards):
                left = (s * 2 * groups + g) * shard_rows
                right = left + groups * shard_rows
                out_ref[:, at : at + shard_rows] = jnp.where(
                    first, ref[:, left : left + shard_rows], ref[:, right : right + shard_rows]
                )
                at += shard_rows
    for g in range(groups):
        top = g * shard_rows
        low = top + groups * shard_rows
        out_ref[:, at : at + width] = jnp.where(
            first, down_ref[top : top + shard_rows, :], down_ref[low : low + shard_rows, :]
        )
        at += width


def pack(core, up, gate, down):
    shard_rows = up.shape[0]
    width = down.shape[1]
    whole = pl.BlockSpec(memory_space=pltpu.VMEM)
    return pl.pallas_call(
        pack_kernel,
        in_specs=[pl.BlockSpec(memory_space=pltpu.SMEM)] + [whole] * 3,
        out_specs=whole,
        out_shape=jax.ShapeDtypeStruct(
            (shard_rows, up.shape[1] + down.shape[0] // shard_rows // 2 * width), jnp.bfloat16
        ),
        compiler_params=pltpu.CompilerParams(vmem_limit_bytes=56 * MIB),
        cost_estimate=SHORT,
    )(core, up, gate, down)


def pack_first_kernel(core, *refs):
    first = core[0] == 0
    half = refs[0].shape[1] // 2
    out_ref = refs[-1]
    for i, ref in enumerate(refs[:4]):
        out_ref[:, i * half : (i + 1) * half] = jnp.where(first, ref[:, :half], ref[:, half:])
    out_ref[:, 4 * half :] = refs[4][...]


def pack_first(core, matrices, vectors):
    rows, width = matrices[0].shape
    whole = pl.BlockSpec(memory_space=pltpu.VMEM)
    return pl.pallas_call(
        pack_first_kernel,
        in_specs=[pl.BlockSpec(memory_space=pltpu.SMEM)] + [whole] * 5,
        out_specs=whole,
        out_shape=jax.ShapeDtypeStruct((rows, 2 * width + vectors.shape[1]), jnp.bfloat16),
        cost_estimate=SHORT,
    )(core, *matrices, vectors)


def on_device(
    tokens, segments, padding,
    w_query, w_key, w_value, w_out, w_up, w_gate, w_down,
    bias_query, bias_value, bias_out, bias_down, gain_attn, shift_attn, gain_ffn, shift_ffn,
    cotangent,
):
    tuned = lax.axis_size("ctx") == 4 and lax.axis_size("fsdp") == 8
    row_gather, row_reduce = (Gather, Reduce) if tuned else (PlainGather, PlainReduce)
    core = lax.axis_index("ctx") % 2
    chip = lax.axis_index("ctx") // 2
    chip_ref = chip[None].astype(jnp.int32)
    core_ref = core[None].astype(jnp.int32)
    inputs = tokens[0]
    rows, width = inputs.shape
    half = width // 2
    half_ff = FF // 2

    def cut(value, which, count, axis):
        return lax.dynamic_slice_in_dim(value, which * count, count, axis)

    def share(mine, theirs, axis):
        return ordered(core, mine, over_core(theirs), axis)

    vectors = jnp.stack(
        (bias_query, bias_value, bias_out, bias_down, gain_attn, shift_attn, gain_ffn, shift_ffn), axis=1
    )
    vectors = jnp.pad(vectors, ((0, 0), (0, 128 - VECTORS)))
    first = row_gather(pack_first(core_ref, (w_query, w_key, w_value, w_out), vectors))
    second = row_gather(pack(core_ref, w_up, w_gate, w_down))
    first.first()

    own_numbers = jnp.stack((segments[0], jnp.where(padding[0] == 1, -1, segments[0])))
    numbers = share(own_numbers, own_numbers, 1)
    slopes = cut(head_slopes(H), core, H // 2, 0)
    (numbers,) = first.join(numbers)
    tags = numbers[1]
    seg_row = numbers[0][None, :]
    if tuned:
        tags_send = jnp.where(chip == 0, tags[rows:], tags[:rows]) + 2
        first.second()
        beyond = over_x(tags_send)
        beyond, second.own = first.join(beyond, second.own)
        beyond = beyond - 2
        tags_reach = ordered(chip, tags, beyond, 0)[:, None]
        tags_local = tags[:, None]
        seg_local = cut(seg_row, chip, rows, 1)
        seg_reach = cut(seg_row, 1 - chip, rows, 1)
    else:
        tag_low = from_previous_chip(tags[rows:] + 2) - 2
        tag_high = from_next_chip(tags[:rows] + 2) - 2
        tags_wide = jnp.concatenate([tag_low, tags, tag_high])[:, None]
    first.third()
    inputs_all = share(inputs, inputs, 0)
    (inputs_all,) = first.join(inputs_all)
    (second.own,) = first.fourth(second.own)
    second.first_z()
    (second.own,) = first.join(second.own)
    second.first_y()

    spot = jnp.stack((core, chip if tuned else jnp.zeros_like(chip))).astype(jnp.int32)
    vec, full_qkv, out_half, queries_local, queries_reach, keys_values, beyond = project(
        first.numbers(), spot, inputs_all, first.pieces()
    )
    out_other = over_core(out_half)
    if tuned:
        queries_local, queries_reach, keys_values, beyond = second.join(
            queries_local, queries_reach, keys_values, beyond
        )
        beyond = over_x(beyond)
        second.second()
        attended_local, lse_local = attention_forward(
            local_blocks, chip_ref, queries_local, keys_values, seg_local, tags_local, slopes
        )
        attended_local, lse_local, beyond = second.join(attended_local, lse_local, beyond)
        keys_values, kv_beyond = second.third(keys_values, beyond)
        attended_reach, lse_reach = attention_forward(
            reach_blocks, chip_ref, queries_reach, keys_values, seg_reach, tags_reach, slopes, kv_beyond
        )
        attended_own = ordered(chip, attended_local, attended_reach, 0)
        (attended_own,) = second.join(attended_own)
        (attended_own,) = second.fourth(attended_own)
    else:
        queries = jnp.concatenate([queries_local, queries_reach], axis=0)
        kv_low = from_previous_chip(keys_values[rows:])
        kv_high = from_next_chip(keys_values[:rows])
        kv_wide = jnp.concatenate([kv_low, keys_values, kv_high], axis=0)
        spans = [(i * rows, i * rows + rows + 2 * HALF) for i in range(2)]
        forward_parts = [
            attention_forward(
                reach_blocks, chip_ref, queries[i * rows : (i + 1) * rows], kv_wide[low:high],
                seg_row[:, i * rows : (i + 1) * rows], tags_wide[low:high], slopes,
            )
            for i, (low, high) in enumerate(spans)
        ]
        attended_own = jnp.concatenate([part[0] for part in forward_parts], axis=0)
    attended_all = share(attended_own, attended_own, 1)
    first_norm, first_normed, first_inverse, own_low, full_out = first_norm_of(
        core_ref, vec, attended_all, out_half, out_other, inputs
    )
    other_low = over_core(own_low)
    if tuned:
        own_low, other_low = second.join(own_low, other_low)
    pieces = second.pieces()
    places = second.numbers()
    hidden, act, slope, ffn_part, ffn_send = ffn_forward(own_low, other_low, pieces, places, half_ff)
    layer_out, grad_second, own_branch, ffn_sums = second_norm(
        vec, first_norm, ffn_part, over_core(ffn_send), cotangent[0]
    )
    branch_other = over_core(own_branch)
    group = chip_ref if tuned else jnp.zeros_like(chip_ref)
    down_send = down_grad(1 - group, own_branch, branch_other, hidden)
    if tuned:
        down_send, own_branch, branch_other = tie(down_send, own_branch, branch_other)
        down_got = over_x(down_send)
    down_keep = down_grad(group, own_branch, branch_other, hidden)
    down_keep, own_branch, branch_other = tie(down_keep, own_branch, branch_other)
    *grad_pieces, normed_part, normed_send = ffn_backward(
        own_low, other_low, own_branch, branch_other, act, slope, pieces, places, half_ff
    )
    if tuned:
        normed_send, down_got, *grad_pieces = tie(normed_send, down_got, *grad_pieces)
        grad_pieces = add_last(places, grad_pieces, down_keep, down_got)
    else:
        shard_rows = width // 8
        grad_pieces = [
            jnp.concatenate(
                [piece[:-1], down_keep[None, i * shard_rows : (i + 1) * shard_rows],
                 down_send[None, i * shard_rows : (i + 1) * shard_rows]]
            )
            for i, piece in enumerate(grad_pieces)
        ]
    reduce_ffn = (LateReduce if tuned else PlainReduce)(grad_pieces)
    (normed_send,) = reduce_ffn.first(normed_send)
    grad_first, low_mine, low_theirs, back_mine, back_theirs, attn_sums = first_norm_back(
        core_ref, vec, full_out, grad_second, normed_part, over_core(normed_send),
        first_normed, first_inverse,
    )
    back_other = over_core(back_theirs)
    low_other = over_core(low_theirs)

    if tuned:
        back_ref = jnp.stack((chip, core == chip)).astype(jnp.int32)
        def reach_part(low, count, into):
            return attention_backward(
                reach_blocks, back_ref, queries_reach, keys_values, attended_reach, back_other, back_mine,
                lse_reach, seg_reach, tags_reach, slopes, None, low, count, into, kv_beyond,
            )

        low_all = ordered(core, low_mine, low_other, 0)
        pairs = half // (2 * HD)
        reached = reduce_ffn.join(*reach_part(0, 1, ()))
        reached = reduce_ffn.second(*reached)
        dq_reach, dkv_reach, beyond = reach_part(1, pairs - 1, tuple(reached))
        dq_reach, dkv_reach, beyond, low_all = tie(dq_reach, dkv_reach, beyond, low_all)
        beyond = over_x(beyond)
        grad_w_out = dot_tn(attended_all, low_all)
        dq_reach, dkv_reach, grad_w_out = reduce_ffn.join(dq_reach, dkv_reach, grad_w_out)
        dq_reach, dkv_reach, grad_w_out = reduce_ffn.third(dq_reach, dkv_reach, grad_w_out)
        dq_local, dkv_local = attention_backward(
            local_blocks, back_ref, queries_local, keys_values, attended_local,
            back_mine, back_other, lse_local, seg_local, tags_local, slopes, dkv_reach,
        )
        dq_local, dkv_local, beyond = reduce_ffn.join(dq_local, dkv_local, beyond)
        reduce_ffn.fourth()
    else:
        grad_attended = ordered(core, back_mine, back_other, 0)
        back_ref = jnp.ones((2,), jnp.int32)
        backward_parts = [
            attention_backward(
                reach_blocks, back_ref, queries[i * rows : (i + 1) * rows], kv_wide[low:high],
                forward_parts[i][0], grad_attended[i * rows : (i + 1) * rows],
                grad_attended[i * rows : (i + 1) * rows], forward_parts[i][1],
                seg_row[:, i * rows : (i + 1) * rows], tags_wide[low:high], slopes, None,
            )
            for i, (low, high) in enumerate(spans)
        ]
        dq_local, dq_reach = [part[0] for part in backward_parts]
        reach_0, reach_1 = [part[1] for part in backward_parts]
        from_next = from_next_chip(reach_0[:, :HALF].astype(jnp.bfloat16)).astype(jnp.float32)
        from_previous = from_previous_chip(reach_1[:, rows + HALF :].astype(jnp.bfloat16)).astype(jnp.float32)
        centre = jnp.pad(reach_0[:, HALF:], ((0, 0), (0, 2 * rows - reach_0.shape[1] + HALF), (0, 0)))
        centre = centre + jnp.pad(
            reach_1[:, : rows + HALF], ((0, 0), (2 * rows - rows - HALF, 0), (0, 0))
        )
        centre = centre.at[:, 2 * rows - HALF :].add(from_next)
        dkv_local = centre.at[:, :HALF].add(from_previous)
        beyond = jnp.zeros_like(from_next, dtype=jnp.bfloat16)
        grad_w_out = dot_tn(attended_all, ordered(core, low_mine, low_other, 0))
    *grad_last, grad_qkv = last_grads(
        places, spot, inputs_all, dq_local, dq_reach, dkv_local, beyond, grad_w_out.astype(jnp.bfloat16),
        attn_sums, ffn_sums,
    )
    last = row_reduce(grad_last)
    last.first()
    if tuned:
        reduce_ffn.part(0, 1)
        last.pieces = last.join(*last.pieces)
        last.pieces = reduce_ffn.last_y(*last.pieces)
    last.second()
    inputs_own, inputs_send = input_part(core_ref, grad_qkv, full_qkv)
    grad_inputs = grad_first + inputs_own + over_core(inputs_send).astype(jnp.float32)
    ffn_mine = reduce_ffn.result()
    if tuned:
        got = over_x(ffn_mine)
        ffn_mine = jnp.concatenate(
            [ffn_mine[:-1] + got[:-1], ordered(chip, ffn_mine[-1:], got[-1:], 0)], axis=0
        )
    else:
        ffn_mine = chips_sum(ffn_mine)
    (grad_inputs,) = last.join(grad_inputs)
    last.third()
    last.join()
    last.fourth()
    grad_up, grad_gate, grad_down = lay_out(core_ref, ffn_mine, over_core(ffn_mine))
    if tuned:
        grad_up, grad_gate, grad_down = last.join(grad_up, grad_gate, grad_down)
    last_mine = chips_sum(last.result())[0]
    last_rows, vector_rows = finish(core_ref, last_mine, over_core(last_mine))

    return (
        layer_out[None],
        grad_inputs[None],
        *last_rows,
        grad_up,
        grad_gate,
        grad_down,
    ) + tuple(row[0] for row in vector_rows)


def solution(mesh):
    rows_spec = P("fsdp", "ctx", None)
    in_specs = (
        (rows_spec, P("fsdp", "ctx"), P("fsdp", "ctx"))
        + (P("fsdp", None),) * 7
        + (P("fsdp"),) * VECTORS
        + (rows_spec,)
    )
    out_specs = (rows_spec, rows_spec) + (P("fsdp", None),) * 7 + (P("fsdp"),) * VECTORS
    return jax.shard_map(
        on_device, mesh=mesh, in_specs=in_specs, out_specs=out_specs, check_vma=False
    )
```
